32 devices in a mesh: section: 2 (over x), lat: 4 (over y, core), lon: 4 (over z).
Axes of the slice: x: 2, y: 2, z: 4, core: 2. Of those that a mesh axis runs over, the one named last changes fastest.
Arguments:
- window_input: bfloat16 [2, 16, 272, 256], P(None, 'lat', 'lon'), may hold values from -8 to 8
- output_cotangent: bfloat16 [2, 16, 272, 256], P(None, 'lat', 'lon'), may hold values from -6 to 6
- ocean_mask: int32 [16, 272], P('lat', 'lon'), may hold values 0 or 1
- dw_kernel: bfloat16 [2, 49, 256], P('section'), may hold values from -1.5 to 1.5
- channel_params: bfloat16 [2, 5, 256], P('section'), may hold values from -1.5 to 1.5
- up_weight: bfloat16 [2, 256, 1024], P('section'), may hold values from -0.375 to 0.375
- up_bias: bfloat16 [2, 1024], P('section'), may hold values from -3 to 3
- down_weight: bfloat16 [2, 1024, 256], P('section'), may hold values from -0.1875 to 0.1875
Outputs:
- boundary: bfloat16 [2, 2, 16, 272, 256], P('section', None, 'lat', 'lon')
- grad_kernel: float32 [2, 49, 256], P('section')
- grad_channels: float32 [2, 5, 256], P('section')
- grad_up: float32 [2, 256, 1024], P('section')
- grad_up_bias: float32 [2, 1024], P('section')
- grad_down: float32 [2, 1024, 256], P('section')
The draws below stay inside these ranges and needn't reach their ends.
All inputs are finite; a program needn't handle non-finite values. No bound on the sum of `ocean_mask` on one device may be relied on, other than what follows from the above.
Results may differ from the reference program's by a relative error of at most 0.012.
Values may be sent and summed in bfloat16 or wider, within the bound.
No kernel may reach another device: no remote copies, remote signals or barrier semaphores. Data moves between devices by JAX's collectives and lax.ppermute only.
A program may use at most 128 MiB of HBM per device.

```python
import math
import jax
import jax.numpy as jnp
from jax import lax

C = 256
HID = 1024
KERNEL = 7
ROWS_DEV = 4
COLS_DEV = 68
BATCH = 2
LAT_CELLS = 16
LON_CELLS = 272
N_SECTION = 2


def rough_values(key, shape):
    return jnp.clip(jax.random.normal(key, shape, jnp.float32), -3.0, 3.0)


def log_spread(key, shape, lowest, highest):
    return jnp.exp(jax.random.uniform(key, shape, jnp.float32, math.log(lowest), math.log(highest)))


def draw_window_input(key, part):
    subkeys = jax.random.split(jax.random.fold_in(key, 11), 3)
    base = rough_values(subkeys[0], (BATCH, LAT_CELLS, LON_CELLS, C))
    cell_scale = log_spread(subkeys[1], (BATCH, LAT_CELLS, LON_CELLS, 1), 0.3, 3.0)
    chan_scale = log_spread(subkeys[2], (1, 1, 1, C), 0.3, 3.0)
    return jnp.clip(base * cell_scale * chan_scale, -8.0, 8.0).astype(jnp.bfloat16)


def draw_dw_kernel(key, part):
    subkeys = jax.random.split(jax.random.fold_in(key, 23), 2)
    base = rough_values(subkeys[0], (N_SECTION, KERNEL * KERNEL, C))
    chan_scale = log_spread(subkeys[1], (N_SECTION, 1, C), 0.05, 0.5)
    return (base * chan_scale).astype(jnp.bfloat16)


def draw_channel_params(key, part):
    subkeys = jax.random.split(jax.random.fold_in(key, 37), 5)
    shape = (N_SECTION, 1, C)
    conv_bias = 0.5 * rough_values(subkeys[0], shape)
    norm_gain = jax.random.uniform(subkeys[1], shape, jnp.float32, 0.6, 1.4)
    norm_shift = 0.3 * rough_values(subkeys[2], shape)
    out_bias = 0.3 * rough_values(subkeys[3], shape)
    layer_scale = log_spread(subkeys[4], shape, 0.2, 1.0)
    return jnp.concatenate([conv_bias, norm_gain, norm_shift, out_bias, layer_scale], axis=1).astype(jnp.bfloat16)


def touch_ends(values, stream_key, low, largest):
    extent = values.shape
    spot = [jax.random.randint(jax.random.fold_in(stream_key, axis), (), 0, extent[axis]) for axis in range(len(extent))]
    values = values.at[tuple(spot)].set(low)
    longest = extent.index(max(extent))
    spot[longest] = (spot[longest] + 1) % extent[longest]
    return values.at[tuple(spot)].set(largest)


def levels(key, shape, cuts, smallest, top_value):
    gain, own = 1.0, jax.random.fold_in(key, 6)
    for position, blocks in cuts:
        heights = jnp.exp(jax.random.uniform(jax.random.fold_in(own, position), (blocks,), jnp.float32, smallest / len(cuts), top_value / len(cuts)))
        gain = gain * jnp.repeat(heights, shape[position] // blocks).reshape([-1 if axis == position else 1 for axis in range(len(shape))])
    return gain


def bell_draw(own_key, dims, scale, most, cuts=(), kind=jnp.bfloat16):
    values = scale * jax.random.normal(own_key, dims, jnp.float32)
    if cuts:
        values = values * levels(own_key, dims, cuts, -0.22, 0.18)
    return jnp.clip(values, -most, most).astype(kind)


def setup_inputs(seed: int = 0) -> dict:
    splits = jax.random.split(jax.random.key(seed), 9)
    return {
        "window_input": draw_window_input(jax.random.fold_in(splits[8], 71), 0),
        "output_cotangent": bell_draw(splits[1], (BATCH, LAT_CELLS, LON_CELLS, C), 1.0, 6.0, ((1, 4), (2, 4))),
        "ocean_mask": touch_ends((jax.random.randint(splits[2], (LAT_CELLS, LON_CELLS), 0, 4) < 3).astype(jnp.int32), jax.random.fold_in(splits[2], 1), 0, 1),
        "dw_kernel": draw_dw_kernel(jax.random.fold_in(splits[8], 71), 0),
        "channel_params": draw_channel_params(jax.random.fold_in(splits[8], 71), 0),
        "up_weight": bell_draw(splits[5], (N_SECTION, C, HID), C ** -0.5, 0.375, ((0, 2),)),
        "up_bias": bell_draw(splits[6], (N_SECTION, HID), 0.5, 3.0, ((0, 2),)),
        "down_weight": bell_draw(splits[7], (N_SECTION, HID, C), HID ** -0.5, 0.1875, ((0, 2),)),
    }


norm_eps = 1e-06
gelu_scale = 0.7978845608028654
gelu_cubic = 0.044715
rows_contract = (((0,), (0,)), ((), ()))
cols_contract = (((1,), (1,)), ((), ()))

def gelu_value(values):
    inner = gelu_scale * (values + gelu_cubic * values * values * values)
    return 0.5 * values * (1.0 + jnp.tanh(inner))

def gelu_slope(values):
    tangent = jnp.tanh(gelu_scale * (values + gelu_cubic * values * values * values))
    return 0.5 * (1.0 + tangent) + 0.5 * values * (1.0 - tangent * tangent) * gelu_scale * (1.0 + 3.0 * gelu_cubic * values * values)

def depthwise(padded, kernel, row_count, col_count):
    summed = jnp.zeros((padded.shape[0], row_count, col_count, padded.shape[3]), jnp.float32)
    for offset in range(KERNEL * KERNEL):
        row_off, col_off = divmod(offset, KERNEL)
        window = padded[:, row_off:row_off + row_count, col_off:col_off + col_count, :]
        summed = summed + window.astype(jnp.float32) * kernel[offset].astype(jnp.float32)
    return summed

def kernel_grads(padded, grad_conv, row_count, col_count):
    channels = grad_conv.shape[-1]
    grad_wide = grad_conv.astype(jnp.float32)
    tap_sums = []
    for offset in range(KERNEL * KERNEL):
        row_off, col_off = divmod(offset, KERNEL)
        window = padded[:, row_off:row_off + row_count, col_off:col_off + col_count, :].astype(jnp.float32)
        tap_sums.append(lax.optimization_barrier(jnp.sum((grad_wide * window).reshape(-1, channels), axis=0)))
    return (jnp.stack(tap_sums), lax.optimization_barrier(jnp.sum(grad_wide.reshape(-1, channels), axis=0)))

def cell_forward(conv_out, inputs, sea_mask, params, w_up, b_up, w_down):
    average = lax.optimization_barrier(jnp.mean(conv_out, axis=-1, keepdims=True))
    centered = conv_out - average
    inverse = lax.rsqrt(lax.optimization_barrier(jnp.mean(centered * centered, axis=-1, keepdims=True)) + norm_eps)
    normed = centered * inverse
    scaled = (normed * params[1].astype(jnp.float32) + params[2].astype(jnp.float32)).astype(jnp.bfloat16)
    channels = scaled.shape[-1]
    flat_rows = scaled.reshape(-1, channels)
    hidden = jnp.dot(flat_rows, w_up, preferred_element_type=jnp.float32) + b_up.astype(jnp.float32)
    active = gelu_value(hidden).astype(jnp.bfloat16)
    branch = jnp.dot(active, w_down, preferred_element_type=jnp.float32) + params[3].astype(jnp.float32)
    branch = branch.reshape(conv_out.shape)
    output = (sea_mask * (inputs.astype(jnp.float32) + params[4].astype(jnp.float32) * branch)).astype(jnp.bfloat16)
    return (output, (normed, inverse, flat_rows, hidden, active, branch))

def cell_backward(saved, sea_mask, cotangent, params, w_up, w_down):
    normed, inverse, flat_rows, hidden, active, branch = saved
    channels = normed.shape[-1]
    upstream = sea_mask * cotangent.astype(jnp.float32)
    grad_scale = lax.optimization_barrier(jnp.sum((upstream * branch).reshape(-1, channels), axis=0))
    grad_branch = (params[4].astype(jnp.float32) * upstream).astype(jnp.bfloat16).reshape(-1, channels)
    grad_down = lax.dot_general(active, grad_branch, rows_contract, preferred_element_type=jnp.float32)
    grad_out_bias = lax.optimization_barrier(jnp.sum(grad_branch.astype(jnp.float32), axis=0))
    grad_active = lax.dot_general(grad_branch, w_down, cols_contract, preferred_element_type=jnp.float32)
    grad_hidden = (grad_active * gelu_slope(hidden)).astype(jnp.bfloat16)
    grad_up = lax.dot_general(flat_rows, grad_hidden, rows_contract, preferred_element_type=jnp.float32)
    grad_up_bias = lax.optimization_barrier(jnp.sum(grad_hidden.astype(jnp.float32), axis=0))
    grad_scaled = lax.dot_general(grad_hidden, w_up, cols_contract, preferred_element_type=jnp.float32)
    grad_scaled = grad_scaled.reshape(normed.shape)
    grad_gain = lax.optimization_barrier(jnp.sum((grad_scaled * normed).reshape(-1, channels), axis=0))
    grad_shift = lax.optimization_barrier(jnp.sum(grad_scaled.reshape(-1, channels), axis=0))
    grad_normed = grad_scaled * params[1].astype(jnp.float32)
    first_mean = lax.optimization_barrier(jnp.mean(grad_normed, axis=-1, keepdims=True))
    second_mean = lax.optimization_barrier(jnp.mean(grad_normed * normed, axis=-1, keepdims=True))
    grad_conv = (inverse * (grad_normed - first_mean - normed * second_mean)).astype(jnp.bfloat16)
    small = (grad_gain, grad_shift, grad_out_bias, grad_scale)
    return (grad_conv, upstream, small, grad_up, grad_up_bias, grad_down)

def pad_field(field):
    reach = KERNEL // 2
    wrapped = jnp.concatenate([field[:, :, field.shape[2] - reach:], field, field[:, :, :reach]], axis=2)
    return jnp.pad(wrapped, ((0, 0), (reach, reach), (0, 0), (0, 0)))

def by_rows(array):
    return jnp.moveaxis(array, 1, 0)

def forward_block(field, sea_rows, weights):
    kernel, params, w_up, b_up, w_down = weights
    padded = pad_field(field)
    conv_out = depthwise(padded, kernel, field.shape[1], field.shape[2]) + params[0].astype(jnp.float32)

    def one_row(pieces):
        conv_row, input_row, mask_row = pieces
        output, unused = cell_forward(conv_row, input_row, mask_row[None, :, None], params, w_up, b_up, w_down)
        return output
    rows_out = lax.map(one_row, (by_rows(conv_out), by_rows(field), sea_rows))
    return jnp.moveaxis(rows_out, 0, 1)

def backward_block(field, sea_rows, weights, cotangent):
    kernel, params, w_up, b_up, w_down = weights
    row_count, col_count = (field.shape[1], field.shape[2])
    channels = field.shape[3]
    hidden_units = w_up.shape[1]
    padded = pad_field(field)
    conv_out = depthwise(padded, kernel, row_count, col_count) + params[0].astype(jnp.float32)
    start = (tuple((jnp.zeros((channels,), jnp.float32) for member in range(4))), jnp.zeros((channels, hidden_units), jnp.float32), jnp.zeros((hidden_units,), jnp.float32), jnp.zeros((hidden_units, channels), jnp.float32))

    def one_row(carry, pieces):
        conv_row, input_row, mask_row, cot_row = pieces
        mask_wide = mask_row[None, :, None]
        output, saved = cell_forward(conv_row, input_row, mask_wide, params, w_up, b_up, w_down)
        grad_conv, upstream, small, grad_up, grad_bias, grad_down = cell_backward(saved, mask_wide, cot_row, params, w_up, w_down)
        carry = jax.tree.map(jnp.add, carry, (small, grad_up, grad_bias, grad_down))
        return (carry, (grad_conv, upstream))
    totals, outputs = lax.scan(one_row, start, (by_rows(conv_out), by_rows(field), sea_rows, by_rows(cotangent)))
    grad_conv = jnp.moveaxis(outputs[0], 0, 1)
    upstream = jnp.moveaxis(outputs[1], 0, 1)
    tap_sums, bias_sum = kernel_grads(padded, grad_conv, row_count, col_count)
    spread = depthwise(pad_field(grad_conv), kernel[::-1], row_count, col_count)
    grad_input = (upstream + spread).astype(jnp.bfloat16)
    small, grad_up, grad_bias, grad_down = totals
    return (grad_input, (tap_sums, jnp.stack((bias_sum,) + tuple(small)), grad_up, grad_bias, grad_down))

def reference(window_input, output_cotangent, ocean_mask, dw_kernel, channel_params, up_weight, up_bias, down_weight):
    sea_rows = ocean_mask.astype(jnp.float32)
    blocks = [(dw_kernel[block_index], channel_params[block_index], up_weight[block_index], up_bias[block_index], down_weight[block_index]) for block_index in range(2)]
    middle = forward_block(window_input, sea_rows, blocks[0])
    final = forward_block(middle, sea_rows, blocks[1])
    grad_middle, grads_second = backward_block(middle, sea_rows, blocks[1], output_cotangent)
    grad_start, grads_first = backward_block(window_input, sea_rows, blocks[0], grad_middle)
    factor = 1.0 / math.sqrt(BATCH * ROWS_DEV * COLS_DEV)
    stacked = jax.tree.map(lambda before, behind: jnp.stack([before, behind]) * factor, grads_first, grads_second)
    boundary = jnp.stack([grad_start, final])
    return (boundary, stacked[0], stacked[1], stacked[2], stacked[3], stacked[4])
```

```python
import functools
import math

import jax
import jax.numpy as jnp
from jax import lax
from jax.experimental import pallas as pl
from jax.experimental.pallas import tpu as pltpu
from jax.sharding import PartitionSpec as P

KERNEL = 7
TAPS = KERNEL * KERNEL
REACH = KERNEL // 2
ROWS_DEV = 4
COLS_DEV = 68
BATCH = 2
HALF = 128
WIDE = 256
HID = 1024
QUARTERS = HID // WIDE
SIDE_X, SIDE_0, SIDE_1 = 12, 9, 6
W_X, W_0, W_1, W_OWN = 96, 88, 80, 72
CHUNK = 32
SMALL = 64

norm_eps = 1e-06
gelu_scale = 0.7978845608028654
gelu_cubic = 0.044715
f32, bf16 = jnp.float32, jnp.bfloat16

nn = (((1,), (0,)), ((), ()))
nt = (((1,), (1,)), ((), ()))
tn = (((0,), (0,)), ((), ()))


def dot(left, right, dims=nn):
    return lax.dot_general(left, right, dims, preferred_element_type=f32)


def lanes(half):
    return slice(half * HALF, (half + 1) * HALF)


def load_padded(pad, odd, center, first, second, offset=0):
    width = center.shape[1]

    def put(row, value):
        value = value.astype(f32)
        for half in range(2):
            pad[half, row, offset : offset + width, :] = value[:, lanes(half)]

    at_first = jnp.where(odd == 1, 0, REACH + ROWS_DEV)
    at_second = jnp.where(odd == 1, REACH + ROWS_DEV, 0)
    for row in range(ROWS_DEV):
        put(REACH + row, center[row])
    for row in range(REACH):
        put(at_first + row, first[row])
        put(at_second + row, second[row])


def load_taps(taps, small):
    for half in range(2):
        taps[half] = jnp.broadcast_to(small[0:TAPS, lanes(half)][:, None, :], (TAPS, 8, HALF))


def conv_tile(pad, taps, half, start, reverse):
    sums = [None] * ROWS_DEV
    for row in range(ROWS_DEV + KERNEL - 1):
        for col_off in range(KERNEL):
            window = pad[half, row, start + col_off : start + col_off + 8, :]
            for out_row in range(ROWS_DEV):
                row_off = row - out_row
                if 0 <= row_off < KERNEL:
                    tap = row_off * KERNEL + col_off
                    term = window * taps[half, TAPS - 1 - tap if reverse else tap]
                    sums[out_row] = term if sums[out_row] is None else sums[out_row] + term
    return sums


def chunks(count, body, start=0):
    return lax.fori_loop(0, count // CHUNK, lambda i, carry: body(pl.ds(pl.multiple_of(i * CHUNK, CHUNK), CHUNK), carry), start)


def fold(value):
    return jnp.sum(value.reshape(CHUNK // 8, 8, value.shape[-1]), axis=0)


def twice(value):
    return jnp.concatenate([value, value], axis=1)


def send_rows(odd, source, send_first, send_second):
    first, second = jnp.where(odd == 1, 0, 1), jnp.where(odd == 1, 1, 0)
    send_first[...] = source[pl.ds(first, REACH)]
    send_second[...] = source[pl.ds(second, REACH)]


def forward_cells(width, pad, taps, small, mask, w_up, w_down, normed, inverse, z, hidden, active, slope, branch, out):
    count = ROWS_DEV * width
    load_taps(taps, small)
    for tile in range(width // 8):
        start = tile * 8
        halves = [conv_tile(pad, taps, half, start, False) for half in range(2)]
        for row in range(ROWS_DEV):
            u = [halves[half][row] + small[TAPS : TAPS + 1, lanes(half)] for half in range(2)]
            mean = jnp.sum(u[0] + u[1], axis=-1, keepdims=True) * (1.0 / WIDE)
            u = [value - mean for value in u]
            spread = jnp.sum(u[0] * u[0] + u[1] * u[1], axis=-1, keepdims=True) * (1.0 / WIDE)
            scale = lax.rsqrt(spread + norm_eps)
            at = slice(row * width + start, row * width + start + 8)
            inverse[at, :] = jnp.broadcast_to(scale, (8, HALF))
            for half in range(2):
                normed[at, lanes(half)] = u[half] * scale

    def scaled(at, carry):
        z[at, :] = (normed[at, :] * small[TAPS + 1 : TAPS + 2, :] + small[TAPS + 2 : TAPS + 3, :]).astype(bf16)
        return carry

    chunks(count, scaled, 0)
    for quarter in range(QUARTERS):
        cols = slice(quarter * WIDE, (quarter + 1) * WIDE)
        hidden[...] = dot(z[...], w_up[:, cols])
        bias = small[TAPS + 5 + quarter : TAPS + 6 + quarter, :]

        def gelu(at, carry):
            h = hidden[at, :] + bias
            square = h * h
            tangent = jnp.tanh(h * (gelu_scale + (gelu_scale * gelu_cubic) * square))
            above = 0.5 + 0.5 * tangent
            active[at, cols] = (h * above).astype(bf16)
            slope[at, cols] = above + (0.5 * h) * (1.0 - tangent * tangent) * (
                gelu_scale + (3.0 * gelu_scale * gelu_cubic) * square
            )
            return carry

        chunks(count, gelu, 0)
    branch[...] = dot(active[...], w_down[...]) + small[TAPS + 3 : TAPS + 4, :]
    for row in range(ROWS_DEV):
        for tile in range(width // 8):
            start = tile * 8
            at = slice(row * width + start, row * width + start + 8)
            for half in range(2):
                value = pad[half, REACH + row, start + REACH : start + REACH + 8, :]
                gain = small[TAPS + 4 : TAPS + 5, lanes(half)]
                out[at, lanes(half)] = mask[at, :] * (value + gain * branch[at, lanes(half)])


def backward_cells(
    width, odd, small, own, own_row, upstream, w_up, w_down, normed, inverse, z, active, slope, branch, hidden, dm, dh, du, keep, send, sums
):
    count = ROWS_DEV * width
    zero = jnp.zeros((8, WIDE), f32)

    def first(at, carry):
        sum_dm, sum_em = carry
        e = upstream[at, :]
        inside = twice(own[at, :])
        grad = (e * small[TAPS + 4 : TAPS + 5, :]).astype(bf16)
        dm[at, :] = grad
        sum_dm = sum_dm + fold(grad.astype(f32) * inside)
        sum_em = sum_em + fold(e * branch[at, :] * inside)
        return sum_dm, sum_em

    sum_dm, sum_em = chunks(count, first, (zero, zero))
    for quarter in range(QUARTERS):
        cols = slice(quarter * WIDE, (quarter + 1) * WIDE)
        hidden[...] = dot(dm[...], w_down[cols, :], nt)

        def through(at, carry):
            dh[at, cols] = (hidden[at, :] * slope[at, cols]).astype(bf16)
            return carry

        chunks(count, through, 0)
    hidden[...] = dot(dh[...], w_up[...], nt)
    sum_dh = dot(own_row[...], dh[...])

    def norm(at, carry):
        sum_dzn, sum_dz, sum_du = carry
        dz = hidden[at, :]
        normal = normed[at, :]
        inside = twice(own[at, :])
        inner = dz * inside
        sum_dz = sum_dz + fold(inner)
        sum_dzn = sum_dzn + fold(inner * normal)
        dn = dz * small[TAPS + 1 : TAPS + 2, :]
        mean = jnp.sum(dn, axis=-1, keepdims=True) * (1.0 / WIDE)
        slant = jnp.sum(dn * normal, axis=-1, keepdims=True) * (1.0 / WIDE)
        grad = (twice(inverse[at, :]) * (dn - mean - normal * slant)).astype(bf16).astype(f32)
        du[at, :] = grad
        sum_du = sum_du + fold(grad * inside)
        dm[at, :] = (dm[at, :].astype(f32) * inside).astype(bf16)
        z[at, :] = (z[at, :].astype(f32) * inside).astype(bf16)
        return sum_dzn, sum_dz, sum_du

    sum_dzn, sum_dz, sum_du = chunks(count, norm, (zero, zero, zero))
    rows = [jnp.sum(value, axis=0, keepdims=True) for value in (sum_du, sum_dzn, sum_dz, sum_dm, sum_em)]
    rows += [sum_dh[0:1, quarter * WIDE : (quarter + 1) * WIDE] for quarter in range(QUARTERS)]
    for index, value in enumerate(rows):
        sums[index : index + 1, :] = value
    sums[len(rows) : 16, :] = jnp.zeros((16 - len(rows), WIDE), f32)

    def weights(up_ref, down_ref):
        for quarter in range(QUARTERS):
            cols = slice(quarter * WIDE, (quarter + 1) * WIDE)
            up_ref[cols, :] = dot(z[...], dh[:, cols], tn).astype(bf16)
            down_ref[cols, :] = dot(active[:, cols], dm[...], tn).astype(bf16)

    @pl.when(odd == 0)
    def _():
        weights(keep, send)

    @pl.when(odd == 1)
    def _():
        weights(send, keep)


def pick_weights(block, flags, own_up, own_down, got_up, got_down, other_up, other_down, w_up, w_down):
    odd, section = flags[0], flags[1]

    @pl.when(section == block)
    def _():
        w_up[...] = own_up[...]
        w_down[...] = own_down[...]

    @pl.when(section != block)
    def _():
        for ref, mine, other in ((w_up, got_up, other_up), (w_down, got_down, other_down)):
            half = mine.shape[0]
            ref[pl.ds(pl.multiple_of(odd * half, half), half), :] = mine[...]
            ref[pl.ds(pl.multiple_of((1 - odd) * half, half), half), :] = other[...]


def write_rows(source, width, out):
    for row in range(ROWS_DEV):
        out[row] = source[row * width : (row + 1) * width, :].astype(bf16)


def first_forward(
    flags, x, x_a, x_b, small, mask, own_up, own_down, got_up, got_down, other_up, other_down,
    y, send_a, send_b, normed, inverse, z, active, slope, branch, w_up, w_down,
    pad, taps, hidden, out,
):
    load_padded(pad, flags[0], x, x_a, x_b)
    pick_weights(0, flags, own_up, own_down, got_up, got_down, other_up, other_down, w_up, w_down)
    forward_cells(W_0, pad, taps, small, mask, w_up, w_down, normed, inverse, z, hidden, active, slope, branch, out)
    write_rows(out, W_0, y)
    send_rows(flags[0], y, send_a, send_b)


def second_block(
    flags, y, y_a, y_b, small, mask, own, own_row, upstream_in, own_up, own_down, got_up, got_down, other_up, other_down,
    final, du_out, send_a, send_b, keep, send, sums,
    pad, taps, hidden, out, normed, inverse, z, active, slope, branch, w_up, w_down, upstream, dm, dh, du,
):
    load_padded(pad, flags[0], y, y_a, y_b)
    pick_weights(1, flags, own_up, own_down, got_up, got_down, other_up, other_down, w_up, w_down)
    forward_cells(W_1, pad, taps, small, mask, w_up, w_down, normed, inverse, z, hidden, active, slope, branch, out)
    for row in range(ROWS_DEV):
        at = row * W_1 + SIDE_1
        final[row] = out[at : at + COLS_DEV, :].astype(bf16)
        upstream[row * W_1 : (row + 1) * W_1, :] = upstream_in[row].astype(f32)
    backward_cells(
        W_1, flags[0], small, own, own_row, upstream, w_up, w_down, normed, inverse, z, active, slope, branch, hidden, dm, dh, du, keep, send, sums
    )
    write_rows(du, W_1, du_out)
    send_rows(flags[0], du_out, send_a, send_b)


def first_backward(
    flags, du1, du1_a, du1_b, small1, small0, mask, own, own_row, upstream_in, normed, inverse, z_in, active, slope, branch, w_up, w_down,
    e_own, du_out, send_a, send_b, keep, send, sums,
    pad, taps, hidden, upstream, z, dm, dh, du,
):
    shift = SIDE_0 + REACH - SIDE_1
    pad[:, :, 0:8, :] = jnp.zeros((2, ROWS_DEV + 2 * REACH, 8, HALF), f32)
    pad[:, :, W_X - 16 : W_X, :] = jnp.zeros((2, ROWS_DEV + 2 * REACH, 16, HALF), f32)
    load_padded(pad, flags[0], du1, du1_a, du1_b, shift)
    load_taps(taps, small1)
    for row in range(ROWS_DEV):
        upstream[row * W_0 : (row + 1) * W_0, :] = upstream_in[row].astype(f32)
    for tile in range(W_0 // 8):
        start = tile * 8
        for half in range(2):
            spread = conv_tile(pad, taps, half, start, True)
            for row in range(ROWS_DEV):
                at = slice(row * W_0 + start, row * W_0 + start + 8)
                value = (upstream[at, lanes(half)] + spread[row]).astype(bf16).astype(f32)
                upstream[at, lanes(half)] = mask[at, :] * value
    for row in range(ROWS_DEV):
        at = row * W_0 + SIDE_0
        e_own[row] = upstream[at : at + W_OWN, :]
    z[...] = z_in[...]
    backward_cells(
        W_0, flags[0], small0, own, own_row, upstream, w_up, w_down, normed, inverse, z, active, slope, branch, hidden, dm, dh, du, keep, send, sums
    )
    write_rows(du, W_0, du_out)
    send_rows(flags[0], du_out, send_a, send_b)


def input_grad(flags, du, du_a, du_b, small, e_own, out, pad, taps, total):
    load_padded(pad, flags[0], du, du_a, du_b)
    load_taps(taps, small)
    for tile in range(W_OWN // 8):
        start = tile * 8
        for half in range(2):
            spread = conv_tile(pad, taps, half, start + SIDE_0 - REACH, True)
            for row in range(ROWS_DEV):
                at = slice(start, start + 8)
                total[row, at, lanes(half)] = e_own[row, at, lanes(half)] + spread[row]
    for row in range(ROWS_DEV):
        out[row] = total[row, 0:COLS_DEV, :].astype(bf16)


def tap_grads(width, flags, v, v_a, v_b, du, own, sums, out, pad, grads, total):
    load_padded(pad, flags[0], v, v_a, v_b)
    for row in range(ROWS_DEV):
        inside = own[row * width : (row + 1) * width, :]
        grads[row] = du[row].astype(f32) * twice(inside)
    total[...] = jnp.zeros((SMALL, WIDE), f32)
    for half in range(2):
        for col_off in range(KERNEL):
            partial = [None] * KERNEL
            for tile in range(width // 8):
                start = tile * 8
                grad = [grads[row, start : start + 8, lanes(half)] for row in range(ROWS_DEV)]
                for row in range(ROWS_DEV + KERNEL - 1):
                    window = pad[half, row, start + col_off : start + col_off + 8, :]
                    for out_row in range(ROWS_DEV):
                        row_off = row - out_row
                        if 0 <= row_off < KERNEL:
                            term = window * grad[out_row]
                            partial[row_off] = term if partial[row_off] is None else partial[row_off] + term
            for row_off in range(KERNEL):
                tap = row_off * KERNEL + col_off
                total[tap : tap + 1, lanes(half)] = jnp.sum(partial[row_off], axis=0, keepdims=True)
    total[TAPS : TAPS + 9, :] = sums[0:9, :]
    out[...] = total[...].astype(bf16)


def in_vmem():
    return pl.BlockSpec(memory_space=pltpu.VMEM)


def call(body, name, inputs, outputs, scratch, flops):
    return pl.pallas_call(
        body,
        name=name,
        out_shape=[jax.ShapeDtypeStruct(shape, dtype) for shape, dtype in outputs],
        in_specs=[pl.BlockSpec(memory_space=pltpu.SMEM)] + [in_vmem()] * (len(inputs) - 1),
        out_specs=[in_vmem()] * len(outputs),
        scratch_shapes=[pltpu.VMEM(shape, dtype) for shape, dtype in scratch],
        compiler_params=pltpu.CompilerParams(vmem_limit_bytes=56 << 20),
        cost_estimate=pl.CostEstimate(flops=flops, bytes_accessed=4 << 20, transcendentals=0),
    )(*inputs)


def swap_pairs(count, bit):
    return [(i, i ^ bit) for i in range(count)]


def on_device(
    window_input,
    output_cotangent,
    ocean_mask,
    dw_kernel,
    channel_params,
    up_weight,
    up_bias,
    down_weight,
):
    section = lax.axis_index("section")
    lat = lax.axis_index("lat")
    lon = lax.axis_index("lon")
    n_lat, n_lon = lax.axis_size("lat"), lax.axis_size("lon")
    odd = lat % 2
    flags = jnp.stack([odd, section]).astype(jnp.int32)
    channels = window_input.shape[-1]

    def over_section(value):
        return lax.ppermute(value, "section", [(0, 1), (1, 0)])

    def over_core(value):
        return lax.ppermute(value, "lat", swap_pairs(n_lat, 1))

    def lat_halo(send_a, send_b):
        pairs = [(i, i + 1) for i in range(1, n_lat - 1, 2)]
        pairs += [(j, i) for i, j in pairs]
        return over_core(send_a), lax.ppermute(send_b, "lat", pairs)

    def by_core(even, other):
        return jnp.where(odd == 0, even, other)

    small_own = jnp.concatenate(
        [dw_kernel[0], channel_params[0], up_bias[0].reshape(QUARTERS, WIDE), jnp.zeros((SMALL - TAPS - 9, WIDE), bf16)], axis=0
    )
    small_got = over_section(small_own)
    up, down = up_weight[0], down_weight[0]
    got_up = over_section(by_core(up[: channels // 2], up[channels // 2 :]))
    got_down = over_section(by_core(down[: HID // 2], down[HID // 2 :]))
    small_0 = jnp.where(section == 0, small_own, small_got).astype(f32)
    small_1 = jnp.where(section == 0, small_got, small_own).astype(f32)

    x = lax.dynamic_index_in_dim(window_input, section, 0, False)
    cot = lax.dynamic_index_in_dim(output_cotangent, section, 0, False)
    sea = ocean_mask.astype(bf16)

    def packed(x_part, cot_part, sea_part):
        sea_row = jnp.pad(sea_part, ((0, 0), (0, channels - sea_part.shape[1])))[:, None, :]
        return jnp.concatenate([x_part, cot_part, sea_row], axis=1)

    ring = [(i, (i + 1) % n_lon) for i in range(n_lon)]
    left = lax.ppermute(packed(x[:, -SIDE_X:], cot[:, -SIDE_1:], sea[:, -SIDE_0:]), "lon", ring)
    right = lax.ppermute(packed(x[:, :SIDE_X], cot[:, :SIDE_1], sea[:, :SIDE_0]), "lon", [(j, i) for i, j in ring])
    cot_at, sea_at = SIDE_X, SIDE_X + SIDE_1
    x_wide = jnp.concatenate([left[:, :SIDE_X], x, right[:, :SIDE_X], jnp.zeros((ROWS_DEV, W_X - COLS_DEV - 2 * SIDE_X, channels), bf16)], axis=1)
    x_a, x_b = lat_halo(by_core(x_wide[1:], x_wide[:REACH]), by_core(x_wide[:REACH], x_wide[1:]))
    mask_wide = jnp.concatenate(
        [left[:, sea_at, :SIDE_0], sea, right[:, sea_at, :SIDE_0], jnp.zeros((ROWS_DEV, W_0 - COLS_DEV - 2 * SIDE_0), bf16)], axis=1
    )
    before = SIDE_0 - SIDE_1
    cot_wide = jnp.concatenate(
        [
            jnp.zeros((ROWS_DEV, before, channels), bf16),
            left[:, cot_at:sea_at],
            cot,
            right[:, cot_at:sea_at],
            jnp.zeros((ROWS_DEV, W_0 - COLS_DEV - SIDE_1 - SIDE_0, channels), bf16),
        ],
        axis=1,
    )
    e_0 = cot_wide * mask_wide[:, :, None]
    e_1 = e_0[:, before : before + W_1]

    def spread_lanes(mask):
        flat = mask.astype(f32).reshape(-1, 1)
        return jnp.broadcast_to(flat, (flat.shape[0], HALF))

    mask_0, mask_1 = spread_lanes(mask_wide), spread_lanes(mask_wide[:, before : before + W_1])

    def own_cells(width, side):
        column = jnp.arange(width)
        inside = ((column >= side) & (column < side + COLS_DEV)).astype(f32)
        flat = jnp.tile(inside, ROWS_DEV)
        return jnp.broadcast_to(flat[:, None], (flat.shape[0], HALF)), jnp.broadcast_to(flat[None, :], (16, flat.shape[0])).astype(bf16)

    own_0, row_0 = own_cells(W_0, SIDE_0)
    own_1, row_1 = own_cells(W_1, SIDE_1)
    other_up, other_down = over_core(got_up), over_core(got_down)
    weights = (up, down, got_up, got_down, other_up, other_down)

    n_0, n_1 = ROWS_DEV * W_0, ROWS_DEV * W_1
    deep = ROWS_DEV + 2 * REACH
    taps_scratch = ((2, TAPS, 8, HALF), f32)

    y, y_send_a, y_send_b, normed, inverse, z, active, slope, branch, w_up, w_down = call(
        first_forward,
        "first_forward",
        (flags, x_wide, x_a, x_b, small_0, mask_0) + weights,
        [
            ((ROWS_DEV, W_0, WIDE), bf16), ((REACH, W_0, WIDE), bf16), ((REACH, W_0, WIDE), bf16),
            ((n_0, WIDE), f32), ((n_0, HALF), f32), ((n_0, WIDE), bf16), ((n_0, HID), bf16), ((n_0, HID), f32), ((n_0, WIDE), f32),
            ((WIDE, HID), bf16), ((HID, WIDE), bf16),
        ],
        [((2, deep, W_X, HALF), f32), taps_scratch, ((n_0, WIDE), f32), ((n_0, WIDE), f32)],
        2_000_000_000,
    )
    y_a, y_b = lat_halo(y_send_a, y_send_b)
    final, du1, du1_send_a, du1_send_b, keep_1, send_1, sums_1 = call(
        second_block,
        "second_block",
        (flags, y, y_a, y_b, small_1, mask_1, own_1, row_1, e_1) + weights,
        [
            ((ROWS_DEV, COLS_DEV, WIDE), bf16), ((ROWS_DEV, W_1, WIDE), bf16), ((REACH, W_1, WIDE), bf16), ((REACH, W_1, WIDE), bf16),
            ((HID, WIDE), bf16), ((HID, WIDE), bf16), ((16, WIDE), f32),
        ],
        [
            ((2, deep, W_0, HALF), f32), taps_scratch, ((n_1, WIDE), f32), ((n_1, WIDE), f32),
            ((n_1, WIDE), f32), ((n_1, HALF), f32), ((n_1, WIDE), bf16), ((n_1, HID), bf16), ((n_1, HID), f32), ((n_1, WIDE), f32),
            ((WIDE, HID), bf16), ((HID, WIDE), bf16), ((n_1, WIDE), f32), ((n_1, WIDE), bf16), ((n_1, HID), bf16), ((n_1, WIDE), f32),
        ],
        4_000_000_000,
    )
    du1_a, du1_b = lat_halo(du1_send_a, du1_send_b)
    e_own, du0, du0_send_a, du0_send_b, keep_0, send_0, sums_0 = call(
        first_backward,
        "first_backward",
        (flags, du1, du1_a, du1_b, small_1, small_0, mask_0, own_0, row_0, e_0, normed, inverse, z, active, slope, branch, w_up, w_down),
        [
            ((ROWS_DEV, W_OWN, WIDE), f32), ((ROWS_DEV, W_0, WIDE), bf16), ((REACH, W_0, WIDE), bf16), ((REACH, W_0, WIDE), bf16),
            ((HID, WIDE), bf16), ((HID, WIDE), bf16), ((16, WIDE), f32),
        ],
        [
            ((2, deep, W_X, HALF), f32), taps_scratch, ((n_0, WIDE), f32), ((n_0, WIDE), f32), ((n_0, WIDE), bf16),
            ((n_0, WIDE), bf16), ((n_0, HID), bf16), ((n_0, WIDE), f32),
        ],
        3_000_000_000,
    )
    du0_a, du0_b = lat_halo(du0_send_a, du0_send_b)
    (taps_1,) = call(
        functools.partial(tap_grads, W_1), "tap_grads_1", (flags, y, y_a, y_b, du1, own_1, sums_1), [((SMALL, WIDE), bf16)],
        [((2, deep, W_0, HALF), f32), ((ROWS_DEV, W_1, WIDE), f32), ((SMALL, WIDE), f32)], 2_000_000_000,
    )
    (taps_0,) = call(
        functools.partial(tap_grads, W_0), "tap_grads_0", (flags, x_wide, x_a, x_b, du0, own_0, sums_0), [((SMALL, WIDE), bf16)],
        [((2, deep, W_X, HALF), f32), ((ROWS_DEV, W_0, WIDE), f32), ((SMALL, WIDE), f32)], 2_000_000_000,
    )
    (start,) = call(
        input_grad, "input_grad", (flags, du0, du0_a, du0_b, small_0, e_own), [((ROWS_DEV, COLS_DEV, WIDE), bf16)],
        [((2, deep, W_0, HALF), f32), taps_scratch, ((ROWS_DEV, W_OWN, WIDE), f32)], 2_000_000_000,
    )

    bits = [("lat", 1 << i) for i in range(1, n_lat.bit_length() - 1)] + [("lon", 1 << i) for i in range(n_lon.bit_length() - 1)]
    orders = (bits, bits[1:] + bits[:1])

    def partner(place, step):
        row, col = place
        axis, bit = orders[row % 2][step]
        return (row ^ bit, col) if axis == "lat" else (row, col ^ bit)

    def exchange(value, step):
        pairs = []
        for row in range(n_lat):
            for col in range(n_lon):
                other = partner((row, col), step)
                pairs.append((row * n_lon + col, other[0] * n_lon + other[1]))
        return lax.ppermute(value, ("lat", "lon"), pairs)

    def side(step):
        def of(order):
            axis, bit = order[step]
            return ((lat if axis == "lat" else lon) // bit) % 2

        return jnp.where(odd == 0, of(orders[0]), of(orders[1]))

    def plus(first, second):
        return (first.astype(f32) + second.astype(f32)).astype(bf16)

    def reduce_scatter(keep, send):
        piece = plus(keep, over_core(send))
        for step in range(len(bits)):
            half = piece.shape[0] // 2
            low, high = piece[:half], piece[half:]
            which = side(step) == 0
            piece = plus(jnp.where(which, low, high), exchange(jnp.where(which, high, low), step))
        return piece

    piece_1 = reduce_scatter(keep_1, send_1)
    piece_0 = reduce_scatter(keep_0, send_0)
    to_first = section == 0
    cut = piece_0.shape[0]

    def both(piece, small):
        return jnp.concatenate([piece, small], axis=0)

    def chosen(first, second):
        return jnp.where(to_first, first, second)

    got = over_section(both(chosen(piece_1, piece_0), chosen(taps_1, taps_0)))
    piece = plus(chosen(piece_0, piece_1), got[:cut])
    small = plus(chosen(taps_0, taps_1), got[cut:])
    for step in reversed(range(len(bits))):
        got = exchange(both(piece, small), step)
        cut = piece.shape[0]
        small = plus(small, got[cut:])
        which = side(step) == 0
        piece = jnp.where(which, jnp.concatenate([piece, got[:cut]]), jnp.concatenate([got[:cut], piece]))
    got = over_core(both(piece, small))
    cut = piece.shape[0]
    factor = 1.0 / math.sqrt(BATCH * ROWS_DEV * COLS_DEV)
    small = (small.astype(f32) + got[cut:].astype(f32)) * factor
    grad_up = by_core(piece, got[:cut]).astype(f32) * factor
    grad_down = by_core(got[:cut], piece).astype(f32) * factor
    grad_up = jnp.concatenate([grad_up[quarter * WIDE : (quarter + 1) * WIDE] for quarter in range(QUARTERS)], axis=1)

    other_end = over_section(chosen(final, start))
    boundary = jnp.stack([chosen(start, other_end), chosen(other_end, final)])[None]
    return (
        boundary,
        small[None, :TAPS],
        small[None, TAPS : TAPS + 5],
        grad_up[None],
        small[TAPS + 5 : TAPS + 9].reshape(1, HID),
        grad_down[None],
    )


def solution(mesh):
    in_specs = (
        P(None, "lat", "lon", None),
        P(None, "lat", "lon", None),
        P("lat", "lon"),
        P("section", None, None),
        P("section", None, None),
        P("section", None, None),
        P("section", None),
        P("section", None, None),
    )
    out_specs = (
        P("section", None, "lat", "lon", None),
        P("section", None, None),
        P("section", None, None),
        P("section", None, None),
        P("section", None),
        P("section", None, None),
    )
    return jax.shard_map(
        on_device, mesh=mesh, in_specs=in_specs, out_specs=out_specs, check_vma=False
    )
```

```python
import math

import jax
import jax.numpy as jnp
from jax import lax
from jax.experimental import pallas as pl
from jax.experimental.pallas import tpu as pltpu
from jax.sharding import PartitionSpec as P

KERNEL = 7
TAPS = KERNEL * KERNEL
REACH = KERNEL // 2
ROWS_DEV = 4
COLS_DEV = 68
BATCH = 2
HALF = 128
WIDE = 256
HID = 1024
QUARTERS = HID // WIDE
SIDE_X, SIDE_0, SIDE_1 = 12, 9, 6
W_X, W_0, W_1, W_OWN = 96, 88, 80, 72
CHUNK = 32
SMALL = 64
N_0, N_1 = ROWS_DEV * W_0, ROWS_DEV * W_1
AT_NORMED, AT_BASE, AT_INVERSE, AT_E_0, AT_E_1 = 0, N_0, 2 * N_0, 3 * N_0, 4 * N_0
KEPT_ROWS = 40960

norm_eps = 1e-06
gelu_scale = 0.7978845608028654
gelu_cubic = 0.044715
f32, bf16 = jnp.float32, jnp.bfloat16

nn = (((1,), (0,)), ((), ()))
nt = (((1,), (1,)), ((), ()))
tn = (((0,), (0,)), ((), ()))


def dot(left, right, dims=nn):
    return lax.dot_general(left, right, dims, preferred_element_type=f32)


def lanes(half):
    return slice(half * HALF, (half + 1) * HALF)


def load_padded(pad, odd, center, first, second, offset=0):
    width = center.shape[1]

    def put(row, value):
        value = value.astype(f32)
        for half in range(2):
            pad[half, row, offset : offset + width, :] = value[:, lanes(half)]

    at_first = jnp.where(odd == 1, 0, REACH + ROWS_DEV)
    at_second = jnp.where(odd == 1, REACH + ROWS_DEV, 0)
    for row in range(ROWS_DEV):
        put(REACH + row, center[row])
    for row in range(REACH):
        put(at_first + row, first[row])
        put(at_second + row, second[row])


def load_taps(taps, small):
    for half in range(2):
        taps[half] = jnp.broadcast_to(small[0:TAPS, lanes(half)][:, None, :], (TAPS, 8, HALF))


def groups(width, most):
    tiles = width // 8
    count = -(-tiles // most)
    bounds = [tiles * i // count for i in range(count + 1)]
    return [range(first, last) for first, last in zip(bounds, bounds[1:])]


def conv_tiles(pad, taps, half, starts, reverse):
    sums = [[None] * ROWS_DEV for _ in starts]
    for col_off in range(KERNEL):
        column = [taps[half, TAPS - 1 - tap if reverse else tap] for tap in range(col_off, TAPS, KERNEL)]
        for row in range(ROWS_DEV + KERNEL - 1):
            for index, start in enumerate(starts):
                window = pad[half, row, start + col_off : start + col_off + 8, :]
                for out_row in range(ROWS_DEV):
                    row_off = row - out_row
                    if 0 <= row_off < KERNEL:
                        term = window * column[row_off]
                        held = sums[index][out_row]
                        sums[index][out_row] = term if held is None else held + term
    return sums


def chunks(count, body, carry=0):
    for i in range(count // CHUNK):
        carry = body(slice(i * CHUNK, (i + 1) * CHUNK), carry)
    return carry


def fold(value):
    return jnp.sum(value.reshape(CHUNK // 8, 8, value.shape[-1]), axis=0)


def twice(value):
    return jnp.concatenate([value, value], axis=1)


def send_rows(odd, source, send_first, send_second):
    first, second = jnp.where(odd == 1, 0, 1), jnp.where(odd == 1, 1, 0)
    send_first[...] = source[pl.ds(first, REACH)]
    send_second[...] = source[pl.ds(second, REACH)]


def forward_conv(width, pad, taps, small, normed, inverse, z, base):
    count = ROWS_DEV * width
    load_taps(taps, small)
    for group in groups(width, 4):
        starts = [tile * 8 for tile in group]
        halves = [conv_tiles(pad, taps, half, starts, False) for half in range(2)]
        for index, row in [(index, row) for index in range(len(starts)) for row in range(ROWS_DEV)]:
            start = starts[index]
            u = [halves[half][index][row] + small[TAPS : TAPS + 1, lanes(half)] for half in range(2)]
            mean = jnp.sum(u[0] + u[1], axis=-1, keepdims=True) * (1.0 / WIDE)
            u = [value - mean for value in u]
            spread = jnp.sum(u[0] * u[0] + u[1] * u[1], axis=-1, keepdims=True) * (1.0 / WIDE)
            scale = lax.rsqrt(spread + norm_eps)
            at = slice(row * width + start, row * width + start + 8)
            inverse[at, :] = jnp.broadcast_to(scale, (8, HALF))
            for half in range(2):
                normed[at, lanes(half)] = u[half] * scale
                base[at, lanes(half)] = pad[half, REACH + row, start + REACH : start + REACH + 8, :]
    scale_cells(count, small, normed, z)


def scale_cells(count, small, normed, z):
    def scaled(at, carry):
        z[at, :] = (normed[at, :] * small[TAPS + 1 : TAPS + 2, :] + small[TAPS + 2 : TAPS + 3, :]).astype(bf16)
        return carry

    chunks(count, scaled, 0)


def forward_mlp(width, small, mask, w_up, w_down, z, base, hidden, active, slope, branch, out):
    count = ROWS_DEV * width
    for quarter in range(QUARTERS):
        cols = slice(quarter * WIDE, (quarter + 1) * WIDE)
        held = hidden.at[quarter % 2]
        held[...] = dot(z[...], w_up[:, cols])
        bias = small[TAPS + 5 + quarter : TAPS + 6 + quarter, :]

        def gelu(at, carry, held=held, cols=cols, bias=bias):
            h = held[at, :] + bias
            square = h * h
            tangent = jnp.tanh(h * (gelu_scale + (gelu_scale * gelu_cubic) * square))
            above = 0.5 + 0.5 * tangent
            active[at, cols] = (h * above).astype(bf16)
            slope[at, cols] = above + (0.5 * h) * (1.0 - tangent * tangent) * (
                gelu_scale + (3.0 * gelu_scale * gelu_cubic) * square
            )
            return carry

        chunks(count, gelu, 0)
    branch[...] = dot(active[...], w_down[...]) + small[TAPS + 3 : TAPS + 4, :]
    if out is None:
        return

    def residual(at, carry):
        out[at, :] = twice(mask[at, :]) * (base[at, :] + small[TAPS + 4 : TAPS + 5, :] * branch[at, :])
        return carry

    chunks(count, residual, 0)


def backward_cells(
    width, odd, small, own, own_row, upstream, w_up, w_down, normed, inverse, z, active, slope, branch, hidden, dm, dh, du, keep, send, sums
):
    count = ROWS_DEV * width
    zero = jnp.zeros((8, WIDE), f32)

    def first(at, carry):
        sum_dm, sum_em = carry
        e = upstream[at, :]
        inside = twice(own[at, :])
        grad = (e * small[TAPS + 4 : TAPS + 5, :]).astype(bf16)
        dm[at, :] = grad
        sum_dm = sum_dm + fold(grad.astype(f32) * inside)
        sum_em = sum_em + fold(e * branch[at, :] * inside)
        return sum_dm, sum_em

    sum_dm, sum_em = chunks(count, first, (zero, zero))
    for quarter in range(QUARTERS):
        cols = slice(quarter * WIDE, (quarter + 1) * WIDE)
        held = hidden.at[quarter % 2]
        held[...] = dot(dm[...], w_down[cols, :], nt)

        def through(at, carry, held=held, cols=cols):
            dh[at, cols] = (held[at, :] * slope[at, cols]).astype(bf16)
            return carry

        chunks(count, through, 0)
    hidden[0] = dot(dh[...], w_up[...], nt)
    sum_dh = dot(own_row[...], dh[...])

    def norm(at, carry):
        sum_dzn, sum_dz, sum_du = carry
        dz = hidden[0, at, :]
        normal = normed[at, :]
        inside = twice(own[at, :])
        inner = dz * inside
        sum_dz = sum_dz + fold(inner)
        sum_dzn = sum_dzn + fold(inner * normal)
        dn = dz * small[TAPS + 1 : TAPS + 2, :]
        mean = jnp.sum(dn, axis=-1, keepdims=True) * (1.0 / WIDE)
        slant = jnp.sum(dn * normal, axis=-1, keepdims=True) * (1.0 / WIDE)
        grad = (twice(inverse[at, :]) * (dn - mean - normal * slant)).astype(bf16).astype(f32)
        du[at, :] = grad
        sum_du = sum_du + fold(grad * inside)
        dm[at, :] = (dm[at, :].astype(f32) * inside).astype(bf16)
        z[at, :] = (z[at, :].astype(f32) * inside).astype(bf16)
        return sum_dzn, sum_dz, sum_du

    sum_dzn, sum_dz, sum_du = chunks(count, norm, (zero, zero, zero))
    rows = [jnp.sum(value, axis=0, keepdims=True) for value in (sum_du, sum_dzn, sum_dz, sum_dm, sum_em)]
    rows += [sum_dh[0:1, quarter * WIDE : (quarter + 1) * WIDE] for quarter in range(QUARTERS)]
    for index, value in enumerate(rows):
        sums[index : index + 1, :] = value
    sums[len(rows) : 16, :] = jnp.zeros((16 - len(rows), WIDE), f32)

    def weights(up_ref, down_ref):
        for quarter in range(QUARTERS):
            cols = slice(quarter * WIDE, (quarter + 1) * WIDE)
            up_ref[cols, :] = dot(z[...], dh[:, cols], tn).astype(bf16)
            down_ref[cols, :] = dot(active[:, cols], dm[...], tn).astype(bf16)

    @pl.when(odd == 0)
    def _():
        weights(keep, send)

    @pl.when(odd == 1)
    def _():
        weights(send, keep)


def weight_copies(block, flags, parts, w_up, w_down, sems, act):
    odd, section = flags[0], flags[1]
    own_up, own_down, got_up, got_down, other_up, other_down = parts

    @pl.when(section == block)
    def _():
        act(pltpu.make_async_copy(own_up, w_up, sems.at[0]))
        act(pltpu.make_async_copy(own_down, w_down, sems.at[1]))

    @pl.when(section != block)
    def _():
        for index, (ref, mine, other) in enumerate(((w_up, got_up, other_up), (w_down, got_down, other_down))):
            half = mine.shape[0]
            for place, part in enumerate((mine, other)):
                first = odd if place == 0 else 1 - odd
                rows = pl.ds(pl.multiple_of(first * half, half), half)
                act(pltpu.make_async_copy(part, ref.at[rows, :], sems.at[2 + 2 * index + place]))


def start_copy(copy):
    copy.start()


def wait_copy(copy):
    copy.wait()


def write_rows(source, width, out):
    for row in range(ROWS_DEV):
        out[row] = source[row * width : (row + 1) * width, :].astype(bf16)


def kept_copies(kept, sems, places, out):
    copies = []
    for index, (ref, first) in enumerate(places):
        rows = kept.at[first : first + ref.shape[0], 0 : ref.shape[1]]
        copies.append(pltpu.make_async_copy(ref, rows, sems.at[index]) if out else pltpu.make_async_copy(rows, ref, sems.at[index]))
    return copies


def first_conv(
    flags, x, x_a, x_b, small, mask, cot, left, right, kept, pad, taps, wide, normed, inverse, z, base, e_1, sems
):
    places = [(wide, AT_E_0), (e_1, AT_E_1), (normed, AT_NORMED), (base, AT_BASE), (inverse, AT_INVERSE)]
    copies = kept_copies(kept, sems, places, True)
    before = SIDE_0 - SIDE_1
    wide[...] = jnp.zeros((N_0, WIDE), f32)
    for row in range(ROWS_DEV):
        at = row * W_0 + before
        wide[at : at + SIDE_1, :] = left[row].astype(f32)[SIDE_X : SIDE_X + SIDE_1]
        wide[at + SIDE_1 : at + SIDE_1 + COLS_DEV, :] = cot[row].astype(f32)
        wide[at + SIDE_1 + COLS_DEV : at + W_1, :] = right[row].astype(f32)[SIDE_X : SIDE_X + SIDE_1]
    wide[...] = wide[...] * twice(mask[...])
    for row in range(ROWS_DEV):
        at = row * W_0 + before
        e_1[row * W_1 : (row + 1) * W_1, :] = wide[at : at + W_1, :]
    for copy in copies[:2]:
        copy.start()
    load_padded(pad, flags[0], x, x_a, x_b)
    forward_conv(W_0, pad, taps, small, normed, inverse, z, base)
    for copy in copies[2:]:
        copy.start()
    for copy in copies:
        copy.wait()


def first_forward(flags, small, mask, kept, *refs):
    parts, refs = refs[:6], refs[6:]
    y, send_a, send_b, normed, z, base, hidden, out, active, slope, branch, w_up, w_down, weight_sems, sems = refs
    copies = kept_copies(kept, sems, [(normed, AT_NORMED), (base, AT_BASE)], False)
    for copy in copies:
        copy.start()
    weight_copies(0, flags, parts, w_up, w_down, weight_sems, start_copy)
    for copy in copies:
        copy.wait()
    scale_cells(N_0, small, normed, z)
    weight_copies(0, flags, parts, w_up, w_down, weight_sems, wait_copy)
    forward_mlp(W_0, small, mask, w_up, w_down, z, base, hidden, active, slope, branch, out)
    write_rows(out, W_0, y)
    send_rows(flags[0], y, send_a, send_b)


def first_again(flags, small, kept, *refs):
    parts, refs = refs[:6], refs[6:]
    active, slope, branch, w_up, w_down, normed, z, hidden, weight_sems, sems = refs
    (copy,) = kept_copies(kept, sems, [(normed, AT_NORMED)], False)
    copy.start()
    weight_copies(0, flags, parts, w_up, w_down, weight_sems, start_copy)
    copy.wait()
    scale_cells(N_0, small, normed, z)
    weight_copies(0, flags, parts, w_up, w_down, weight_sems, wait_copy)
    forward_mlp(W_0, small, None, w_up, w_down, z, None, hidden, active, slope, branch, None)


def second_block(flags, y, y_a, y_b, small, mask, own, own_row, kept, *refs):
    parts, refs = refs[:6], refs[6:]
    final, du_out, send_a, send_b, keep, send, sums, pad = refs[:8]
    taps, hidden, out, normed, inverse, z, base, active, slope, branch, w_up, w_down, upstream, dm, dh, du, weight_sems, sems = refs[8:]
    (copy,) = kept_copies(kept, sems, [(upstream, AT_E_1)], False)
    copy.start()
    weight_copies(1, flags, parts, w_up, w_down, weight_sems, start_copy)
    load_padded(pad, flags[0], y, y_a, y_b)
    forward_conv(W_1, pad, taps, small, normed, inverse, z, base)
    weight_copies(1, flags, parts, w_up, w_down, weight_sems, wait_copy)
    copy.wait()
    forward_mlp(W_1, small, mask, w_up, w_down, z, base, hidden, active, slope, branch, out)
    for row in range(ROWS_DEV):
        at = row * W_1 + SIDE_1
        final[row] = out[at : at + COLS_DEV, :].astype(bf16)
    backward_cells(
        W_1, flags[0], small, own, own_row, upstream, w_up, w_down, normed, inverse, z, active, slope, branch, hidden, dm, dh, du, keep, send, sums
    )
    write_rows(du, W_1, du_out)
    send_rows(flags[0], du_out, send_a, send_b)


def first_backward(
    flags, du1, du1_a, du1_b, small1, small0, mask, own, own_row, active, slope, branch, w_up, w_down, kept,
    e_own, du_out, send_a, send_b, keep, send, sums,
    pad, taps, hidden, upstream, z, dm, dh, du, normed, inverse, sems,
):
    copies = kept_copies(kept, sems, [(upstream, AT_E_0), (normed, AT_NORMED), (inverse, AT_INVERSE)], False)
    for copy in copies:
        copy.start()
    shift = SIDE_0 + REACH - SIDE_1
    pad[:, :, 0:8, :] = jnp.zeros((2, ROWS_DEV + 2 * REACH, 8, HALF), f32)
    pad[:, :, W_X - 16 : W_X, :] = jnp.zeros((2, ROWS_DEV + 2 * REACH, 16, HALF), f32)
    load_padded(pad, flags[0], du1, du1_a, du1_b, shift)
    load_taps(taps, small1)
    for copy in copies:
        copy.wait()
    for group in groups(W_0, 4):
        starts = [tile * 8 for tile in group]
        for half in range(2):
            spread = conv_tiles(pad, taps, half, starts, True)
            for index, start in enumerate(starts):
                for row in range(ROWS_DEV):
                    at = slice(row * W_0 + start, row * W_0 + start + 8)
                    value = (upstream[at, lanes(half)] + spread[index][row]).astype(bf16).astype(f32)
                    upstream[at, lanes(half)] = mask[at, :] * value
    for row in range(ROWS_DEV):
        at = row * W_0 + SIDE_0
        e_own[row] = upstream[at : at + W_OWN, :]
    scale_cells(N_0, small0, normed, z)
    backward_cells(
        W_0, flags[0], small0, own, own_row, upstream, w_up, w_down, normed, inverse, z, active, slope, branch, hidden, dm, dh, du, keep, send, sums
    )
    write_rows(du, W_0, du_out)
    send_rows(flags[0], du_out, send_a, send_b)


def input_grad(flags, du, du_a, du_b, small, e_own, out, pad, taps, total):
    load_padded(pad, flags[0], du, du_a, du_b)
    load_taps(taps, small)
    for group in groups(W_OWN, 5):
        starts = [tile * 8 for tile in group]
        for half in range(2):
            spread = conv_tiles(pad, taps, half, [start + SIDE_0 - REACH for start in starts], True)
            for index, start in enumerate(starts):
                for row in range(ROWS_DEV):
                    at = slice(start, start + 8)
                    total[row, at, lanes(half)] = e_own[row, at, lanes(half)] + spread[index][row]
    for row in range(ROWS_DEV):
        out[row] = total[row, 0:COLS_DEV, :].astype(bf16)


def tap_grads_1(flags, pad, du, own, sums, out, grads, total):
    tap_sums(W_1, pad, du, own, sums, out, grads, total)


def tap_grads_0(flags, v, v_a, v_b, du, own, sums, out, pad, grads, total):
    load_padded(pad, flags[0], v, v_a, v_b)
    tap_sums(W_0, pad, du, own, sums, out, grads, total)


def tap_sums(width, pad, du, own, sums, out, grads, total):
    for row in range(ROWS_DEV):
        inside = own[row * width : (row + 1) * width, :]
        grads[row] = du[row].astype(f32) * twice(inside)
    total[...] = jnp.zeros((SMALL, WIDE), f32)
    for half in range(2):
        for offsets in (range(0, 4), range(4, KERNEL)):
            partial = [[None] * KERNEL for _ in offsets]
            for tile in range(width // 8):
                start = tile * 8
                grad = [grads[row, start : start + 8, lanes(half)] for row in range(ROWS_DEV)]
                for row in range(ROWS_DEV + KERNEL - 1):
                    for index, col_off in enumerate(offsets):
                        window = pad[half, row, start + col_off : start + col_off + 8, :]
                        for out_row in range(ROWS_DEV):
                            row_off = row - out_row
                            if 0 <= row_off < KERNEL:
                                term = window * grad[out_row]
                                held = partial[index][row_off]
                                partial[index][row_off] = term if held is None else held + term
            for index, col_off in enumerate(offsets):
                for row_off in range(KERNEL):
                    tap = row_off * KERNEL + col_off
                    total[tap : tap + 1, lanes(half)] = jnp.sum(partial[index][row_off], axis=0, keepdims=True)
    total[TAPS : TAPS + 9, :] = sums[0:9, :]
    out[...] = total[...].astype(bf16)


def finish(flags, piece, small, got, up, down, taps, channels, bias, up_vmem, down_vmem, sems):
    factor = 1.0 / math.sqrt(BATCH * ROWS_DEV * COLS_DEV)

    def copies(quarter):
        cols = slice(quarter * WIDE, (quarter + 1) * WIDE)
        return (
            pltpu.make_async_copy(up_vmem.at[:, cols], up.at[0, :, cols], sems.at[0, quarter]),
            pltpu.make_async_copy(down_vmem.at[cols, :], down.at[0, cols, :], sems.at[1, quarter]),
        )

    def write(up_rows, down_rows):
        for quarter in range(QUARTERS):
            cols = slice(quarter * WIDE, (quarter + 1) * WIDE)
            up_vmem[:, cols] = up_rows[cols, :].astype(f32) * factor
            down_vmem[cols, :] = down_rows[cols, :].astype(f32) * factor
            for copy in copies(quarter):
                copy.start()

    @pl.when(flags[0] == 0)
    def _():
        write(piece, got)

    @pl.when(flags[0] == 1)
    def _():
        write(got, piece)

    sums = (small[...].astype(f32) + got[HID:, :].astype(f32)) * factor
    taps[0] = sums[:TAPS]
    channels[0] = sums[TAPS : TAPS + 5]
    for quarter in range(QUARTERS):
        bias[:, quarter * WIDE : (quarter + 1) * WIDE] = sums[TAPS + 5 + quarter : TAPS + 6 + quarter]
    for quarter in range(QUARTERS):
        for copy in copies(quarter):
            copy.wait()


def in_vmem():
    return pl.BlockSpec(memory_space=pltpu.VMEM)


def call(body, name, inputs, outputs, scratch, flops, hbm_in=0, hbm_out=0, sems=()):
    in_hbm = pl.BlockSpec(memory_space=pltpu.HBM)
    return pl.pallas_call(
        body,
        name=name,
        out_shape=[jax.ShapeDtypeStruct(shape, dtype) for shape, dtype in outputs],
        in_specs=[pl.BlockSpec(memory_space=pltpu.SMEM)] + [in_vmem()] * (len(inputs) - 1 - hbm_in) + [in_hbm] * hbm_in,
        out_specs=[in_hbm] * hbm_out + [in_vmem()] * (len(outputs) - hbm_out),
        scratch_shapes=[pltpu.VMEM(shape, dtype) for shape, dtype in scratch] + [pltpu.SemaphoreType.DMA(shape) for shape in sems],
        compiler_params=pltpu.CompilerParams(vmem_limit_bytes=28 << 20),
        cost_estimate=pl.CostEstimate(flops=10 * flops, bytes_accessed=4 << 20, transcendentals=0),
    )(*inputs)


def swap_pairs(count, bit):
    return [(i, i ^ bit) for i in range(count)]


def on_device(
    window_input,
    output_cotangent,
    ocean_mask,
    dw_kernel,
    channel_params,
    up_weight,
    up_bias,
    down_weight,
):
    section = lax.axis_index("section")
    lat = lax.axis_index("lat")
    lon = lax.axis_index("lon")
    n_lat, n_lon = lax.axis_size("lat"), lax.axis_size("lon")
    odd = lat % 2
    flags = jnp.stack([odd, section]).astype(jnp.int32)
    channels = window_input.shape[-1]

    def over_section(value):
        return lax.ppermute(value, "section", [(0, 1), (1, 0)])

    def over_core(value):
        return lax.ppermute(value, "lat", swap_pairs(n_lat, 1))

    def lat_halo(send_a, send_b):
        pairs = [(i, i + 1) for i in range(1, n_lat - 1, 2)]
        pairs += [(j, i) for i, j in pairs]
        return over_core(send_a), lax.ppermute(send_b, "lat", pairs)

    def by_core(even, other):
        return jnp.where(odd == 0, even, other)

    x = lax.dynamic_index_in_dim(window_input, section, 0, False)
    cot = lax.dynamic_index_in_dim(output_cotangent, section, 0, False)
    sea = ocean_mask.astype(bf16)

    def packed(x_part, cot_part, sea_part):
        sea_row = jnp.pad(sea_part, ((0, 0), (0, channels - sea_part.shape[1])))[:, None, :]
        return jnp.concatenate([x_part, cot_part, sea_row], axis=1)

    ring = [(i, (i + 1) % n_lon) for i in range(n_lon)]
    left = lax.ppermute(packed(x[:, -SIDE_X:], cot[:, -SIDE_1:], sea[:, -SIDE_0:]), "lon", ring)
    right = lax.ppermute(packed(x[:, :SIDE_X], cot[:, :SIDE_1], sea[:, :SIDE_0]), "lon", [(j, i) for i, j in ring])
    small_own = jnp.concatenate(
        [dw_kernel[0], channel_params[0], up_bias[0].reshape(QUARTERS, WIDE), jnp.zeros((SMALL - TAPS - 9, WIDE), bf16)], axis=0
    )
    up, down = up_weight[0], down_weight[0]
    cut = channels // 2
    small_got = over_section(small_own)
    send_up = by_core(up[:cut], up[cut:])
    send_down = by_core(down[: HID // 2], down[HID // 2 :])
    send_up, send_down, left, right, small_got = lax.optimization_barrier((send_up, send_down, left, right, small_got))
    got_up, got_down = over_section(send_up), over_section(send_down)
    small_0 = jnp.where(section == 0, small_own, small_got).astype(f32)
    small_1 = jnp.where(section == 0, small_got, small_own).astype(f32)

    before = SIDE_0 - SIDE_1
    sea_at = SIDE_X + SIDE_1
    x_wide = jnp.concatenate([left[:, :SIDE_X], x, right[:, :SIDE_X], jnp.zeros((ROWS_DEV, W_X - COLS_DEV - 2 * SIDE_X, channels), bf16)], axis=1)
    x_a, x_b = lat_halo(by_core(x_wide[1:], x_wide[:REACH]), by_core(x_wide[:REACH], x_wide[1:]))
    mask_wide = jnp.concatenate(
        [left[:, sea_at, :SIDE_0], sea, right[:, sea_at, :SIDE_0], jnp.zeros((ROWS_DEV, W_0 - COLS_DEV - 2 * SIDE_0), bf16)], axis=1
    )
    before = SIDE_0 - SIDE_1
    def spread_lanes(mask):
        flat = mask.astype(f32).reshape(-1, 1)
        return jnp.broadcast_to(flat, (flat.shape[0], HALF))

    mask_0, mask_1 = spread_lanes(mask_wide), spread_lanes(mask_wide[:, before : before + W_1])

    def own_cells(width, side):
        column = jnp.arange(width)
        inside = ((column >= side) & (column < side + COLS_DEV)).astype(f32)
        flat = jnp.tile(inside, ROWS_DEV)
        return jnp.broadcast_to(flat[:, None], (flat.shape[0], HALF)), jnp.broadcast_to(flat[None, :], (16, flat.shape[0])).astype(bf16)

    owN_0, row_0 = own_cells(W_0, SIDE_0)
    owN_1, row_1 = own_cells(W_1, SIDE_1)

    deep = ROWS_DEV + 2 * REACH
    taps_scratch = ((2, TAPS, 8, HALF), f32)

    (kept,) = call(
        first_conv,
        "first_conv",
        (flags, x_wide, x_a, x_b, small_0, mask_0, cot, left, right),
        [((KEPT_ROWS, WIDE), f32)],
        [
            ((2, deep, W_X, HALF), f32), taps_scratch, ((N_0, WIDE), f32), ((N_0, WIDE), f32), ((N_0, HALF), f32),
            ((N_0, WIDE), bf16), ((N_0, WIDE), f32), ((N_1, WIDE), f32),
        ],
        2_000_000_000,
        hbm_out=1,
        sems=((5,),),
    )
    got_up, got_down, kept = lax.optimization_barrier((got_up, got_down, kept))
    other_up, other_down = over_core(got_up), over_core(got_down)
    weights = (up, down, got_up, got_down, other_up, other_down)
    y, y_send_a, y_send_b = call(
        first_forward,
        "first_forward",
        (flags, small_0, mask_0, kept) + weights,
        [((ROWS_DEV, W_0, WIDE), bf16), ((REACH, W_0, WIDE), bf16), ((REACH, W_0, WIDE), bf16)],
        [
            ((N_0, WIDE), f32), ((N_0, WIDE), bf16), ((N_0, WIDE), f32), ((2, N_0, WIDE), f32), ((N_0, WIDE), f32),
            ((N_0, HID), bf16), ((N_0, HID), f32), ((N_0, WIDE), f32), ((WIDE, HID), bf16), ((HID, WIDE), bf16),
        ],
        2_000_000_000,
        hbm_in=7,
        sems=((6,), (2,)),
    )
    y_a, y_b = lat_halo(y_send_a, y_send_b)
    final, du1, du1_send_a, du1_send_b, keep_1, send_1, sums_1, pad_1 = call(
        second_block,
        "second_block",
        (flags, y, y_a, y_b, small_1, mask_1, owN_1, row_1, kept) + weights,
        [
            ((ROWS_DEV, COLS_DEV, WIDE), bf16), ((ROWS_DEV, W_1, WIDE), bf16), ((REACH, W_1, WIDE), bf16), ((REACH, W_1, WIDE), bf16),
            ((HID, WIDE), bf16), ((HID, WIDE), bf16), ((16, WIDE), f32), ((2, deep, W_0, HALF), f32),
        ],
        [
            taps_scratch, ((2, N_1, WIDE), f32), ((N_1, WIDE), f32),
            ((N_1, WIDE), f32), ((N_1, HALF), f32), ((N_1, WIDE), bf16), ((N_1, WIDE), f32), ((N_1, HID), bf16), ((N_1, HID), f32), ((N_1, WIDE), f32),
            ((WIDE, HID), bf16), ((HID, WIDE), bf16), ((N_1, WIDE), f32), ((N_1, WIDE), bf16), ((N_1, HID), bf16), ((N_1, WIDE), f32),
        ],
        4_000_000_000,
        hbm_in=7,
        sems=((6,), (1,)),
    )
    du1_a, du1_b = lat_halo(du1_send_a, du1_send_b)
    small_again, _ = lax.optimization_barrier((small_0, du1_send_a))
    active, slope, branch, w_up, w_down = call(
        first_again,
        "first_again",
        (flags, small_again, kept) + weights,
        [((N_0, HID), bf16), ((N_0, HID), f32), ((N_0, WIDE), f32), ((WIDE, HID), bf16), ((HID, WIDE), bf16)],
        [((N_0, WIDE), f32), ((N_0, WIDE), bf16), ((2, N_0, WIDE), f32)],
        2_000_000_000,
        hbm_in=7,
        sems=((6,), (1,)),
    )
    send_1, du1_a, du1_b, active = lax.optimization_barrier((send_1, du1_a, du1_b, active))
    e_own, du0, du0_send_a, du0_send_b, keep_0, send_0, sums_0 = call(
        first_backward,
        "first_backward",
        (flags, du1, du1_a, du1_b, small_1, small_0, mask_0, owN_0, row_0, active, slope, branch, w_up, w_down, kept),
        [
            ((ROWS_DEV, W_OWN, WIDE), f32), ((ROWS_DEV, W_0, WIDE), bf16), ((REACH, W_0, WIDE), bf16), ((REACH, W_0, WIDE), bf16),
            ((HID, WIDE), bf16), ((HID, WIDE), bf16), ((16, WIDE), f32),
        ],
        [
            ((2, deep, W_X, HALF), f32), taps_scratch, ((2, N_0, WIDE), f32), ((N_0, WIDE), f32), ((N_0, WIDE), bf16),
            ((N_0, WIDE), bf16), ((N_0, HID), bf16), ((N_0, WIDE), f32),
            ((N_0, WIDE), f32), ((N_0, HALF), f32),
        ],
        3_000_000_000,
        hbm_in=1,
        sems=((3,),),
    )
    bits = [("lat", 1 << i) for i in range(1, n_lat.bit_length() - 1)] + [("lon", 1 << i) for i in range(n_lon.bit_length() - 1)]
    orders = (bits, bits[1:] + bits[:1])

    def partner(place, step):
        row, col = place
        axis, bit = orders[row % 2][step]
        return (row ^ bit, col) if axis == "lat" else (row, col ^ bit)

    def exchange(value, step):
        pairs = []
        for row in range(n_lat):
            for col in range(n_lon):
                other = partner((row, col), step)
                pairs.append((row * n_lon + col, other[0] * n_lon + other[1]))
        return lax.ppermute(value, ("lat", "lon"), pairs)

    def side(step):
        def of(order):
            axis, bit = order[step]
            return ((lat if axis == "lat" else lon) // bit) % 2

        return jnp.where(odd == 0, of(orders[0]), of(orders[1]))

    def plus(first, second):
        return (first.astype(f32) + second.astype(f32)).astype(bf16)

    def reduce_scatter(keep, send):
        piece = plus(keep, over_core(send))
        for step in range(len(bits)):
            half = piece.shape[0] // 2
            low, high = piece[:half], piece[half:]
            which = side(step) == 0
            piece = plus(jnp.where(which, low, high), exchange(jnp.where(which, high, low), step))
        return piece

    def reduce_step(piece, step):
        half = piece.shape[0] // 2
        low, high = piece[:half], piece[half:]
        which = side(step) == 0
        return plus(jnp.where(which, low, high), exchange(jnp.where(which, high, low), step))

    to_first = section == 0

    def chosen(first, second):
        return jnp.where(to_first, first, second)

    core_1 = over_core(send_1)
    core_0 = over_core(send_0)
    piece_1 = plus(keep_1, core_1)
    du0_a, du0_b = lat_halo(du0_send_a, du0_send_b)
    (taps_1,) = call(
        tap_grads_1, "tap_grads_1", (flags, pad_1, du1, owN_1, sums_1), [((SMALL, WIDE), bf16)],
        [((ROWS_DEV, W_1, WIDE), f32), ((SMALL, WIDE), f32)], 2_000_000_000,
    )
    (taps_0,) = call(
        tap_grads_0, "tap_grads_0", (flags, x_wide, x_a, x_b, du0, owN_0, sums_0), [((SMALL, WIDE), bf16)],
        [((2, deep, W_X, HALF), f32), ((ROWS_DEV, W_0, WIDE), f32), ((SMALL, WIDE), f32)], 2_000_000_000,
    )
    piece_0, taps_0, taps_1 = lax.optimization_barrier((plus(keep_0, core_0), taps_0, taps_1))
    steps = len(bits)
    for step in range(steps):
        piece_1, piece_0 = reduce_step(piece_1, step), reduce_step(piece_0, step)
        if step == 0:
            (start,) = call(
                input_grad, "input_grad", (flags, du0, du0_a, du0_b, small_0, e_own), [((ROWS_DEV, COLS_DEV, WIDE), bf16)],
                [((2, deep, W_0, HALF), f32), taps_scratch, ((ROWS_DEV, W_OWN, WIDE), f32)], 2_000_000_000,
            )
            other_end = over_section(chosen(final, start))
            piece_0, start = lax.optimization_barrier((piece_0, start))
    cut = piece_0.shape[0]
    piece_0, other_end = lax.optimization_barrier((piece_0, other_end))
    boundary = jnp.stack([chosen(start, other_end), chosen(other_end, final)])[None]

    def both(piece, small):
        return jnp.concatenate([piece, small], axis=0)

    got = over_section(both(chosen(piece_1, piece_0), chosen(taps_1, taps_0)))
    got, boundary = lax.optimization_barrier((got, boundary))
    piece = plus(chosen(piece_0, piece_1), got[:cut])
    small = plus(chosen(taps_0, taps_1), got[cut:])
    for step in reversed(range(len(bits))):
        got = exchange(both(piece, small), step)
        cut = piece.shape[0]
        small = plus(small, got[cut:])
        which = side(step) == 0
        piece = jnp.where(which, jnp.concatenate([piece, got[:cut]]), jnp.concatenate([got[:cut], piece]))
    got = over_core(both(piece, small))
    grad_up, grad_down, grad_taps, grad_channels, grad_bias = call(
        finish,
        "finish",
        (flags, piece, small, got),
        [((1, WIDE, HID), f32), ((1, HID, WIDE), f32), ((1, TAPS, WIDE), f32), ((1, 5, WIDE), f32), ((1, HID), f32)],
        [((WIDE, HID), f32), ((HID, WIDE), f32)],
        10_000_000,
        hbm_out=2,
        sems=((2, QUARTERS),),
    )
    return (
        boundary,
        grad_taps,
        grad_channels,
        grad_up,
        grad_bias,
        grad_down,
    )


def solution(mesh):
    in_specs = (
        P(None, "lat", "lon", None),
        P(None, "lat", "lon", None),
        P("lat", "lon"),
        P("section", None, None),
        P("section", None, None),
        P("section", None, None),
        P("section", None),
        P("section", None, None),
    )
    out_specs = (
        P("section", None, "lat", "lon", None),
        P("section", None, None),
        P("section", None, None),
        P("section", None, None),
        P("section", None),
        P("section", None, None),
    )
    return jax.shard_map(
        on_device, mesh=mesh, in_specs=in_specs, out_specs=out_specs, check_vma=False
    )
```

```python
import math

import jax
import jax.numpy as jnp
from jax import lax
from jax.experimental import pallas as pl
from jax.experimental.pallas import tpu as pltpu
from jax.sharding import PartitionSpec as P

KERNEL = 7
TAPS = KERNEL * KERNEL
REACH = KERNEL // 2
ROWS_DEV = 4
COLS_DEV = 68
BATCH = 2
HALF = 128
WIDE = 256
HID = 1024
QUARTERS = HID // WIDE
SIDE_X, SIDE_0, SIDE_1 = 12, 9, 6
W_X, W_0, W_1, W_OWN = 96, 88, 80, 72
CHUNK = 32
SMALL = 64
N_0, N_1 = ROWS_DEV * W_0, ROWS_DEV * W_1
AT_NORMED, AT_BASE, AT_INVERSE, AT_E_0, AT_E_1 = 0, N_0, 2 * N_0, 3 * N_0, 4 * N_0
KEPT_ROWS = 40960

norm_eps = 1e-06
gelu_scale = 0.7978845608028654
gelu_cubic = 0.044715
f32, bf16 = jnp.float32, jnp.bfloat16

nn = (((1,), (0,)), ((), ()))
nt = (((1,), (1,)), ((), ()))
tn = (((0,), (0,)), ((), ()))


def dot(left, right, dims=nn):
    return lax.dot_general(left, right, dims, preferred_element_type=f32)


def lanes(half):
    return slice(half * HALF, (half + 1) * HALF)


def load_padded(pad, odd, center, first, second, offset=0):
    width = center.shape[1]

    def put(row, value):
        value = value.astype(f32)
        for half in range(2):
            pad[half, row, offset : offset + width, :] = value[:, lanes(half)]

    at_first = jnp.where(odd == 1, 0, REACH + ROWS_DEV)
    at_second = jnp.where(odd == 1, REACH + ROWS_DEV, 0)
    for row in range(ROWS_DEV):
        put(REACH + row, center[row])
    for row in range(REACH):
        put(at_first + row, first[row])
        put(at_second + row, second[row])


def load_taps(taps, small):
    for half in range(2):
        taps[half] = jnp.broadcast_to(small[0:TAPS, lanes(half)][:, None, :], (TAPS, 8, HALF))


def groups(width, most):
    tiles = width // 8
    count = -(-tiles // most)
    bounds = [tiles * i // count for i in range(count + 1)]
    return [range(first, last) for first, last in zip(bounds, bounds[1:])]


def conv_tiles(pad, taps, half, starts, reverse):
    sums = [[None] * ROWS_DEV for _ in starts]
    for col_off in range(KERNEL):
        column = [taps[half, TAPS - 1 - tap if reverse else tap] for tap in range(col_off, TAPS, KERNEL)]
        for row in range(ROWS_DEV + KERNEL - 1):
            for index, start in enumerate(starts):
                window = pad[half, row, start + col_off : start + col_off + 8, :]
                for out_row in range(ROWS_DEV):
                    row_off = row - out_row
                    if 0 <= row_off < KERNEL:
                        term = window * column[row_off]
                        held = sums[index][out_row]
                        sums[index][out_row] = term if held is None else held + term
    return sums


def chunks(count, body, carry=0):
    for i in range(count // CHUNK):
        carry = body(slice(i * CHUNK, (i + 1) * CHUNK), carry)
    return carry


def fold(value):
    return jnp.sum(value.reshape(CHUNK // 8, 8, value.shape[-1]), axis=0)


def twice(value):
    return jnp.concatenate([value, value], axis=1)


def send_rows(odd, source, send_first, send_second):
    first, second = jnp.where(odd == 1, 0, 1), jnp.where(odd == 1, 1, 0)
    send_first[...] = source[pl.ds(first, REACH)]
    send_second[...] = source[pl.ds(second, REACH)]


def forward_conv(width, pad, taps, small, normed, inverse, z, base):
    count = ROWS_DEV * width
    load_taps(taps, small)
    for group in groups(width, 4):
        starts = [tile * 8 for tile in group]
        halves = [conv_tiles(pad, taps, half, starts, False) for half in range(2)]
        for index, row in [(index, row) for index in range(len(starts)) for row in range(ROWS_DEV)]:
            start = starts[index]
            u = [halves[half][index][row] + small[TAPS : TAPS + 1, lanes(half)] for half in range(2)]
            mean = jnp.sum(u[0] + u[1], axis=-1, keepdims=True) * (1.0 / WIDE)
            u = [value - mean for value in u]
            spread = jnp.sum(u[0] * u[0] + u[1] * u[1], axis=-1, keepdims=True) * (1.0 / WIDE)
            scale = lax.rsqrt(spread + norm_eps)
            at = slice(row * width + start, row * width + start + 8)
            inverse[at, :] = jnp.broadcast_to(scale, (8, HALF))
            for half in range(2):
                normed[at, lanes(half)] = u[half] * scale
                base[at, lanes(half)] = pad[half, REACH + row, start + REACH : start + REACH + 8, :]
    scale_cells(count, small, normed, z)


def scale_cells(count, small, normed, z):
    def scaled(at, carry):
        z[at, :] = (normed[at, :] * small[TAPS + 1 : TAPS + 2, :] + small[TAPS + 2 : TAPS + 3, :]).astype(bf16)
        return carry

    chunks(count, scaled, 0)


def forward_mlp(width, small, mask, w_up, w_down, z, base, hidden, active, slope, branch, out):
    count = ROWS_DEV * width
    for quarter in range(QUARTERS):
        cols = slice(quarter * WIDE, (quarter + 1) * WIDE)
        held = hidden.at[quarter % 2]
        held[...] = dot(z[...], w_up[:, cols])
        bias = small[TAPS + 5 + quarter : TAPS + 6 + quarter, :]

        def gelu(at, carry, held=held, cols=cols, bias=bias):
            h = held[at, :] + bias
            square = h * h
            tangent = jnp.tanh(h * (gelu_scale + (gelu_scale * gelu_cubic) * square))
            above = 0.5 + 0.5 * tangent
            active[at, cols] = (h * above).astype(bf16)
            slope[at, cols] = above + (0.5 * h) * (1.0 - tangent * tangent) * (
                gelu_scale + (3.0 * gelu_scale * gelu_cubic) * square
            )
            return carry

        chunks(count, gelu, 0)
    branch[...] = dot(active[...], w_down[...]) + small[TAPS + 3 : TAPS + 4, :]
    if out is None:
        return

    def residual(at, carry):
        out[at, :] = twice(mask[at, :]) * (base[at, :] + small[TAPS + 4 : TAPS + 5, :] * branch[at, :])
        return carry

    chunks(count, residual, 0)


def backward_cells(
    width, odd, small, own, own_row, upstream, w_up, w_down, normed, inverse, z, active, slope, branch, hidden, dm, dh, du, keep, send, sums
):
    count = ROWS_DEV * width
    zero = jnp.zeros((8, WIDE), f32)

    def first(at, carry):
        sum_dm, sum_em = carry
        e = upstream[at, :]
        inside = twice(own[at, :])
        grad = (e * small[TAPS + 4 : TAPS + 5, :]).astype(bf16)
        dm[at, :] = grad
        sum_dm = sum_dm + fold(grad.astype(f32) * inside)
        sum_em = sum_em + fold(e * branch[at, :] * inside)
        return sum_dm, sum_em

    sum_dm, sum_em = chunks(count, first, (zero, zero))
    for quarter in range(QUARTERS):
        cols = slice(quarter * WIDE, (quarter + 1) * WIDE)
        held = hidden.at[quarter % 2]
        held[...] = dot(dm[...], w_down[cols, :], nt)

        def through(at, carry, held=held, cols=cols):
            dh[at, cols] = (held[at, :] * slope[at, cols]).astype(bf16)
            return carry

        chunks(count, through, 0)
    hidden[0] = dot(dh[...], w_up[...], nt)
    sum_dh = dot(own_row[...], dh[...])

    def norm(at, carry):
        sum_dzn, sum_dz, sum_du = carry
        dz = hidden[0, at, :]
        normal = normed[at, :]
        inside = twice(own[at, :])
        inner = dz * inside
        sum_dz = sum_dz + fold(inner)
        sum_dzn = sum_dzn + fold(inner * normal)
        dn = dz * small[TAPS + 1 : TAPS + 2, :]
        mean = jnp.sum(dn, axis=-1, keepdims=True) * (1.0 / WIDE)
        slant = jnp.sum(dn * normal, axis=-1, keepdims=True) * (1.0 / WIDE)
        grad = (twice(inverse[at, :]) * (dn - mean - normal * slant)).astype(bf16).astype(f32)
        du[at, :] = grad
        sum_du = sum_du + fold(grad * inside)
        dm[at, :] = (dm[at, :].astype(f32) * inside).astype(bf16)
        z[at, :] = (z[at, :].astype(f32) * inside).astype(bf16)
        return sum_dzn, sum_dz, sum_du

    sum_dzn, sum_dz, sum_du = chunks(count, norm, (zero, zero, zero))
    rows = [jnp.sum(value, axis=0, keepdims=True) for value in (sum_du, sum_dzn, sum_dz, sum_dm, sum_em)]
    rows += [sum_dh[0:1, quarter * WIDE : (quarter + 1) * WIDE] for quarter in range(QUARTERS)]
    for index, value in enumerate(rows):
        sums[index : index + 1, :] = value
    sums[len(rows) : 16, :] = jnp.zeros((16 - len(rows), WIDE), f32)

    def weights(up_ref, down_ref):
        for quarter in range(QUARTERS):
            cols = slice(quarter * WIDE, (quarter + 1) * WIDE)
            up_ref[cols, :] = dot(z[...], dh[:, cols], tn).astype(bf16)
            down_ref[cols, :] = dot(active[:, cols], dm[...], tn).astype(bf16)

    @pl.when(odd == 0)
    def _():
        weights(keep, send)

    @pl.when(odd == 1)
    def _():
        weights(send, keep)


def weight_copies(block, flags, parts, w_up, w_down, sems, act):
    odd, section = flags[0], flags[1]
    own_up, own_down, got_up, got_down, other_up, other_down = parts

    @pl.when(section == block)
    def _():
        act(pltpu.make_async_copy(own_up, w_up, sems.at[0]))
        act(pltpu.make_async_copy(own_down, w_down, sems.at[1]))

    @pl.when(section != block)
    def _():
        for index, (ref, mine, other) in enumerate(((w_up, got_up, other_up), (w_down, got_down, other_down))):
            half = mine.shape[0]
            for place, part in enumerate((mine, other)):
                first = odd if place == 0 else 1 - odd
                rows = pl.ds(pl.multiple_of(first * half, half), half)
                act(pltpu.make_async_copy(part, ref.at[rows, :], sems.at[2 + 2 * index + place]))


def start_copy(copy):
    copy.start()


def wait_copy(copy):
    copy.wait()


def write_rows(source, width, out):
    for row in range(ROWS_DEV):
        out[row] = source[row * width : (row + 1) * width, :].astype(bf16)


def kept_copies(kept, sems, places, out):
    copies = []
    for index, (ref, first) in enumerate(places):
        rows = kept.at[first : first + ref.shape[0], 0 : ref.shape[1]]
        copies.append(pltpu.make_async_copy(ref, rows, sems.at[index]) if out else pltpu.make_async_copy(rows, ref, sems.at[index]))
    return copies


def first_conv(
    flags, x, x_a, x_b, small, mask, cot, left, right, kept, pad, taps, wide, normed, inverse, z, base, e_1, sems
):
    places = [(wide, AT_E_0), (e_1, AT_E_1), (normed, AT_NORMED), (base, AT_BASE), (inverse, AT_INVERSE)]
    copies = kept_copies(kept, sems, places, True)
    before = SIDE_0 - SIDE_1
    wide[...] = jnp.zeros((N_0, WIDE), f32)
    for row in range(ROWS_DEV):
        at = row * W_0 + before
        wide[at : at + SIDE_1, :] = left[row].astype(f32)[SIDE_X : SIDE_X + SIDE_1]
        wide[at + SIDE_1 : at + SIDE_1 + COLS_DEV, :] = cot[row].astype(f32)
        wide[at + SIDE_1 + COLS_DEV : at + W_1, :] = right[row].astype(f32)[SIDE_X : SIDE_X + SIDE_1]
    wide[...] = wide[...] * twice(mask[...])
    for row in range(ROWS_DEV):
        at = row * W_0 + before
        e_1[row * W_1 : (row + 1) * W_1, :] = wide[at : at + W_1, :]
    for copy in copies[:2]:
        copy.start()
    load_padded(pad, flags[0], x, x_a, x_b)
    forward_conv(W_0, pad, taps, small, normed, inverse, z, base)
    for copy in copies[2:]:
        copy.start()
    for copy in copies:
        copy.wait()


def first_forward(flags, small, mask, kept, *refs):
    parts, refs = refs[:6], refs[6:]
    y, send_a, send_b, normed, z, base, hidden, out, active, slope, branch, w_up, w_down, weight_sems, sems = refs
    copies = kept_copies(kept, sems, [(normed, AT_NORMED), (base, AT_BASE)], False)
    for copy in copies:
        copy.start()
    weight_copies(0, flags, parts, w_up, w_down, weight_sems, start_copy)
    for copy in copies:
        copy.wait()
    scale_cells(N_0, small, normed, z)
    weight_copies(0, flags, parts, w_up, w_down, weight_sems, wait_copy)
    forward_mlp(W_0, small, mask, w_up, w_down, z, base, hidden, active, slope, branch, out)
    write_rows(out, W_0, y)
    send_rows(flags[0], y, send_a, send_b)


def first_again(flags, small, kept, *refs):
    parts, refs = refs[:6], refs[6:]
    active, slope, branch, w_up, w_down, normed, z, hidden, weight_sems, sems = refs
    (copy,) = kept_copies(kept, sems, [(normed, AT_NORMED)], False)
    copy.start()
    weight_copies(0, flags, parts, w_up, w_down, weight_sems, start_copy)
    copy.wait()
    scale_cells(N_0, small, normed, z)
    weight_copies(0, flags, parts, w_up, w_down, weight_sems, wait_copy)
    forward_mlp(W_0, small, None, w_up, w_down, z, None, hidden, active, slope, branch, None)


def second_block(flags, y, y_a, y_b, small, mask, own, own_row, kept, *refs):
    parts, refs = refs[:6], refs[6:]
    final, du_out, send_a, send_b, keep, send, sums, pad = refs[:8]
    taps, hidden, out, normed, inverse, z, base, active, slope, branch, w_up, w_down, upstream, dm, dh, du, weight_sems, sems = refs[8:]
    (copy,) = kept_copies(kept, sems, [(upstream, AT_E_1)], False)
    copy.start()
    weight_copies(1, flags, parts, w_up, w_down, weight_sems, start_copy)
    load_padded(pad, flags[0], y, y_a, y_b)
    forward_conv(W_1, pad, taps, small, normed, inverse, z, base)
    weight_copies(1, flags, parts, w_up, w_down, weight_sems, wait_copy)
    copy.wait()
    forward_mlp(W_1, small, mask, w_up, w_down, z, base, hidden, active, slope, branch, out)
    for row in range(ROWS_DEV):
        at = row * W_1 + SIDE_1
        final[row] = out[at : at + COLS_DEV, :].astype(bf16)
    backward_cells(
        W_1, flags[0], small, own, own_row, upstream, w_up, w_down, normed, inverse, z, active, slope, branch, hidden, dm, dh, du, keep, send, sums
    )
    write_rows(du, W_1, du_out)
    send_rows(flags[0], du_out, send_a, send_b)


def first_backward(
    flags, du1, du1_a, du1_b, small1, small0, mask, own, own_row, active, slope, branch, w_up, w_down, kept,
    e_own, du_out, send_a, send_b, keep, send, sums,
    pad, taps, hidden, upstream, z, dm, dh, du, normed, inverse, sems,
):
    copies = kept_copies(kept, sems, [(upstream, AT_E_0), (normed, AT_NORMED), (inverse, AT_INVERSE)], False)
    for copy in copies:
        copy.start()
    shift = SIDE_0 + REACH - SIDE_1
    pad[:, :, 0:8, :] = jnp.zeros((2, ROWS_DEV + 2 * REACH, 8, HALF), f32)
    pad[:, :, W_X - 16 : W_X, :] = jnp.zeros((2, ROWS_DEV + 2 * REACH, 16, HALF), f32)
    load_padded(pad, flags[0], du1, du1_a, du1_b, shift)
    load_taps(taps, small1)
    copies[0].wait()
    for group in groups(W_0, 4):
        starts = [tile * 8 for tile in group]
        for half in range(2):
            spread = conv_tiles(pad, taps, half, starts, True)
            for index, start in enumerate(starts):
                for row in range(ROWS_DEV):
                    at = slice(row * W_0 + start, row * W_0 + start + 8)
                    value = (upstream[at, lanes(half)] + spread[index][row]).astype(bf16).astype(f32)
                    upstream[at, lanes(half)] = mask[at, :] * value
    for row in range(ROWS_DEV):
        at = row * W_0 + SIDE_0
        e_own[row] = upstream[at : at + W_OWN, :]
    for copy in copies[1:]:
        copy.wait()
    scale_cells(N_0, small0, normed, z)
    backward_cells(
        W_0, flags[0], small0, own, own_row, upstream, w_up, w_down, normed, inverse, z, active, slope, branch, hidden, dm, dh, du, keep, send, sums
    )
    write_rows(du, W_0, du_out)
    send_rows(flags[0], du_out, send_a, send_b)


def input_grad(flags, du, du_a, du_b, small, e_own, out, pad, taps, total):
    load_padded(pad, flags[0], du, du_a, du_b)
    load_taps(taps, small)
    for group in groups(W_OWN, 5):
        starts = [tile * 8 for tile in group]
        for half in range(2):
            spread = conv_tiles(pad, taps, half, [start + SIDE_0 - REACH for start in starts], True)
            for index, start in enumerate(starts):
                for row in range(ROWS_DEV):
                    at = slice(start, start + 8)
                    total[row, at, lanes(half)] = e_own[row, at, lanes(half)] + spread[index][row]
    for row in range(ROWS_DEV):
        out[row] = total[row, 0:COLS_DEV, :].astype(bf16)


def tap_grads_1(flags, pad, du, own, sums, out, grads, total):
    tap_sums(W_1, pad, du, own, sums, out, grads, total)


def tap_grads_0(flags, v, v_a, v_b, du, own, sums, out, pad, grads, total):
    load_padded(pad, flags[0], v, v_a, v_b)
    tap_sums(W_0, pad, du, own, sums, out, grads, total)


def tap_sums(width, pad, du, own, sums, out, grads, total):
    for row in range(ROWS_DEV):
        inside = own[row * width : (row + 1) * width, :]
        grads[row] = du[row].astype(f32) * twice(inside)
    total[...] = jnp.zeros((SMALL, WIDE), f32)
    for half in range(2):
        for offsets in (range(0, 4), range(4, KERNEL)):
            partial = [[None] * KERNEL for _ in offsets]
            for tile in range(width // 8):
                start = tile * 8
                grad = [grads[row, start : start + 8, lanes(half)] for row in range(ROWS_DEV)]
                for row in range(ROWS_DEV + KERNEL - 1):
                    for index, col_off in enumerate(offsets):
                        window = pad[half, row, start + col_off : start + col_off + 8, :]
                        for out_row in range(ROWS_DEV):
                            row_off = row - out_row
                            if 0 <= row_off < KERNEL:
                                term = window * grad[out_row]
                                held = partial[index][row_off]
                                partial[index][row_off] = term if held is None else held + term
            for index, col_off in enumerate(offsets):
                for row_off in range(KERNEL):
                    tap = row_off * KERNEL + col_off
                    total[tap : tap + 1, lanes(half)] = jnp.sum(partial[index][row_off], axis=0, keepdims=True)
    total[TAPS : TAPS + 9, :] = sums[0:9, :]
    out[...] = total[...].astype(bf16)


factor = 1.0 / math.sqrt(BATCH * ROWS_DEV * COLS_DEV)


def write_weights(is_up, rows, up, down, up_vmem, down_vmem, sems, beside=None):
    def send(copies, fill):
        for quarter in range(QUARTERS):
            fill(quarter, rows[quarter * WIDE : (quarter + 1) * WIDE, :].astype(f32) * factor)
            copies[quarter].start()
        if beside:
            beside()
        for copy in copies:
            copy.wait()

    def cols(quarter):
        return slice(quarter * WIDE, (quarter + 1) * WIDE)

    @pl.when(is_up)
    def _():
        def fill(quarter, value):
            up_vmem[:, cols(quarter)] = value

        send([pltpu.make_async_copy(up_vmem.at[:, cols(q)], up.at[0, :, cols(q)], sems.at[0, q]) for q in range(QUARTERS)], fill)

    @pl.when(jnp.logical_not(is_up))
    def _():
        def fill(quarter, value):
            down_vmem[cols(quarter), :] = value

        send([pltpu.make_async_copy(down_vmem.at[cols(q), :], down.at[0, cols(q), :], sems.at[1, q]) for q in range(QUARTERS)], fill)


def finish_own(flags, piece, up, down, up_vmem, down_vmem, sems):
    write_weights(flags[0] == 0, piece, up, down, up_vmem, down_vmem, sems)


def finish_got(flags, small, got, up_in, down_in, up, down, taps, channels, bias, up_vmem, down_vmem, sems):
    def rest():
        sums = (small[...].astype(f32) + got[HID:, :].astype(f32)) * factor
        for tap in range(TAPS):
            taps[tap] = sums[tap : tap + 1]
        for index in range(5):
            channels[index] = sums[TAPS + index : TAPS + index + 1]
        for quarter in range(QUARTERS):
            bias[:, quarter * WIDE : (quarter + 1) * WIDE] = sums[TAPS + 5 + quarter : TAPS + 6 + quarter]

    write_weights(flags[0] == 1, got, up, down, up_vmem, down_vmem, sems, rest)


def in_vmem():
    return pl.BlockSpec(memory_space=pltpu.VMEM)


def call(body, name, inputs, outputs, scratch, flops, hbm_in=0, hbm_out=0, sems=(), aliases=None):
    in_hbm = pl.BlockSpec(memory_space=pltpu.HBM)
    return pl.pallas_call(
        body,
        name=name,
        out_shape=[jax.ShapeDtypeStruct(shape, dtype) for shape, dtype in outputs],
        in_specs=[pl.BlockSpec(memory_space=pltpu.SMEM)] + [in_vmem()] * (len(inputs) - 1 - hbm_in) + [in_hbm] * hbm_in,
        out_specs=[in_hbm] * hbm_out + [in_vmem()] * (len(outputs) - hbm_out),
        input_output_aliases=aliases or {},
        scratch_shapes=[pltpu.VMEM(shape, dtype) for shape, dtype in scratch] + [pltpu.SemaphoreType.DMA(shape) for shape in sems],
        compiler_params=pltpu.CompilerParams(vmem_limit_bytes=28 << 20),
        cost_estimate=pl.CostEstimate(flops=10 * flops, bytes_accessed=4 << 20, transcendentals=0),
    )(*inputs)


def swap_pairs(count, bit):
    return [(i, i ^ bit) for i in range(count)]


def on_device(
    window_input,
    output_cotangent,
    ocean_mask,
    dw_kernel,
    channel_params,
    up_weight,
    up_bias,
    down_weight,
):
    section = lax.axis_index("section")
    lat = lax.axis_index("lat")
    lon = lax.axis_index("lon")
    n_lat, n_lon = lax.axis_size("lat"), lax.axis_size("lon")
    odd = lat % 2
    flags = jnp.stack([odd, section]).astype(jnp.int32)
    channels = window_input.shape[-1]

    def over_section(value):
        return lax.ppermute(value, "section", [(0, 1), (1, 0)])

    def over_core(value):
        return lax.ppermute(value, "lat", swap_pairs(n_lat, 1))

    def lat_halo(send_a, send_b):
        pairs = [(i, i + 1) for i in range(1, n_lat - 1, 2)]
        pairs += [(j, i) for i, j in pairs]
        got_b = lax.ppermute(send_b, "lat", pairs)
        beside = jnp.where(odd == 1, lat < n_lat - 1, lat > 0)
        return over_core(send_a), jnp.where(beside, got_b, jnp.zeros_like(got_b))

    def by_core(even, other):
        return jnp.where(odd == 0, even, other)

    x = lax.dynamic_index_in_dim(window_input, section, 0, False)
    cot = lax.dynamic_index_in_dim(output_cotangent, section, 0, False)
    sea = ocean_mask.astype(bf16)

    def packed(x_part, cot_part, sea_part):
        sea_row = jnp.pad(sea_part, ((0, 0), (0, channels - sea_part.shape[1])))[:, None, :]
        return jnp.concatenate([x_part, cot_part, sea_row], axis=1)

    ring = [(i, (i + 1) % n_lon) for i in range(n_lon)]
    to_right = packed(x[:, -SIDE_X:], cot[:, -SIDE_1:], sea[:, -SIDE_0:])
    to_left = packed(x[:, :SIDE_X], cot[:, :SIDE_1], sea[:, :SIDE_0])
    to_right, to_left, dw_kernel = lax.optimization_barrier((to_right, to_left, dw_kernel))
    left = lax.ppermute(to_right, "lon", ring)
    right = lax.ppermute(to_left, "lon", [(j, i) for i, j in ring])
    small_own = jnp.concatenate(
        [dw_kernel[0], channel_params[0], up_bias[0].reshape(QUARTERS, WIDE), jnp.zeros((SMALL - TAPS - 9, WIDE), bf16)], axis=0
    )
    up, down = up_weight[0], down_weight[0]
    cut = channels // 2
    small_got = over_section(small_own)
    send_up = by_core(up[:cut], up[cut:])
    send_down = by_core(down[: HID // 2], down[HID // 2 :])
    send_up, send_down, small_got = lax.optimization_barrier((send_up, send_down, small_got))
    got_up, got_down = over_section(send_up), over_section(send_down)
    small_0 = jnp.where(section == 0, small_own, small_got).astype(f32)
    small_1 = jnp.where(section == 0, small_got, small_own).astype(f32)

    before = SIDE_0 - SIDE_1
    sea_at = SIDE_X + SIDE_1
    x_wide = jnp.concatenate([left[:, :SIDE_X], x, right[:, :SIDE_X], jnp.zeros((ROWS_DEV, W_X - COLS_DEV - 2 * SIDE_X, channels), bf16)], axis=1)
    x_a, x_b = lat_halo(by_core(x_wide[1:], x_wide[:REACH]), by_core(x_wide[:REACH], x_wide[1:]))
    mask_wide = jnp.concatenate(
        [left[:, sea_at, :SIDE_0], sea, right[:, sea_at, :SIDE_0], jnp.zeros((ROWS_DEV, W_0 - COLS_DEV - 2 * SIDE_0), bf16)], axis=1
    )
    before = SIDE_0 - SIDE_1
    def spread_lanes(mask):
        flat = mask.astype(f32).reshape(-1, 1)
        return jnp.broadcast_to(flat, (flat.shape[0], HALF))

    mask_0, mask_1 = spread_lanes(mask_wide), spread_lanes(mask_wide[:, before : before + W_1])

    def own_cells(width, side):
        column = jnp.arange(width)
        inside = ((column >= side) & (column < side + COLS_DEV)).astype(f32)
        flat = jnp.tile(inside, ROWS_DEV)
        return jnp.broadcast_to(flat[:, None], (flat.shape[0], HALF)), jnp.broadcast_to(flat[None, :], (16, flat.shape[0])).astype(bf16)

    own_0, row_0 = own_cells(W_0, SIDE_0)
    own_1, row_1 = own_cells(W_1, SIDE_1)

    deep = ROWS_DEV + 2 * REACH
    taps_scratch = ((2, TAPS, 8, HALF), f32)

    (kept,) = call(
        first_conv,
        "first_conv",
        (flags, x_wide, x_a, x_b, small_0, mask_0, cot, left, right),
        [((KEPT_ROWS, WIDE), f32)],
        [
            ((2, deep, W_X, HALF), f32), taps_scratch, ((N_0, WIDE), f32), ((N_0, WIDE), f32), ((N_0, HALF), f32),
            ((N_0, WIDE), bf16), ((N_0, WIDE), f32), ((N_1, WIDE), f32),
        ],
        2_000_000_000,
        hbm_out=1,
        sems=((5,),),
    )
    got_up, got_down, kept = lax.optimization_barrier((got_up, got_down, kept))
    other_up, other_down = over_core(got_up), over_core(got_down)
    weights = (up, down, got_up, got_down, other_up, other_down)
    y, y_send_a, y_send_b = call(
        first_forward,
        "first_forward",
        (flags, small_0, mask_0, kept) + weights,
        [((ROWS_DEV, W_0, WIDE), bf16), ((REACH, W_0, WIDE), bf16), ((REACH, W_0, WIDE), bf16)],
        [
            ((N_0, WIDE), f32), ((N_0, WIDE), bf16), ((N_0, WIDE), f32), ((2, N_0, WIDE), f32), ((N_0, WIDE), f32),
            ((N_0, HID), bf16), ((N_0, HID), f32), ((N_0, WIDE), f32), ((WIDE, HID), bf16), ((HID, WIDE), bf16),
        ],
        2_000_000_000,
        hbm_in=7,
        sems=((6,), (2,)),
    )
    y_a, y_b = lat_halo(y_send_a, y_send_b)
    final, du1, du1_send_a, du1_send_b, keep_1, send_1, sums_1, pad_1 = call(
        second_block,
        "second_block",
        (flags, y, y_a, y_b, small_1, mask_1, own_1, row_1, kept) + weights,
        [
            ((ROWS_DEV, COLS_DEV, WIDE), bf16), ((ROWS_DEV, W_1, WIDE), bf16), ((REACH, W_1, WIDE), bf16), ((REACH, W_1, WIDE), bf16),
            ((HID, WIDE), bf16), ((HID, WIDE), bf16), ((16, WIDE), f32), ((2, deep, W_0, HALF), f32),
        ],
        [
            taps_scratch, ((2, N_1, WIDE), f32), ((N_1, WIDE), f32),
            ((N_1, WIDE), f32), ((N_1, HALF), f32), ((N_1, WIDE), bf16), ((N_1, WIDE), f32), ((N_1, HID), bf16), ((N_1, HID), f32), ((N_1, WIDE), f32),
            ((WIDE, HID), bf16), ((HID, WIDE), bf16), ((N_1, WIDE), f32), ((N_1, WIDE), bf16), ((N_1, HID), bf16), ((N_1, WIDE), f32),
        ],
        4_000_000_000,
        hbm_in=7,
        sems=((6,), (1,)),
    )
    du1_a, du1_b = lat_halo(du1_send_a, du1_send_b)
    small_again, _ = lax.optimization_barrier((small_0, du1_send_a))
    active, slope, branch, w_up, w_down = call(
        first_again,
        "first_again",
        (flags, small_again, kept) + weights,
        [((N_0, HID), bf16), ((N_0, HID), f32), ((N_0, WIDE), f32), ((WIDE, HID), bf16), ((HID, WIDE), bf16)],
        [((N_0, WIDE), f32), ((N_0, WIDE), bf16), ((2, N_0, WIDE), f32)],
        2_000_000_000,
        hbm_in=7,
        sems=((6,), (1,)),
    )
    send_1, du1_a, du1_b, active = lax.optimization_barrier((send_1, du1_a, du1_b, active))
    e_own, du0, du0_send_a, du0_send_b, keep_0, send_0, sums_0 = call(
        first_backward,
        "first_backward",
        (flags, du1, du1_a, du1_b, small_1, small_0, mask_0, own_0, row_0, active, slope, branch, w_up, w_down, kept),
        [
            ((ROWS_DEV, W_OWN, WIDE), f32), ((ROWS_DEV, W_0, WIDE), bf16), ((REACH, W_0, WIDE), bf16), ((REACH, W_0, WIDE), bf16),
            ((HID, WIDE), bf16), ((HID, WIDE), bf16), ((16, WIDE), f32),
        ],
        [
            ((2, deep, W_X, HALF), f32), taps_scratch, ((2, N_0, WIDE), f32), ((N_0, WIDE), f32), ((N_0, WIDE), bf16),
            ((N_0, WIDE), bf16), ((N_0, HID), bf16), ((N_0, WIDE), f32),
            ((N_0, WIDE), f32), ((N_0, HALF), f32),
        ],
        3_000_000_000,
        hbm_in=1,
        sems=((3,),),
    )
    bits = [("lat", 1 << i) for i in range(1, n_lat.bit_length() - 1)] + [("lon", 1 << i) for i in range(n_lon.bit_length() - 1)]
    orders = (bits, bits[1:2] + bits[:1] + bits[2:])

    def partner(place, step):
        row, col = place
        axis, bit = orders[row % 2][step]
        return (row ^ bit, col) if axis == "lat" else (row, col ^ bit)

    def exchange(value, step):
        pairs = []
        for row in range(n_lat):
            for col in range(n_lon):
                other = partner((row, col), step)
                pairs.append((row * n_lon + col, other[0] * n_lon + other[1]))
        return lax.ppermute(value, ("lat", "lon"), pairs)

    def side(step):
        def of(order):
            axis, bit = order[step]
            return ((lat if axis == "lat" else lon) // bit) % 2

        return jnp.where(odd == 0, of(orders[0]), of(orders[1]))

    def plus(first, second):
        return (first.astype(f32) + second.astype(f32)).astype(bf16)

    def reduce_scatter(keep, send):
        piece = plus(keep, over_core(send))
        for step in range(len(bits)):
            half = piece.shape[0] // 2
            low, high = piece[:half], piece[half:]
            which = side(step) == 0
            piece = plus(jnp.where(which, low, high), exchange(jnp.where(which, high, low), step))
        return piece

    def reduce_step(pieces, step):
        half = pieces.shape[1] // 2
        low, high = pieces[:, :half], pieces[:, half:]
        which = side(step) == 0
        return plus(jnp.where(which, low, high), exchange(jnp.where(which, high, low), step))

    to_first = section == 0

    def chosen(first, second):
        return jnp.where(to_first, first, second)

    core_1 = over_core(send_1)
    core_0 = over_core(send_0)
    (taps_0,) = call(
        tap_grads_0, "tap_grads_0", (flags, x_wide, x_a, x_b, du0, own_0, sums_0), [((SMALL, WIDE), bf16)],
        [((2, deep, W_X, HALF), f32), ((ROWS_DEV, W_0, WIDE), f32), ((SMALL, WIDE), f32)], 2_000_000_000,
    )
    core_0, taps_0, pad_1 = lax.optimization_barrier((core_0, taps_0, pad_1))
    pieces = jnp.stack([plus(keep_0, core_0), plus(keep_1, core_1)])
    (taps_1,) = call(
        tap_grads_1, "tap_grads_1", (flags, pad_1, du1, own_1, sums_1), [((SMALL, WIDE), bf16)],
        [((ROWS_DEV, W_1, WIDE), f32), ((SMALL, WIDE), f32)], 2_000_000_000,
    )
    pieces = reduce_step(pieces, 0)
    pieces, taps_1, du0_send_a, du0_send_b = lax.optimization_barrier((pieces, taps_1, du0_send_a, du0_send_b))
    du0_a, du0_b = lat_halo(du0_send_a, du0_send_b)
    pieces = reduce_step(pieces, 1)
    pieces, du0_a, du0_b = lax.optimization_barrier((pieces, du0_a, du0_b))
    (start,) = call(
        input_grad, "input_grad", (flags, du0, du0_a, du0_b, small_0, e_own), [((ROWS_DEV, COLS_DEV, WIDE), bf16)],
        [((2, deep, W_0, HALF), f32), taps_scratch, ((ROWS_DEV, W_OWN, WIDE), f32)], 2_000_000_000,
    )
    for step in range(2, len(bits)):
        pieces = reduce_step(pieces, step)
    pieces, start = lax.optimization_barrier((pieces, start))
    other_end = over_section(chosen(final, start))
    piece_0, piece_1 = pieces[0], pieces[1]
    cut = piece_0.shape[0]
    boundary = jnp.stack([chosen(start, other_end), chosen(other_end, final)])[None]

    def both(piece, small):
        return jnp.concatenate([piece, small], axis=0)

    got = over_section(both(chosen(piece_1, piece_0), chosen(taps_1, taps_0)))
    piece = plus(chosen(piece_0, piece_1), got[:cut])
    small = plus(chosen(taps_0, taps_1), got[cut:])
    for step in reversed(range(len(bits))):
        if step == 0:
            piece, boundary = lax.optimization_barrier((piece, boundary))
        got = exchange(both(piece, small), step)
        cut = piece.shape[0]
        small = plus(small, got[cut:])
        which = side(step) == 0
        piece = jnp.where(which, jnp.concatenate([piece, got[:cut]]), jnp.concatenate([got[:cut], piece]))
    got = over_core(both(piece, small))
    weight_outs = [((1, WIDE, HID), f32), ((1, HID, WIDE), f32)]
    weight_scratch = [((WIDE, HID), f32), ((HID, WIDE), f32)]
    halves = call(
        finish_own, "finish_own", (flags, piece), weight_outs, weight_scratch, 1_000_000, hbm_out=2, sems=((2, QUARTERS),)
    )
    grad_up, grad_down, grad_taps, grad_channels, grad_bias = call(
        finish_got,
        "finish_got",
        (flags, small, got, *halves),
        weight_outs + [((TAPS, 1, WIDE), f32), ((5, 1, WIDE), f32), ((1, HID), f32)],
        weight_scratch,
        1_000_000,
        hbm_in=2,
        hbm_out=2,
        sems=((2, QUARTERS),),
        aliases={3: 0, 4: 1},
    )
    grad_taps, grad_channels = jnp.swapaxes(grad_taps, 0, 1), jnp.swapaxes(grad_channels, 0, 1)
    return (
        boundary,
        grad_taps,
        grad_channels,
        grad_up,
        grad_bias,
        grad_down,
    )


def solution(mesh):
    in_specs = (
        P(None, "lat", "lon", None),
        P(None, "lat", "lon", None),
        P("lat", "lon"),
        P("section", None, None),
        P("section", None, None),
        P("section", None, None),
        P("section", None),
        P("section", None, None),
    )
    out_specs = (
        P("section", None, "lat", "lon", None),
        P("section", None, None),
        P("section", None, None),
        P("section", None, None),
        P("section", None),
        P("section", None, None),
    )
    return jax.shard_map(
        on_device, mesh=mesh, in_specs=in_specs, out_specs=out_specs, check_vma=False
    )
```

```python
import math

import jax
import jax.numpy as jnp
from jax import lax
from jax.experimental import pallas as pl
from jax.experimental.pallas import tpu as pltpu
from jax.sharding import PartitionSpec as P

KERNEL = 7
TAPS = KERNEL * KERNEL
REACH = KERNEL // 2
ROWS_DEV = 4
COLS_DEV = 68
BATCH = 2
HALF = 128
WIDE = 256
HID = 1024
QUARTERS = HID // WIDE
SIDE_X, SIDE_0, SIDE_1 = 12, 9, 6
W_X, W_0, W_1, W_OWN = 96, 88, 80, 72
CHUNK = 32
SMALL = 64
N_0, N_1 = ROWS_DEV * W_0, ROWS_DEV * W_1
AT_NORMED, AT_BASE, AT_INVERSE, AT_E_0, AT_E_1 = 0, N_0, 2 * N_0, 3 * N_0, 4 * N_0
KEPT_ROWS = 40960

norm_eps = 1e-06
gelu_scale = 0.7978845608028654
gelu_cubic = 0.044715
f32, bf16 = jnp.float32, jnp.bfloat16

nn = (((1,), (0,)), ((), ()))
nt = (((1,), (1,)), ((), ()))
tn = (((0,), (0,)), ((), ()))


def dot(left, right, dims=nn):
    return lax.dot_general(left, right, dims, preferred_element_type=f32)


def lanes(half):
    return slice(half * HALF, (half + 1) * HALF)


def load_padded(pad, odd, center, first, second, offset=0):
    width = center.shape[1]

    def put(row, value):
        value = value.astype(f32)
        for half in range(2):
            pad[half, row, offset : offset + width, :] = value[:, lanes(half)]

    at_first = jnp.where(odd == 1, 0, REACH + ROWS_DEV)
    at_second = jnp.where(odd == 1, REACH + ROWS_DEV, 0)
    for row in range(ROWS_DEV):
        put(REACH + row, center[row])
    for row in range(REACH):
        put(at_first + row, first[row])
        put(at_second + row, second[row])


def load_taps(taps, small):
    for half in range(2):
        taps[half] = jnp.broadcast_to(small[0:TAPS, lanes(half)][:, None, :], (TAPS, 8, HALF))


def groups(width, most):
    tiles = width // 8
    count = -(-tiles // most)
    bounds = [tiles * i // count for i in range(count + 1)]
    return [range(first, last) for first, last in zip(bounds, bounds[1:])]


def conv_tiles(pad, taps, half, starts, reverse):
    sums = [[None] * ROWS_DEV for _ in starts]
    for col_off in range(KERNEL):
        column = [taps[half, TAPS - 1 - tap if reverse else tap] for tap in range(col_off, TAPS, KERNEL)]
        for row in range(ROWS_DEV + KERNEL - 1):
            for index, start in enumerate(starts):
                window = pad[half, row, start + col_off : start + col_off + 8, :]
                for out_row in range(ROWS_DEV):
                    row_off = row - out_row
                    if 0 <= row_off < KERNEL:
                        term = window * column[row_off]
                        held = sums[index][out_row]
                        sums[index][out_row] = term if held is None else held + term
    return sums


def chunks(count, body, carry=0):
    for i in range(count // CHUNK):
        carry = body(slice(i * CHUNK, (i + 1) * CHUNK), carry)
    return carry


def fold(value):
    return jnp.sum(value.reshape(CHUNK // 8, 8, value.shape[-1]), axis=0)


def twice(value):
    return jnp.concatenate([value, value], axis=1)


def send_rows(odd, source, send_first, send_second):
    first, second = jnp.where(odd == 1, 0, 1), jnp.where(odd == 1, 1, 0)
    send_first[...] = source[pl.ds(first, REACH)]
    send_second[...] = source[pl.ds(second, REACH)]


def forward_conv(width, pad, taps, small, normed, inverse, z, base):
    count = ROWS_DEV * width
    load_taps(taps, small)
    for group in groups(width, 4):
        starts = [tile * 8 for tile in group]
        halves = [conv_tiles(pad, taps, half, starts, False) for half in range(2)]
        for index, row in [(index, row) for index in range(len(starts)) for row in range(ROWS_DEV)]:
            start = starts[index]
            u = [halves[half][index][row] + small[TAPS : TAPS + 1, lanes(half)] for half in range(2)]
            mean = jnp.sum(u[0] + u[1], axis=-1, keepdims=True) * (1.0 / WIDE)
            u = [value - mean for value in u]
            spread = jnp.sum(u[0] * u[0] + u[1] * u[1], axis=-1, keepdims=True) * (1.0 / WIDE)
            scale = lax.rsqrt(spread + norm_eps)
            at = slice(row * width + start, row * width + start + 8)
            inverse[at, :] = jnp.broadcast_to(scale, (8, HALF))
            for half in range(2):
                normed[at, lanes(half)] = u[half] * scale
                base[at, lanes(half)] = pad[half, REACH + row, start + REACH : start + REACH + 8, :]
    scale_cells(count, small, normed, z)


def scale_cells(count, small, normed, z):
    def scaled(at, carry):
        z[at, :] = (normed[at, :] * small[TAPS + 1 : TAPS + 2, :] + small[TAPS + 2 : TAPS + 3, :]).astype(bf16)
        return carry

    chunks(count, scaled, 0)


def forward_mlp(width, small, mask, w_up, w_down, z, base, hidden, active, slope, branch, out):
    count = ROWS_DEV * width
    for quarter in range(QUARTERS):
        cols = slice(quarter * WIDE, (quarter + 1) * WIDE)
        held = hidden.at[quarter % 2]
        held[...] = dot(z[...], w_up[:, cols])
        bias = small[TAPS + 5 + quarter : TAPS + 6 + quarter, :]

        def gelu(at, carry, held=held, cols=cols, bias=bias):
            h = held[at, :] + bias
            square = h * h
            tangent = jnp.tanh(h * (gelu_scale + (gelu_scale * gelu_cubic) * square))
            above = 0.5 + 0.5 * tangent
            active[at, cols] = (h * above).astype(bf16)
            slope[at, cols] = above + (0.5 * h) * (1.0 - tangent * tangent) * (
                gelu_scale + (3.0 * gelu_scale * gelu_cubic) * square
            )
            return carry

        chunks(count, gelu, 0)
    branch[...] = dot(active[...], w_down[...]) + small[TAPS + 3 : TAPS + 4, :]
    if out is None:
        return

    def residual(at, carry):
        out[at, :] = twice(mask[at, :]) * (base[at, :] + small[TAPS + 4 : TAPS + 5, :] * branch[at, :])
        return carry

    chunks(count, residual, 0)


def backward_cells(
    width, odd, small, own, own_row, upstream, w_up, w_down, normed, inverse, z, active, slope, branch, hidden, dm, dh, du, keep, send, sums
):
    count = ROWS_DEV * width
    zero = jnp.zeros((8, WIDE), f32)

    def first(at, carry):
        sum_dm, sum_em = carry
        e = upstream[at, :]
        inside = twice(own[at, :])
        grad = (e * small[TAPS + 4 : TAPS + 5, :]).astype(bf16)
        dm[at, :] = grad
        sum_dm = sum_dm + fold(grad.astype(f32) * inside)
        sum_em = sum_em + fold(e * branch[at, :] * inside)
        return sum_dm, sum_em

    sum_dm, sum_em = chunks(count, first, (zero, zero))
    for quarter in range(QUARTERS):
        cols = slice(quarter * WIDE, (quarter + 1) * WIDE)
        held = hidden.at[quarter % 2]
        held[...] = dot(dm[...], w_down[cols, :], nt)

        def through(at, carry, held=held, cols=cols):
            dh[at, cols] = (held[at, :] * slope[at, cols]).astype(bf16)
            return carry

        chunks(count, through, 0)
    hidden[0] = dot(dh[...], w_up[...], nt)
    sum_dh = dot(own_row[...], dh[...])

    def norm(at, carry):
        sum_dzn, sum_dz, sum_du = carry
        dz = hidden[0, at, :]
        normal = normed[at, :]
        inside = twice(own[at, :])
        inner = dz * inside
        sum_dz = sum_dz + fold(inner)
        sum_dzn = sum_dzn + fold(inner * normal)
        dn = dz * small[TAPS + 1 : TAPS + 2, :]
        mean = jnp.sum(dn, axis=-1, keepdims=True) * (1.0 / WIDE)
        slant = jnp.sum(dn * normal, axis=-1, keepdims=True) * (1.0 / WIDE)
        grad = (twice(inverse[at, :]) * (dn - mean - normal * slant)).astype(bf16).astype(f32)
        du[at, :] = grad
        sum_du = sum_du + fold(grad * inside)
        dm[at, :] = (dm[at, :].astype(f32) * inside).astype(bf16)
        z[at, :] = (z[at, :].astype(f32) * inside).astype(bf16)
        return sum_dzn, sum_dz, sum_du

    sum_dzn, sum_dz, sum_du = chunks(count, norm, (zero, zero, zero))
    rows = [jnp.sum(value, axis=0, keepdims=True) for value in (sum_du, sum_dzn, sum_dz, sum_dm, sum_em)]
    rows += [sum_dh[0:1, quarter * WIDE : (quarter + 1) * WIDE] for quarter in range(QUARTERS)]
    for index, value in enumerate(rows):
        sums[index : index + 1, :] = value
    sums[len(rows) : 16, :] = jnp.zeros((16 - len(rows), WIDE), f32)

    def weights(up_ref, down_ref):
        for quarter in range(QUARTERS):
            cols = slice(quarter * WIDE, (quarter + 1) * WIDE)
            up_ref[cols, :] = dot(z[...], dh[:, cols], tn).astype(bf16)
            down_ref[cols, :] = dot(active[:, cols], dm[...], tn).astype(bf16)

    @pl.when(odd == 0)
    def _():
        weights(keep, send)

    @pl.when(odd == 1)
    def _():
        weights(send, keep)


def weight_copies(block, flags, parts, w_up, w_down, sems, act):
    odd, section = flags[0], flags[1]
    own_up, own_down, got_up, got_down, other_up, other_down = parts

    @pl.when(section == block)
    def _():
        act(pltpu.make_async_copy(own_up, w_up, sems.at[0]))
        act(pltpu.make_async_copy(own_down, w_down, sems.at[1]))

    @pl.when(section != block)
    def _():
        for index, (ref, mine, other) in enumerate(((w_up, got_up, other_up), (w_down, got_down, other_down))):
            half = mine.shape[0]
            for place, part in enumerate((mine, other)):
                first = odd if place == 0 else 1 - odd
                rows = pl.ds(pl.multiple_of(first * half, half), half)
                act(pltpu.make_async_copy(part, ref.at[rows, :], sems.at[2 + 2 * index + place]))


def start_copy(copy):
    copy.start()


def wait_copy(copy):
    copy.wait()


def write_rows(source, width, out):
    for row in range(ROWS_DEV):
        out[row] = source[row * width : (row + 1) * width, :].astype(bf16)


def kept_copies(kept, sems, places, out):
    copies = []
    for index, (ref, first) in enumerate(places):
        rows = kept.at[first : first + ref.shape[0], 0 : ref.shape[1]]
        copies.append(pltpu.make_async_copy(ref, rows, sems.at[index]) if out else pltpu.make_async_copy(rows, ref, sems.at[index]))
    return copies


def first_conv(
    flags, x, x_a, x_b, small, mask, cot, left, right, kept, pad, taps, wide, normed, inverse, z, base, e_1, sems
):
    places = [(wide, AT_E_0), (e_1, AT_E_1), (normed, AT_NORMED), (base, AT_BASE), (inverse, AT_INVERSE)]
    copies = kept_copies(kept, sems, places, True)
    before = SIDE_0 - SIDE_1
    wide[...] = jnp.zeros((N_0, WIDE), f32)
    for row in range(ROWS_DEV):
        at = row * W_0 + before
        wide[at : at + SIDE_1, :] = left[row].astype(f32)[SIDE_X : SIDE_X + SIDE_1]
        wide[at + SIDE_1 : at + SIDE_1 + COLS_DEV, :] = cot[row].astype(f32)
        wide[at + SIDE_1 + COLS_DEV : at + W_1, :] = right[row].astype(f32)[SIDE_X : SIDE_X + SIDE_1]
    wide[...] = wide[...] * twice(mask[...])
    for row in range(ROWS_DEV):
        at = row * W_0 + before
        e_1[row * W_1 : (row + 1) * W_1, :] = wide[at : at + W_1, :]
    for copy in copies[:2]:
        copy.start()
    load_padded(pad, flags[0], x, x_a, x_b)
    forward_conv(W_0, pad, taps, small, normed, inverse, z, base)
    for copy in copies[2:]:
        copy.start()
    for copy in copies:
        copy.wait()


def first_forward(flags, small, mask, kept, *refs):
    parts, refs = refs[:6], refs[6:]
    y, send_a, send_b, normed, z, base, hidden, out, active, slope, branch, w_up, w_down, weight_sems, sems = refs
    copies = kept_copies(kept, sems, [(normed, AT_NORMED), (base, AT_BASE)], False)
    for copy in copies:
        copy.start()
    weight_copies(0, flags, parts, w_up, w_down, weight_sems, start_copy)
    for copy in copies:
        copy.wait()
    scale_cells(N_0, small, normed, z)
    weight_copies(0, flags, parts, w_up, w_down, weight_sems, wait_copy)
    forward_mlp(W_0, small, mask, w_up, w_down, z, base, hidden, active, slope, branch, out)
    write_rows(out, W_0, y)
    send_rows(flags[0], y, send_a, send_b)


def first_again(flags, small, kept, *refs):
    parts, refs = refs[:6], refs[6:]
    active, slope, branch, w_up, w_down, normed, z, hidden, weight_sems, sems = refs
    (copy,) = kept_copies(kept, sems, [(normed, AT_NORMED)], False)
    copy.start()
    weight_copies(0, flags, parts, w_up, w_down, weight_sems, start_copy)
    copy.wait()
    scale_cells(N_0, small, normed, z)
    weight_copies(0, flags, parts, w_up, w_down, weight_sems, wait_copy)
    forward_mlp(W_0, small, None, w_up, w_down, z, None, hidden, active, slope, branch, None)


def second_block(flags, y, y_a, y_b, small, mask, own, own_row, kept, *refs):
    parts, refs = refs[:6], refs[6:]
    final, du_out, send_a, send_b, keep, send, sums, pad = refs[:8]
    taps, hidden, out, normed, inverse, z, base, active, slope, branch, w_up, w_down, upstream, dm, dh, du, weight_sems, sems = refs[8:]
    (copy,) = kept_copies(kept, sems, [(upstream, AT_E_1)], False)
    copy.start()
    weight_copies(1, flags, parts, w_up, w_down, weight_sems, start_copy)
    load_padded(pad, flags[0], y, y_a, y_b)
    forward_conv(W_1, pad, taps, small, normed, inverse, z, base)
    weight_copies(1, flags, parts, w_up, w_down, weight_sems, wait_copy)
    copy.wait()
    forward_mlp(W_1, small, mask, w_up, w_down, z, base, hidden, active, slope, branch, out)
    for row in range(ROWS_DEV):
        at = row * W_1 + SIDE_1
        final[row] = out[at : at + COLS_DEV, :].astype(bf16)
    backward_cells(
        W_1, flags[0], small, own, own_row, upstream, w_up, w_down, normed, inverse, z, active, slope, branch, hidden, dm, dh, du, keep, send, sums
    )
    write_rows(du, W_1, du_out)
    send_rows(flags[0], du_out, send_a, send_b)


def first_backward(
    flags, du1, du1_a, du1_b, small1, small0, mask, own, own_row, active, slope, branch, w_up, w_down, kept,
    e_own, du_out, send_a, send_b, keep, send, sums,
    pad, taps, hidden, upstream, z, dm, dh, du, normed, inverse, sems,
):
    copies = kept_copies(kept, sems, [(upstream, AT_E_0), (normed, AT_NORMED), (inverse, AT_INVERSE)], False)
    for copy in copies:
        copy.start()
    shift = SIDE_0 + REACH - SIDE_1
    pad[:, :, 0:8, :] = jnp.zeros((2, ROWS_DEV + 2 * REACH, 8, HALF), f32)
    pad[:, :, W_X - 16 : W_X, :] = jnp.zeros((2, ROWS_DEV + 2 * REACH, 16, HALF), f32)
    load_padded(pad, flags[0], du1, du1_a, du1_b, shift)
    load_taps(taps, small1)
    copies[0].wait()
    for group in groups(W_0, 4):
        starts = [tile * 8 for tile in group]
        for half in range(2):
            spread = conv_tiles(pad, taps, half, starts, True)
            for index, start in enumerate(starts):
                for row in range(ROWS_DEV):
                    at = slice(row * W_0 + start, row * W_0 + start + 8)
                    value = (upstream[at, lanes(half)] + spread[index][row]).astype(bf16).astype(f32)
                    upstream[at, lanes(half)] = mask[at, :] * value
    for row in range(ROWS_DEV):
        at = row * W_0 + SIDE_0
        e_own[row] = upstream[at : at + W_OWN, :]
    for copy in copies[1:]:
        copy.wait()
    scale_cells(N_0, small0, normed, z)
    backward_cells(
        W_0, flags[0], small0, own, own_row, upstream, w_up, w_down, normed, inverse, z, active, slope, branch, hidden, dm, dh, du, keep, send, sums
    )
    write_rows(du, W_0, du_out)
    send_rows(flags[0], du_out, send_a, send_b)


def input_grad(flags, du, du_a, du_b, small, e_own, out, pad, taps, total):
    load_padded(pad, flags[0], du, du_a, du_b)
    load_taps(taps, small)
    for group in groups(W_OWN, 5):
        starts = [tile * 8 for tile in group]
        for half in range(2):
            spread = conv_tiles(pad, taps, half, [start + SIDE_0 - REACH for start in starts], True)
            for index, start in enumerate(starts):
                for row in range(ROWS_DEV):
                    at = slice(start, start + 8)
                    total[row, at, lanes(half)] = e_own[row, at, lanes(half)] + spread[index][row]
    for row in range(ROWS_DEV):
        out[row] = total[row, 0:COLS_DEV, :].astype(bf16)


def tap_grads_1(flags, pad, du, own, sums, out, grads, total):
    tap_sums(W_1, pad, du, own, sums, out, grads, total)


def tap_grads_0(flags, v, v_a, v_b, du, own, sums, out, pad, grads, total):
    load_padded(pad, flags[0], v, v_a, v_b)
    tap_sums(W_0, pad, du, own, sums, out, grads, total)


def tap_sums(width, pad, du, own, sums, out, grads, total):
    for row in range(ROWS_DEV):
        inside = own[row * width : (row + 1) * width, :]
        grads[row] = du[row].astype(f32) * twice(inside)
    total[...] = jnp.zeros((SMALL, WIDE), f32)
    for half in range(2):
        for offsets in (range(0, 4), range(4, KERNEL)):
            partial = [[None] * KERNEL for _ in offsets]
            for tile in range(width // 8):
                start = tile * 8
                grad = [grads[row, start : start + 8, lanes(half)] for row in range(ROWS_DEV)]
                for row in range(ROWS_DEV + KERNEL - 1):
                    for index, col_off in enumerate(offsets):
                        window = pad[half, row, start + col_off : start + col_off + 8, :]
                        for out_row in range(ROWS_DEV):
                            row_off = row - out_row
                            if 0 <= row_off < KERNEL:
                                term = window * grad[out_row]
                                held = partial[index][row_off]
                                partial[index][row_off] = term if held is None else held + term
            for index, col_off in enumerate(offsets):
                for row_off in range(KERNEL):
                    tap = row_off * KERNEL + col_off
                    total[tap : tap + 1, lanes(half)] = jnp.sum(partial[index][row_off], axis=0, keepdims=True)
    total[TAPS : TAPS + 9, :] = sums[0:9, :]
    out[...] = total[...].astype(bf16)


factor = 1.0 / math.sqrt(BATCH * ROWS_DEV * COLS_DEV)


def write_weights(is_up, rows, up, down, up_vmem, down_vmem, sems, beside=None):
    def send(copies, fill):
        for quarter in range(QUARTERS):
            fill(quarter, rows[quarter * WIDE : (quarter + 1) * WIDE, :].astype(f32) * factor)
            copies[quarter].start()
        if beside:
            beside()
        for copy in copies:
            copy.wait()

    def cols(quarter):
        return slice(quarter * WIDE, (quarter + 1) * WIDE)

    @pl.when(is_up)
    def _():
        def fill(quarter, value):
            up_vmem[:, cols(quarter)] = value

        send([pltpu.make_async_copy(up_vmem.at[:, cols(q)], up.at[0, :, cols(q)], sems.at[0, q]) for q in range(QUARTERS)], fill)

    @pl.when(jnp.logical_not(is_up))
    def _():
        def fill(quarter, value):
            down_vmem[cols(quarter), :] = value

        send([pltpu.make_async_copy(down_vmem.at[cols(q), :], down.at[0, cols(q), :], sems.at[1, q]) for q in range(QUARTERS)], fill)


def finish_own(flags, piece, up, down, up_vmem, down_vmem, sems):
    write_weights(flags[0] == 0, piece, up, down, up_vmem, down_vmem, sems)


def finish_got(flags, small, got, up_in, down_in, up, down, taps, channels, bias, up_vmem, down_vmem, sems):
    def rest():
        sums = (small[...].astype(f32) + got[HID:, :].astype(f32)) * factor
        for tap in range(TAPS):
            taps[tap] = sums[tap : tap + 1]
        for index in range(5):
            channels[index] = sums[TAPS + index : TAPS + index + 1]
        for quarter in range(QUARTERS):
            bias[:, quarter * WIDE : (quarter + 1) * WIDE] = sums[TAPS + 5 + quarter : TAPS + 6 + quarter]

    write_weights(flags[0] == 1, got, up, down, up_vmem, down_vmem, sems, rest)


def in_vmem():
    return pl.BlockSpec(memory_space=pltpu.VMEM)


def call(body, name, inputs, outputs, scratch, flops, hbm_in=0, hbm_out=0, sems=(), aliases=None):
    in_hbm = pl.BlockSpec(memory_space=pltpu.HBM)
    return pl.pallas_call(
        body,
        name=name,
        out_shape=[jax.ShapeDtypeStruct(shape, dtype) for shape, dtype in outputs],
        in_specs=[pl.BlockSpec(memory_space=pltpu.SMEM)] + [in_vmem()] * (len(inputs) - 1 - hbm_in) + [in_hbm] * hbm_in,
        out_specs=[in_hbm] * hbm_out + [in_vmem()] * (len(outputs) - hbm_out),
        input_output_aliases=aliases or {},
        scratch_shapes=[pltpu.VMEM(shape, dtype) for shape, dtype in scratch] + [pltpu.SemaphoreType.DMA(shape) for shape in sems],
        compiler_params=pltpu.CompilerParams(vmem_limit_bytes=28 << 20),
        cost_estimate=pl.CostEstimate(flops=10 * flops, bytes_accessed=4 << 20, transcendentals=0),
    )(*inputs)


def swap_pairs(count, bit):
    return [(i, i ^ bit) for i in range(count)]


def on_device(
    window_input,
    output_cotangent,
    ocean_mask,
    dw_kernel,
    channel_params,
    up_weight,
    up_bias,
    down_weight,
):
    section = lax.axis_index("section")
    lat = lax.axis_index("lat")
    lon = lax.axis_index("lon")
    n_lat, n_lon = lax.axis_size("lat"), lax.axis_size("lon")
    odd = lat % 2
    flags = jnp.stack([odd, section]).astype(jnp.int32)
    channels = window_input.shape[-1]

    def over_section(value):
        return lax.ppermute(value, "section", [(0, 1), (1, 0)])

    def over_core(value):
        return lax.ppermute(value, "lat", swap_pairs(n_lat, 1))

    def lat_halo(send_a, send_b, choose=False):
        pairs = [(i, i + 1) for i in range(1, n_lat - 1, 2)]
        pairs += [(j, i) for i, j in pairs]
        got_b = lax.ppermute(send_b, "lat", pairs)
        if not choose:
            return over_core(send_a), got_b
        beside = jnp.where(odd == 1, lat < n_lat - 1, lat > 0)
        return over_core(send_a), jnp.where(beside, got_b, jnp.zeros_like(got_b))

    def by_core(even, other):
        return jnp.where(odd == 0, even, other)

    x = lax.dynamic_index_in_dim(window_input, section, 0, False)
    cot = lax.dynamic_index_in_dim(output_cotangent, section, 0, False)
    sea = ocean_mask.astype(bf16)

    def packed(x_part, cot_part, sea_part):
        sea_row = jnp.pad(sea_part, ((0, 0), (0, channels - sea_part.shape[1])))[:, None, :]
        return jnp.concatenate([x_part, cot_part, sea_row], axis=1)

    ring = [(i, (i + 1) % n_lon) for i in range(n_lon)]
    to_right = packed(x[:, -SIDE_X:], cot[:, -SIDE_1:], sea[:, -SIDE_0:])
    to_left = packed(x[:, :SIDE_X], cot[:, :SIDE_1], sea[:, :SIDE_0])
    to_right, to_left, dw_kernel = lax.optimization_barrier((to_right, to_left, dw_kernel))
    left = lax.ppermute(to_right, "lon", ring)
    right = lax.ppermute(to_left, "lon", [(j, i) for i, j in ring])
    small_own = jnp.concatenate(
        [dw_kernel[0], channel_params[0], up_bias[0].reshape(QUARTERS, WIDE), jnp.zeros((SMALL - TAPS - 9, WIDE), bf16)], axis=0
    )
    up, down = up_weight[0], down_weight[0]
    cut = channels // 2
    small_got = over_section(small_own)
    send_up = by_core(up[:cut], up[cut:])
    send_down = by_core(down[: HID // 2], down[HID // 2 :])
    send_up, send_down, small_got = lax.optimization_barrier((send_up, send_down, small_got))
    got_up, got_down = over_section(send_up), over_section(send_down)
    small_0 = jnp.where(section == 0, small_own, small_got).astype(f32)
    small_1 = jnp.where(section == 0, small_got, small_own).astype(f32)

    before = SIDE_0 - SIDE_1
    sea_at = SIDE_X + SIDE_1
    x_wide = jnp.concatenate([left[:, :SIDE_X], x, right[:, :SIDE_X], jnp.zeros((ROWS_DEV, W_X - COLS_DEV - 2 * SIDE_X, channels), bf16)], axis=1)
    x_a, x_b = lat_halo(by_core(x_wide[1:], x_wide[:REACH]), by_core(x_wide[:REACH], x_wide[1:]), True)
    mask_wide = jnp.concatenate(
        [left[:, sea_at, :SIDE_0], sea, right[:, sea_at, :SIDE_0], jnp.zeros((ROWS_DEV, W_0 - COLS_DEV - 2 * SIDE_0), bf16)], axis=1
    )
    before = SIDE_0 - SIDE_1
    def spread_lanes(mask):
        flat = mask.astype(f32).reshape(-1, 1)
        return jnp.broadcast_to(flat, (flat.shape[0], HALF))

    mask_0, mask_1 = spread_lanes(mask_wide), spread_lanes(mask_wide[:, before : before + W_1])

    def own_cells(width, side):
        column = jnp.arange(width)
        inside = ((column >= side) & (column < side + COLS_DEV)).astype(f32)
        flat = jnp.tile(inside, ROWS_DEV)
        return jnp.broadcast_to(flat[:, None], (flat.shape[0], HALF)), jnp.broadcast_to(flat[None, :], (16, flat.shape[0])).astype(bf16)

    own_0, row_0 = own_cells(W_0, SIDE_0)
    own_1, row_1 = own_cells(W_1, SIDE_1)

    deep = ROWS_DEV + 2 * REACH
    taps_scratch = ((2, TAPS, 8, HALF), f32)

    (kept,) = call(
        first_conv,
        "first_conv",
        (flags, x_wide, x_a, x_b, small_0, mask_0, cot, left, right),
        [((KEPT_ROWS, WIDE), f32)],
        [
            ((2, deep, W_X, HALF), f32), taps_scratch, ((N_0, WIDE), f32), ((N_0, WIDE), f32), ((N_0, HALF), f32),
            ((N_0, WIDE), bf16), ((N_0, WIDE), f32), ((N_1, WIDE), f32),
        ],
        2_000_000_000,
        hbm_out=1,
        sems=((5,),),
    )
    got_up, got_down, kept = lax.optimization_barrier((got_up, got_down, kept))
    other_up, other_down = over_core(got_up), over_core(got_down)
    weights = (up, down, got_up, got_down, other_up, other_down)
    y, y_send_a, y_send_b = call(
        first_forward,
        "first_forward",
        (flags, small_0, mask_0, kept) + weights,
        [((ROWS_DEV, W_0, WIDE), bf16), ((REACH, W_0, WIDE), bf16), ((REACH, W_0, WIDE), bf16)],
        [
            ((N_0, WIDE), f32), ((N_0, WIDE), bf16), ((N_0, WIDE), f32), ((2, N_0, WIDE), f32), ((N_0, WIDE), f32),
            ((N_0, HID), bf16), ((N_0, HID), f32), ((N_0, WIDE), f32), ((WIDE, HID), bf16), ((HID, WIDE), bf16),
        ],
        2_000_000_000,
        hbm_in=7,
        sems=((6,), (2,)),
    )
    y_a, y_b = lat_halo(y_send_a, y_send_b)
    final, du1, du1_send_a, du1_send_b, keep_1, send_1, sums_1, pad_1 = call(
        second_block,
        "second_block",
        (flags, y, y_a, y_b, small_1, mask_1, own_1, row_1, kept) + weights,
        [
            ((ROWS_DEV, COLS_DEV, WIDE), bf16), ((ROWS_DEV, W_1, WIDE), bf16), ((REACH, W_1, WIDE), bf16), ((REACH, W_1, WIDE), bf16),
            ((HID, WIDE), bf16), ((HID, WIDE), bf16), ((16, WIDE), f32), ((2, deep, W_0, HALF), f32),
        ],
        [
            taps_scratch, ((2, N_1, WIDE), f32), ((N_1, WIDE), f32),
            ((N_1, WIDE), f32), ((N_1, HALF), f32), ((N_1, WIDE), bf16), ((N_1, WIDE), f32), ((N_1, HID), bf16), ((N_1, HID), f32), ((N_1, WIDE), f32),
            ((WIDE, HID), bf16), ((HID, WIDE), bf16), ((N_1, WIDE), f32), ((N_1, WIDE), bf16), ((N_1, HID), bf16), ((N_1, WIDE), f32),
        ],
        4_000_000_000,
        hbm_in=7,
        sems=((6,), (1,)),
    )
    du1_a, du1_b = lat_halo(du1_send_a, du1_send_b)
    bits = [("lat", 1 << i) for i in range(1, n_lat.bit_length() - 1)] + [("lon", 1 << i) for i in range(n_lon.bit_length() - 1)]
    orders = (bits, bits[1:2] + bits[:1] + bits[2:])

    def partner(place, step):
        row, col = place
        axis, bit = orders[row % 2][step]
        return (row ^ bit, col) if axis == "lat" else (row, col ^ bit)

    def exchange(value, step):
        pairs = []
        for row in range(n_lat):
            for col in range(n_lon):
                other = partner((row, col), step)
                pairs.append((row * n_lon + col, other[0] * n_lon + other[1]))
        return lax.ppermute(value, ("lat", "lon"), pairs)

    def side(step):
        def of(order):
            axis, bit = order[step]
            return ((lat if axis == "lat" else lon) // bit) % 2

        return jnp.where(odd == 0, of(orders[0]), of(orders[1]))

    def plus(first, second):
        return (first.astype(f32) + second.astype(f32)).astype(bf16)

    def reduce_scatter(keep, send):
        piece = plus(keep, over_core(send))
        for step in range(len(bits)):
            half = piece.shape[0] // 2
            low, high = piece[:half], piece[half:]
            which = side(step) == 0
            piece = plus(jnp.where(which, low, high), exchange(jnp.where(which, high, low), step))
        return piece

    def reduce_send(piece, step):
        half = piece.shape[-2] // 2
        low, high = piece[..., :half, :], piece[..., half:, :]
        which = side(step) == 0
        return jnp.where(which, low, high), exchange(jnp.where(which, high, low), step)

    def reduce_step(piece, step):
        return plus(*reduce_send(piece, step))

    small_again, _ = lax.optimization_barrier((small_0, du1_send_a))
    active, slope, branch, w_up, w_down = call(
        first_again,
        "first_again",
        (flags, small_again, kept) + weights,
        [((N_0, HID), bf16), ((N_0, HID), f32), ((N_0, WIDE), f32), ((WIDE, HID), bf16), ((HID, WIDE), bf16)],
        [((N_0, WIDE), f32), ((N_0, WIDE), bf16), ((2, N_0, WIDE), f32)],
        2_000_000_000,
        hbm_in=7,
        sems=((6,), (1,)),
    )
    send_1, du1_a = lax.optimization_barrier((send_1, du1_a))
    held_1, got_1 = reduce_send(plus(keep_1, over_core(send_1)), 0)
    e_own, du0, du0_send_a, du0_send_b, keep_0, send_0, sums_0 = call(
        first_backward,
        "first_backward",
        (flags, du1, du1_a, du1_b, small_1, small_0, mask_0, own_0, row_0, active, slope, branch, w_up, w_down, kept),
        [
            ((ROWS_DEV, W_OWN, WIDE), f32), ((ROWS_DEV, W_0, WIDE), bf16), ((REACH, W_0, WIDE), bf16), ((REACH, W_0, WIDE), bf16),
            ((HID, WIDE), bf16), ((HID, WIDE), bf16), ((16, WIDE), f32),
        ],
        [
            ((2, deep, W_X, HALF), f32), taps_scratch, ((2, N_0, WIDE), f32), ((N_0, WIDE), f32), ((N_0, WIDE), bf16),
            ((N_0, WIDE), bf16), ((N_0, HID), bf16), ((N_0, WIDE), f32),
            ((N_0, WIDE), f32), ((N_0, HALF), f32),
        ],
        3_000_000_000,
        hbm_in=1,
        sems=((3,),),
    )
    to_first = section == 0

    def chosen(first, second):
        return jnp.where(to_first, first, second)

    core_0 = over_core(send_0)
    (taps_0,) = call(
        tap_grads_0, "tap_grads_0", (flags, x_wide, x_a, x_b, du0, own_0, sums_0), [((SMALL, WIDE), bf16)],
        [((2, deep, W_X, HALF), f32), ((ROWS_DEV, W_0, WIDE), f32), ((SMALL, WIDE), f32)], 2_000_000_000,
    )
    core_0, taps_0, pad_1 = lax.optimization_barrier((core_0, taps_0, pad_1))
    piece_0 = plus(keep_0, core_0)
    (taps_1,) = call(
        tap_grads_1, "tap_grads_1", (flags, pad_1, du1, own_1, sums_1), [((SMALL, WIDE), bf16)],
        [((ROWS_DEV, W_1, WIDE), f32), ((SMALL, WIDE), f32)], 2_000_000_000,
    )
    held_0, got_0 = reduce_send(piece_0, 0)
    taps_1, du0_send_a, du0_send_b = lax.optimization_barrier((taps_1, du0_send_a, du0_send_b))
    du0_a, du0_b = lat_halo(du0_send_a, du0_send_b)
    got_0, got_1, du0_a, du0_b = lax.optimization_barrier((got_0, got_1, du0_a, du0_b))
    pieces = jnp.stack([plus(held_0, got_0), plus(held_1, got_1)])
    pieces = reduce_step(pieces, 1)
    (start,) = call(
        input_grad, "input_grad", (flags, du0, du0_a, du0_b, small_0, e_own), [((ROWS_DEV, COLS_DEV, WIDE), bf16)],
        [((2, deep, W_0, HALF), f32), taps_scratch, ((ROWS_DEV, W_OWN, WIDE), f32)], 2_000_000_000,
    )
    for step in range(2, len(bits)):
        pieces = reduce_step(pieces, step)
    pieces, start = lax.optimization_barrier((pieces, start))
    other_end = over_section(chosen(final, start))
    piece_0, piece_1 = pieces[0], pieces[1]
    cut = piece_0.shape[0]
    boundary = jnp.stack([chosen(start, other_end), chosen(other_end, final)])[None]

    def both(piece, small):
        return jnp.concatenate([piece, small], axis=0)

    got = over_section(both(chosen(piece_1, piece_0), chosen(taps_1, taps_0)))
    piece = plus(chosen(piece_0, piece_1), got[:cut])
    small = plus(chosen(taps_0, taps_1), got[cut:])
    for step in reversed(range(len(bits))):
        if step == 0:
            piece, boundary = lax.optimization_barrier((piece, boundary))
        got = exchange(both(piece, small), step)
        cut = piece.shape[0]
        small = plus(small, got[cut:])
        which = side(step) == 0
        piece = jnp.where(which, jnp.concatenate([piece, got[:cut]]), jnp.concatenate([got[:cut], piece]))
    got = over_core(both(piece, small))
    weight_outs = [((1, WIDE, HID), f32), ((1, HID, WIDE), f32)]
    weight_scratch = [((WIDE, HID), f32), ((HID, WIDE), f32)]
    halves = call(
        finish_own, "finish_own", (flags, piece), weight_outs, weight_scratch, 1_000_000, hbm_out=2, sems=((2, QUARTERS),)
    )
    grad_up, grad_down, grad_taps, grad_channels, grad_bias = call(
        finish_got,
        "finish_got",
        (flags, small, got, *halves),
        weight_outs + [((TAPS, 1, WIDE), f32), ((5, 1, WIDE), f32), ((1, HID), f32)],
        weight_scratch,
        1_000_000,
        hbm_in=2,
        hbm_out=2,
        sems=((2, QUARTERS),),
        aliases={3: 0, 4: 1},
    )
    grad_taps, grad_channels = jnp.swapaxes(grad_taps, 0, 1), jnp.swapaxes(grad_channels, 0, 1)
    return (
        boundary,
        grad_taps,
        grad_channels,
        grad_up,
        grad_bias,
        grad_down,
    )


def solution(mesh):
    in_specs = (
        P(None, "lat", "lon", None),
        P(None, "lat", "lon", None),
        P("lat", "lon"),
        P("section", None, None),
        P("section", None, None),
        P("section", None, None),
        P("section", None),
        P("section", None, None),
    )
    out_specs = (
        P("section", None, "lat", "lon", None),
        P("section", None, None),
        P("section", None, None),
        P("section", None, None),
        P("section", None),
        P("section", None, None),
    )
    return jax.shard_map(
        on_device, mesh=mesh, in_specs=in_specs, out_specs=out_specs, check_vma=False
    )
```

```python
import math

import jax
import jax.numpy as jnp
from jax import lax
from jax.experimental import pallas as pl
from jax.experimental.pallas import tpu as pltpu
from jax.sharding import PartitionSpec as P

KERNEL = 7
TAPS = KERNEL * KERNEL
REACH = KERNEL // 2
ROWS_DEV = 4
COLS_DEV = 68
BATCH = 2
HALF = 128
WIDE = 256
HID = 1024
QUARTERS = HID // WIDE
SIDE_X, SIDE_0, SIDE_1 = 12, 9, 6
W_X, W_0, W_1, W_OWN = 96, 88, 80, 72
CHUNK = 32
SMALL = 64
N_0, N_1 = ROWS_DEV * W_0, ROWS_DEV * W_1
AT_NORMED, AT_BASE, AT_INVERSE, AT_E_0, AT_E_1 = 0, N_0, 2 * N_0, 3 * N_0, 4 * N_0
KEPT_ROWS = 40960

norm_eps = 1e-06
gelu_scale = 0.7978845608028654
gelu_cubic = 0.044715
f32, bf16 = jnp.float32, jnp.bfloat16

nn = (((1,), (0,)), ((), ()))
nt = (((1,), (1,)), ((), ()))
tn = (((0,), (0,)), ((), ()))


def dot(left, right, dims=nn):
    return lax.dot_general(left, right, dims, preferred_element_type=f32)


def lanes(half):
    return slice(half * HALF, (half + 1) * HALF)


def load_padded(pad, odd, center, first, second, offset=0):
    width = center.shape[1]

    def put(row, value):
        value = value.astype(f32)
        for half in range(2):
            pad[half, row, offset : offset + width, :] = value[:, lanes(half)]

    at_first = jnp.where(odd == 1, 0, REACH + ROWS_DEV)
    at_second = jnp.where(odd == 1, REACH + ROWS_DEV, 0)
    for row in range(ROWS_DEV):
        put(REACH + row, center[row])
    for row in range(REACH):
        put(at_first + row, first[row])
        put(at_second + row, second[row])


def load_taps(taps, small):
    for half in range(2):
        taps[half] = jnp.broadcast_to(small[0:TAPS, lanes(half)][:, None, :], (TAPS, 8, HALF))


def groups(width, most):
    tiles = width // 8
    count = -(-tiles // most)
    bounds = [tiles * i // count for i in range(count + 1)]
    return [range(first, last) for first, last in zip(bounds, bounds[1:])]


def conv_tiles(pad, taps, half, starts, reverse):
    sums = [[None] * ROWS_DEV for _ in starts]
    for col_off in range(KERNEL):
        column = [taps[half, TAPS - 1 - tap if reverse else tap] for tap in range(col_off, TAPS, KERNEL)]
        for row in range(ROWS_DEV + KERNEL - 1):
            for index, start in enumerate(starts):
                window = pad[half, row, start + col_off : start + col_off + 8, :]
                for out_row in range(ROWS_DEV):
                    row_off = row - out_row
                    if 0 <= row_off < KERNEL:
                        term = window * column[row_off]
                        held = sums[index][out_row]
                        sums[index][out_row] = term if held is None else held + term
    return sums


def chunks(count, body, carry=0):
    for i in range(count // CHUNK):
        carry = body(slice(i * CHUNK, (i + 1) * CHUNK), carry)
    return carry


def fold(value):
    return jnp.sum(value.reshape(CHUNK // 8, 8, value.shape[-1]), axis=0)


def twice(value):
    return jnp.concatenate([value, value], axis=1)


def send_rows(odd, source, send_first, send_second):
    first, second = jnp.where(odd == 1, 0, 1), jnp.where(odd == 1, 1, 0)
    send_first[...] = source[pl.ds(first, REACH)]
    send_second[...] = source[pl.ds(second, REACH)]


def forward_conv(width, pad, taps, small, normed, inverse, z, base):
    count = ROWS_DEV * width
    load_taps(taps, small)
    for group in groups(width, 4):
        starts = [tile * 8 for tile in group]
        halves = [conv_tiles(pad, taps, half, starts, False) for half in range(2)]
        for index, row in [(index, row) for index in range(len(starts)) for row in range(ROWS_DEV)]:
            start = starts[index]
            u = [halves[half][index][row] + small[TAPS : TAPS + 1, lanes(half)] for half in range(2)]
            mean = jnp.sum(u[0] + u[1], axis=-1, keepdims=True) * (1.0 / WIDE)
            u = [value - mean for value in u]
            spread = jnp.sum(u[0] * u[0] + u[1] * u[1], axis=-1, keepdims=True) * (1.0 / WIDE)
            scale = lax.rsqrt(spread + norm_eps)
            at = slice(row * width + start, row * width + start + 8)
            inverse[at, :] = jnp.broadcast_to(scale, (8, HALF))
            for half in range(2):
                normed[at, lanes(half)] = u[half] * scale
                base[at, lanes(half)] = pad[half, REACH + row, start + REACH : start + REACH + 8, :]
    scale_cells(count, small, normed, z)


def scale_cells(count, small, normed, z):
    def scaled(at, carry):
        z[at, :] = (normed[at, :] * small[TAPS + 1 : TAPS + 2, :] + small[TAPS + 2 : TAPS + 3, :]).astype(bf16)
        return carry

    chunks(count, scaled, 0)


def forward_mlp(width, small, mask, w_up, w_down, z, base, hidden, active, slope, branch, out):
    count = ROWS_DEV * width
    for quarter in range(QUARTERS):
        cols = slice(quarter * WIDE, (quarter + 1) * WIDE)
        held = hidden.at[quarter % 2]
        held[...] = dot(z[...], w_up[:, cols])
        bias = small[TAPS + 5 + quarter : TAPS + 6 + quarter, :]

        def gelu(at, carry, held=held, cols=cols, bias=bias):
            h = held[at, :] + bias
            square = h * h
            tangent = jnp.tanh(h * (gelu_scale + (gelu_scale * gelu_cubic) * square))
            above = 0.5 + 0.5 * tangent
            active[at, cols] = (h * above).astype(bf16)
            slope[at, cols] = above + (0.5 * h) * (1.0 - tangent * tangent) * (
                gelu_scale + (3.0 * gelu_scale * gelu_cubic) * square
            )
            return carry

        chunks(count, gelu, 0)
    branch[...] = dot(active[...], w_down[...]) + small[TAPS + 3 : TAPS + 4, :]
    if out is None:
        return

    def residual(at, carry):
        out[at, :] = twice(mask[at, :]) * (base[at, :] + small[TAPS + 4 : TAPS + 5, :] * branch[at, :])
        return carry

    chunks(count, residual, 0)


def backward_cells(
    width, odd, small, own, own_row, upstream, w_up, w_down, normed, inverse, z, active, slope, branch, hidden, dm, dh, du, keep, send, sums
):
    count = ROWS_DEV * width
    zero = jnp.zeros((8, WIDE), f32)

    def first(at, carry):
        sum_dm, sum_em = carry
        e = upstream[at, :]
        inside = twice(own[at, :])
        grad = (e * small[TAPS + 4 : TAPS + 5, :]).astype(bf16)
        dm[at, :] = grad
        sum_dm = sum_dm + fold(grad.astype(f32) * inside)
        sum_em = sum_em + fold(e * branch[at, :] * inside)
        return sum_dm, sum_em

    sum_dm, sum_em = chunks(count, first, (zero, zero))
    for quarter in range(QUARTERS):
        cols = slice(quarter * WIDE, (quarter + 1) * WIDE)
        held = hidden.at[quarter % 2]
        held[...] = dot(dm[...], w_down[cols, :], nt)

        def through(at, carry, held=held, cols=cols):
            dh[at, cols] = (held[at, :] * slope[at, cols]).astype(bf16)
            return carry

        chunks(count, through, 0)
    hidden[0] = dot(dh[...], w_up[...], nt)
    sum_dh = dot(own_row[...], dh[...])

    def norm(at, carry):
        sum_dzn, sum_dz, sum_du = carry
        dz = hidden[0, at, :]
        normal = normed[at, :]
        inside = twice(own[at, :])
        inner = dz * inside
        sum_dz = sum_dz + fold(inner)
        sum_dzn = sum_dzn + fold(inner * normal)
        dn = dz * small[TAPS + 1 : TAPS + 2, :]
        mean = jnp.sum(dn, axis=-1, keepdims=True) * (1.0 / WIDE)
        slant = jnp.sum(dn * normal, axis=-1, keepdims=True) * (1.0 / WIDE)
        grad = (twice(inverse[at, :]) * (dn - mean - normal * slant)).astype(bf16).astype(f32)
        du[at, :] = grad
        sum_du = sum_du + fold(grad * inside)
        dm[at, :] = (dm[at, :].astype(f32) * inside).astype(bf16)
        z[at, :] = (z[at, :].astype(f32) * inside).astype(bf16)
        return sum_dzn, sum_dz, sum_du

    sum_dzn, sum_dz, sum_du = chunks(count, norm, (zero, zero, zero))
    rows = [jnp.sum(value, axis=0, keepdims=True) for value in (sum_du, sum_dzn, sum_dz, sum_dm, sum_em)]
    rows += [sum_dh[0:1, quarter * WIDE : (quarter + 1) * WIDE] for quarter in range(QUARTERS)]
    for index, value in enumerate(rows):
        sums[index : index + 1, :] = value
    sums[len(rows) : 16, :] = jnp.zeros((16 - len(rows), WIDE), f32)

    def weights(up_ref, down_ref):
        for quarter in range(QUARTERS):
            cols = slice(quarter * WIDE, (quarter + 1) * WIDE)
            up_ref[cols, :] = dot(z[...], dh[:, cols], tn).astype(bf16)
            down_ref[cols, :] = dot(active[:, cols], dm[...], tn).astype(bf16)

    @pl.when(odd == 0)
    def _():
        weights(keep, send)

    @pl.when(odd == 1)
    def _():
        weights(send, keep)


def weight_copies(block, flags, parts, w_up, w_down, sems, act):
    odd, section = flags[0], flags[1]
    own_up, own_down, got_up, got_down, other_up, other_down = parts

    @pl.when(section == block)
    def _():
        act(pltpu.make_async_copy(own_up, w_up, sems.at[0]))
        act(pltpu.make_async_copy(own_down, w_down, sems.at[1]))

    @pl.when(section != block)
    def _():
        for index, (ref, mine, other) in enumerate(((w_up, got_up, other_up), (w_down, got_down, other_down))):
            half = mine.shape[0]
            for place, part in enumerate((mine, other)):
                first = odd if place == 0 else 1 - odd
                rows = pl.ds(pl.multiple_of(first * half, half), half)
                act(pltpu.make_async_copy(part, ref.at[rows, :], sems.at[2 + 2 * index + place]))


def start_copy(copy):
    copy.start()


def wait_copy(copy):
    copy.wait()


def write_rows(source, width, out):
    for row in range(ROWS_DEV):
        out[row] = source[row * width : (row + 1) * width, :].astype(bf16)


def kept_copies(kept, sems, places, out):
    copies = []
    for index, (ref, first) in enumerate(places):
        rows = kept.at[first : first + ref.shape[0], 0 : ref.shape[1]]
        copies.append(pltpu.make_async_copy(ref, rows, sems.at[index]) if out else pltpu.make_async_copy(rows, ref, sems.at[index]))
    return copies


def first_conv(
    flags, x, x_a, x_b, small, mask, cot, left, right, kept, pad, taps, wide, normed, inverse, z, base, e_1, sems
):
    places = [(wide, AT_E_0), (e_1, AT_E_1), (normed, AT_NORMED), (base, AT_BASE), (inverse, AT_INVERSE)]
    copies = kept_copies(kept, sems, places, True)
    before = SIDE_0 - SIDE_1
    wide[...] = jnp.zeros((N_0, WIDE), f32)
    for row in range(ROWS_DEV):
        at = row * W_0 + before
        wide[at : at + SIDE_1, :] = left[row].astype(f32)[SIDE_X : SIDE_X + SIDE_1]
        wide[at + SIDE_1 : at + SIDE_1 + COLS_DEV, :] = cot[row].astype(f32)
        wide[at + SIDE_1 + COLS_DEV : at + W_1, :] = right[row].astype(f32)[SIDE_X : SIDE_X + SIDE_1]
    wide[...] = wide[...] * twice(mask[...])
    for row in range(ROWS_DEV):
        at = row * W_0 + before
        e_1[row * W_1 : (row + 1) * W_1, :] = wide[at : at + W_1, :]
    for copy in copies[:2]:
        copy.start()
    load_padded(pad, flags[0], x, x_a, x_b)
    forward_conv(W_0, pad, taps, small, normed, inverse, z, base)
    for copy in copies[2:]:
        copy.start()
    for copy in copies:
        copy.wait()


def first_forward(flags, small, mask, kept, *refs):
    parts, refs = refs[:6], refs[6:]
    y, send_a, send_b, normed, z, base, hidden, out, active, slope, branch, w_up, w_down, weight_sems, sems = refs
    copies = kept_copies(kept, sems, [(normed, AT_NORMED), (base, AT_BASE)], False)
    for copy in copies:
        copy.start()
    weight_copies(0, flags, parts, w_up, w_down, weight_sems, start_copy)
    for copy in copies:
        copy.wait()
    scale_cells(N_0, small, normed, z)
    weight_copies(0, flags, parts, w_up, w_down, weight_sems, wait_copy)
    forward_mlp(W_0, small, mask, w_up, w_down, z, base, hidden, active, slope, branch, out)
    write_rows(out, W_0, y)
    send_rows(flags[0], y, send_a, send_b)


def first_again(flags, small, kept, *refs):
    parts, refs = refs[:6], refs[6:]
    active, slope, branch, w_up, w_down, normed, z, hidden, weight_sems, sems = refs
    (copy,) = kept_copies(kept, sems, [(normed, AT_NORMED)], False)
    copy.start()
    weight_copies(0, flags, parts, w_up, w_down, weight_sems, start_copy)
    copy.wait()
    scale_cells(N_0, small, normed, z)
    weight_copies(0, flags, parts, w_up, w_down, weight_sems, wait_copy)
    forward_mlp(W_0, small, None, w_up, w_down, z, None, hidden, active, slope, branch, None)


def second_block(flags, y, y_a, y_b, small, mask, own, own_row, kept, *refs):
    parts, refs = refs[:6], refs[6:]
    final, du_out, send_a, send_b, keep, send, sums, pad = refs[:8]
    taps, hidden, out, normed, inverse, z, base, active, slope, branch, w_up, w_down, upstream, dm, dh, du, weight_sems, sems = refs[8:]
    (copy,) = kept_copies(kept, sems, [(upstream, AT_E_1)], False)
    copy.start()
    weight_copies(1, flags, parts, w_up, w_down, weight_sems, start_copy)
    load_padded(pad, flags[0], y, y_a, y_b)
    forward_conv(W_1, pad, taps, small, normed, inverse, z, base)
    weight_copies(1, flags, parts, w_up, w_down, weight_sems, wait_copy)
    copy.wait()
    forward_mlp(W_1, small, mask, w_up, w_down, z, base, hidden, active, slope, branch, out)
    for row in range(ROWS_DEV):
        at = row * W_1 + SIDE_1
        final[row] = out[at : at + COLS_DEV, :].astype(bf16)
    backward_cells(
        W_1, flags[0], small, own, own_row, upstream, w_up, w_down, normed, inverse, z, active, slope, branch, hidden, dm, dh, du, keep, send, sums
    )
    write_rows(du, W_1, du_out)
    send_rows(flags[0], du_out, send_a, send_b)


def first_backward(
    flags, du1, du1_a, du1_b, small1, small0, mask, own, own_row, active, slope, branch, w_up, w_down, kept,
    e_own, du_out, send_a, send_b, keep, send, sums,
    pad, taps, hidden, upstream, z, dm, dh, du, normed, inverse, sems,
):
    copies = kept_copies(kept, sems, [(upstream, AT_E_0), (normed, AT_NORMED), (inverse, AT_INVERSE)], False)
    for copy in copies:
        copy.start()
    shift = SIDE_0 + REACH - SIDE_1
    pad[:, :, 0:8, :] = jnp.zeros((2, ROWS_DEV + 2 * REACH, 8, HALF), f32)
    pad[:, :, W_X - 16 : W_X, :] = jnp.zeros((2, ROWS_DEV + 2 * REACH, 16, HALF), f32)
    load_padded(pad, flags[0], du1, du1_a, du1_b, shift)
    load_taps(taps, small1)
    copies[0].wait()
    for group in groups(W_0, 4):
        starts = [tile * 8 for tile in group]
        for half in range(2):
            spread = conv_tiles(pad, taps, half, starts, True)
            for index, start in enumerate(starts):
                for row in range(ROWS_DEV):
                    at = slice(row * W_0 + start, row * W_0 + start + 8)
                    value = (upstream[at, lanes(half)] + spread[index][row]).astype(bf16).astype(f32)
                    upstream[at, lanes(half)] = mask[at, :] * value
    for row in range(ROWS_DEV):
        at = row * W_0 + SIDE_0
        e_own[row] = upstream[at : at + W_OWN, :]
    for copy in copies[1:]:
        copy.wait()
    scale_cells(N_0, small0, normed, z)
    backward_cells(
        W_0, flags[0], small0, own, own_row, upstream, w_up, w_down, normed, inverse, z, active, slope, branch, hidden, dm, dh, du, keep, send, sums
    )
    write_rows(du, W_0, du_out)
    send_rows(flags[0], du_out, send_a, send_b)


def input_grad(flags, du, du_a, du_b, small, e_own, out, pad, taps, total):
    load_padded(pad, flags[0], du, du_a, du_b)
    load_taps(taps, small)
    for group in groups(W_OWN, 5):
        starts = [tile * 8 for tile in group]
        for half in range(2):
            spread = conv_tiles(pad, taps, half, [start + SIDE_0 - REACH for start in starts], True)
            for index, start in enumerate(starts):
                for row in range(ROWS_DEV):
                    at = slice(start, start + 8)
                    total[row, at, lanes(half)] = e_own[row, at, lanes(half)] + spread[index][row]
    for row in range(ROWS_DEV):
        out[row] = total[row, 0:COLS_DEV, :].astype(bf16)


def tap_grads_1(flags, pad, du, own, sums, out, grads, total):
    tap_sums(W_1, pad, du, own, sums, out, grads, total)


def tap_grads_0(flags, v, v_a, v_b, du, own, sums, out, pad, grads, total):
    load_padded(pad, flags[0], v, v_a, v_b)
    tap_sums(W_0, pad, du, own, sums, out, grads, total)


def tap_sums(width, pad, du, own, sums, out, grads, total):
    for row in range(ROWS_DEV):
        inside = own[row * width : (row + 1) * width, :]
        grads[row] = du[row].astype(f32) * twice(inside)
    total[...] = jnp.zeros((SMALL, WIDE), f32)
    for half in range(2):
        for offsets in (range(0, 4), range(4, KERNEL)):
            partial = [[None] * KERNEL for _ in offsets]
            for tile in range(width // 8):
                start = tile * 8
                grad = [grads[row, start : start + 8, lanes(half)] for row in range(ROWS_DEV)]
                for row in range(ROWS_DEV + KERNEL - 1):
                    for index, col_off in enumerate(offsets):
                        window = pad[half, row, start + col_off : start + col_off + 8, :]
                        for out_row in range(ROWS_DEV):
                            row_off = row - out_row
                            if 0 <= row_off < KERNEL:
                                term = window * grad[out_row]
                                held = partial[index][row_off]
                                partial[index][row_off] = term if held is None else held + term
            for index, col_off in enumerate(offsets):
                for row_off in range(KERNEL):
                    tap = row_off * KERNEL + col_off
                    total[tap : tap + 1, lanes(half)] = jnp.sum(partial[index][row_off], axis=0, keepdims=True)
    total[TAPS : TAPS + 9, :] = sums[0:9, :]
    out[...] = total[...].astype(bf16)


factor = 1.0 / math.sqrt(BATCH * ROWS_DEV * COLS_DEV)


def write_weights(is_up, rows, up, down, up_vmem, down_vmem, sems, beside=None):
    def send(copies, fill):
        for quarter in range(QUARTERS):
            fill(quarter, rows[quarter * WIDE : (quarter + 1) * WIDE, :].astype(f32) * factor)
            copies[quarter].start()
        if beside:
            beside()
        for copy in copies:
            copy.wait()

    def cols(quarter):
        return slice(quarter * WIDE, (quarter + 1) * WIDE)

    @pl.when(is_up)
    def _():
        def fill(quarter, value):
            up_vmem[:, cols(quarter)] = value

        send([pltpu.make_async_copy(up_vmem.at[:, cols(q)], up.at[0, :, cols(q)], sems.at[0, q]) for q in range(QUARTERS)], fill)

    @pl.when(jnp.logical_not(is_up))
    def _():
        def fill(quarter, value):
            down_vmem[cols(quarter), :] = value

        send([pltpu.make_async_copy(down_vmem.at[cols(q), :], down.at[0, cols(q), :], sems.at[1, q]) for q in range(QUARTERS)], fill)


def finish_own(flags, piece, up, down, up_vmem, down_vmem, sems):
    write_weights(flags[0] == 0, piece, up, down, up_vmem, down_vmem, sems)


def finish_got(flags, small, got, up_in, down_in, up, down, taps, channels, bias, up_vmem, down_vmem, sems):
    def rest():
        sums = (small[...].astype(f32) + got[HID:, :].astype(f32)) * factor
        for tap in range(TAPS):
            taps[tap] = sums[tap : tap + 1]
        for index in range(5):
            channels[index] = sums[TAPS + index : TAPS + index + 1]
        for quarter in range(QUARTERS):
            bias[:, quarter * WIDE : (quarter + 1) * WIDE] = sums[TAPS + 5 + quarter : TAPS + 6 + quarter]

    write_weights(flags[0] == 1, got, up, down, up_vmem, down_vmem, sems, rest)


def in_vmem():
    return pl.BlockSpec(memory_space=pltpu.VMEM)


def call(body, name, inputs, outputs, scratch, flops, hbm_in=0, hbm_out=0, sems=(), aliases=None):
    in_hbm = pl.BlockSpec(memory_space=pltpu.HBM)
    return pl.pallas_call(
        body,
        name=name,
        out_shape=[jax.ShapeDtypeStruct(shape, dtype) for shape, dtype in outputs],
        in_specs=[pl.BlockSpec(memory_space=pltpu.SMEM)] + [in_vmem()] * (len(inputs) - 1 - hbm_in) + [in_hbm] * hbm_in,
        out_specs=[in_hbm] * hbm_out + [in_vmem()] * (len(outputs) - hbm_out),
        input_output_aliases=aliases or {},
        scratch_shapes=[pltpu.VMEM(shape, dtype) for shape, dtype in scratch] + [pltpu.SemaphoreType.DMA(shape) for shape in sems],
        compiler_params=pltpu.CompilerParams(vmem_limit_bytes=28 << 20),
        cost_estimate=pl.CostEstimate(flops=10 * flops, bytes_accessed=4 << 20, transcendentals=0),
    )(*inputs)


def swap_pairs(count, bit):
    return [(i, i ^ bit) for i in range(count)]


def on_device(
    window_input,
    output_cotangent,
    ocean_mask,
    dw_kernel,
    channel_params,
    up_weight,
    up_bias,
    down_weight,
):
    section = lax.axis_index("section")
    lat = lax.axis_index("lat")
    lon = lax.axis_index("lon")
    n_lat, n_lon = lax.axis_size("lat"), lax.axis_size("lon")
    odd = lat % 2
    flags = jnp.stack([odd, section]).astype(jnp.int32)
    channels = window_input.shape[-1]

    def over_section(value):
        return lax.ppermute(value, "section", [(0, 1), (1, 0)])

    def over_core(value):
        return lax.ppermute(value, "lat", swap_pairs(n_lat, 1))

    def lat_halo(send_a, send_b, choose=False):
        pairs = [(i, i + 1) for i in range(1, n_lat - 1, 2)]
        pairs += [(j, i) for i, j in pairs]
        got_b = lax.ppermute(send_b, "lat", pairs)
        if not choose:
            return over_core(send_a), got_b
        beside = jnp.where(odd == 1, lat < n_lat - 1, lat > 0)
        return over_core(send_a), jnp.where(beside, got_b, jnp.zeros_like(got_b))

    def by_core(even, other):
        return jnp.where(odd == 0, even, other)

    x = lax.dynamic_index_in_dim(window_input, section, 0, False)
    cot = lax.dynamic_index_in_dim(output_cotangent, section, 0, False)
    sea = ocean_mask.astype(bf16)

    def packed(x_part, cot_part, sea_part):
        sea_row = jnp.pad(sea_part, ((0, 0), (0, channels - sea_part.shape[1])))[:, None, :]
        return jnp.concatenate([x_part, cot_part, sea_row], axis=1)

    ring = [(i, (i + 1) % n_lon) for i in range(n_lon)]
    to_right = packed(x[:, -SIDE_X:], cot[:, -SIDE_1:], sea[:, -SIDE_0:])
    to_left = packed(x[:, :SIDE_X], cot[:, :SIDE_1], sea[:, :SIDE_0])
    to_right, to_left, dw_kernel, up_bias = lax.optimization_barrier((to_right, to_left, dw_kernel, up_bias))
    left = lax.ppermute(to_right, "lon", ring)
    right = lax.ppermute(to_left, "lon", [(j, i) for i, j in ring])
    small_own = jnp.concatenate(
        [dw_kernel[0], channel_params[0], up_bias[0].reshape(QUARTERS, WIDE), jnp.zeros((SMALL - TAPS - 9, WIDE), bf16)], axis=0
    )
    up, down = up_weight[0], down_weight[0]
    cut = channels // 2
    small_got = over_section(small_own)
    send_up = by_core(up[:cut], up[cut:])
    send_down = by_core(down[: HID // 2], down[HID // 2 :])
    send_up, send_down, small_got = lax.optimization_barrier((send_up, send_down, small_got))
    got_up, got_down = over_section(send_up), over_section(send_down)
    small_0 = jnp.where(section == 0, small_own, small_got).astype(f32)
    small_1 = jnp.where(section == 0, small_got, small_own).astype(f32)

    before = SIDE_0 - SIDE_1
    sea_at = SIDE_X + SIDE_1
    x_wide = jnp.concatenate([left[:, :SIDE_X], x, right[:, :SIDE_X], jnp.zeros((ROWS_DEV, W_X - COLS_DEV - 2 * SIDE_X, channels), bf16)], axis=1)
    x_a, x_b = lat_halo(by_core(x_wide[1:], x_wide[:REACH]), by_core(x_wide[:REACH], x_wide[1:]), True)
    mask_wide = jnp.concatenate(
        [left[:, sea_at, :SIDE_0], sea, right[:, sea_at, :SIDE_0], jnp.zeros((ROWS_DEV, W_0 - COLS_DEV - 2 * SIDE_0), bf16)], axis=1
    )
    before = SIDE_0 - SIDE_1
    def spread_lanes(mask):
        flat = mask.astype(f32).reshape(-1, 1)
        return jnp.broadcast_to(flat, (flat.shape[0], HALF))

    mask_0, mask_1 = spread_lanes(mask_wide), spread_lanes(mask_wide[:, before : before + W_1])

    def own_cells(width, side):
        column = jnp.arange(width)
        inside = ((column >= side) & (column < side + COLS_DEV)).astype(f32)
        flat = jnp.tile(inside, ROWS_DEV)
        return jnp.broadcast_to(flat[:, None], (flat.shape[0], HALF)), jnp.broadcast_to(flat[None, :], (16, flat.shape[0])).astype(bf16)

    own_0, row_0 = own_cells(W_0, SIDE_0)
    own_1, row_1 = own_cells(W_1, SIDE_1)

    deep = ROWS_DEV + 2 * REACH
    taps_scratch = ((2, TAPS, 8, HALF), f32)

    (kept,) = call(
        first_conv,
        "first_conv",
        (flags, x_wide, x_a, x_b, small_0, mask_0, cot, left, right),
        [((KEPT_ROWS, WIDE), f32)],
        [
            ((2, deep, W_X, HALF), f32), taps_scratch, ((N_0, WIDE), f32), ((N_0, WIDE), f32), ((N_0, HALF), f32),
            ((N_0, WIDE), bf16), ((N_0, WIDE), f32), ((N_1, WIDE), f32),
        ],
        2_000_000_000,
        hbm_out=1,
        sems=((5,),),
    )
    got_up, got_down, kept = lax.optimization_barrier((got_up, got_down, kept))
    other_up, other_down = over_core(got_up), over_core(got_down)
    weights = (up, down, got_up, got_down, other_up, other_down)
    y, y_send_a, y_send_b = call(
        first_forward,
        "first_forward",
        (flags, small_0, mask_0, kept) + weights,
        [((ROWS_DEV, W_0, WIDE), bf16), ((REACH, W_0, WIDE), bf16), ((REACH, W_0, WIDE), bf16)],
        [
            ((N_0, WIDE), f32), ((N_0, WIDE), bf16), ((N_0, WIDE), f32), ((2, N_0, WIDE), f32), ((N_0, WIDE), f32),
            ((N_0, HID), bf16), ((N_0, HID), f32), ((N_0, WIDE), f32), ((WIDE, HID), bf16), ((HID, WIDE), bf16),
        ],
        2_000_000_000,
        hbm_in=7,
        sems=((6,), (2,)),
    )
    y_a, y_b = lat_halo(y_send_a, y_send_b, True)
    final, du1, du1_send_a, du1_send_b, keep_1, send_1, sums_1, pad_1 = call(
        second_block,
        "second_block",
        (flags, y, y_a, y_b, small_1, mask_1, own_1, row_1, kept) + weights,
        [
            ((ROWS_DEV, COLS_DEV, WIDE), bf16), ((ROWS_DEV, W_1, WIDE), bf16), ((REACH, W_1, WIDE), bf16), ((REACH, W_1, WIDE), bf16),
            ((HID, WIDE), bf16), ((HID, WIDE), bf16), ((16, WIDE), f32), ((2, deep, W_0, HALF), f32),
        ],
        [
            taps_scratch, ((2, N_1, WIDE), f32), ((N_1, WIDE), f32),
            ((N_1, WIDE), f32), ((N_1, HALF), f32), ((N_1, WIDE), bf16), ((N_1, WIDE), f32), ((N_1, HID), bf16), ((N_1, HID), f32), ((N_1, WIDE), f32),
            ((WIDE, HID), bf16), ((HID, WIDE), bf16), ((N_1, WIDE), f32), ((N_1, WIDE), bf16), ((N_1, HID), bf16), ((N_1, WIDE), f32),
        ],
        4_000_000_000,
        hbm_in=7,
        sems=((6,), (1,)),
    )
    du1_a, du1_b = lat_halo(du1_send_a, du1_send_b)
    bits = [("lat", 1 << i) for i in range(1, n_lat.bit_length() - 1)] + [("lon", 1 << i) for i in range(n_lon.bit_length() - 1)]
    orders = (bits, bits[1:2] + bits[:1] + bits[2:])

    def partner(place, step):
        row, col = place
        axis, bit = orders[row % 2][step]
        return (row ^ bit, col) if axis == "lat" else (row, col ^ bit)

    def exchange(value, step):
        pairs = []
        for row in range(n_lat):
            for col in range(n_lon):
                other = partner((row, col), step)
                pairs.append((row * n_lon + col, other[0] * n_lon + other[1]))
        return lax.ppermute(value, ("lat", "lon"), pairs)

    def side(step):
        def of(order):
            axis, bit = order[step]
            return ((lat if axis == "lat" else lon) // bit) % 2

        return jnp.where(odd == 0, of(orders[0]), of(orders[1]))

    def plus(first, second):
        return (first.astype(f32) + second.astype(f32)).astype(bf16)

    def reduce_scatter(keep, send):
        piece = plus(keep, over_core(send))
        for step in range(len(bits)):
            half = piece.shape[0] // 2
            low, high = piece[:half], piece[half:]
            which = side(step) == 0
            piece = plus(jnp.where(which, low, high), exchange(jnp.where(which, high, low), step))
        return piece

    def reduce_send(piece, step):
        half = piece.shape[-2] // 2
        low, high = piece[..., :half, :], piece[..., half:, :]
        which = side(step) == 0
        return jnp.where(which, low, high), exchange(jnp.where(which, high, low), step)

    def reduce_step(piece, step):
        return plus(*reduce_send(piece, step))

    small_again, _ = lax.optimization_barrier((small_0, du1_send_a))
    active, slope, branch, w_up, w_down = call(
        first_again,
        "first_again",
        (flags, small_again, kept) + weights,
        [((N_0, HID), bf16), ((N_0, HID), f32), ((N_0, WIDE), f32), ((WIDE, HID), bf16), ((HID, WIDE), bf16)],
        [((N_0, WIDE), f32), ((N_0, WIDE), bf16), ((2, N_0, WIDE), f32)],
        2_000_000_000,
        hbm_in=7,
        sems=((6,), (1,)),
    )
    send_1, du1_a = lax.optimization_barrier((send_1, du1_a))
    held_1, got_1 = reduce_send(plus(keep_1, over_core(send_1)), 0)
    e_own, du0, du0_send_a, du0_send_b, keep_0, send_0, sums_0 = call(
        first_backward,
        "first_backward",
        (flags, du1, du1_a, du1_b, small_1, small_0, mask_0, own_0, row_0, active, slope, branch, w_up, w_down, kept),
        [
            ((ROWS_DEV, W_OWN, WIDE), f32), ((ROWS_DEV, W_0, WIDE), bf16), ((REACH, W_0, WIDE), bf16), ((REACH, W_0, WIDE), bf16),
            ((HID, WIDE), bf16), ((HID, WIDE), bf16), ((16, WIDE), f32),
        ],
        [
            ((2, deep, W_X, HALF), f32), taps_scratch, ((2, N_0, WIDE), f32), ((N_0, WIDE), f32), ((N_0, WIDE), bf16),
            ((N_0, WIDE), bf16), ((N_0, HID), bf16), ((N_0, WIDE), f32),
            ((N_0, WIDE), f32), ((N_0, HALF), f32),
        ],
        3_000_000_000,
        hbm_in=1,
        sems=((3,),),
    )
    to_first = section == 0

    def chosen(first, second):
        return jnp.where(to_first, first, second)

    core_0 = over_core(send_0)
    (taps_0,) = call(
        tap_grads_0, "tap_grads_0", (flags, x_wide, x_a, x_b, du0, own_0, sums_0), [((SMALL, WIDE), bf16)],
        [((2, deep, W_X, HALF), f32), ((ROWS_DEV, W_0, WIDE), f32), ((SMALL, WIDE), f32)], 2_000_000_000,
    )
    core_0, taps_0, pad_1 = lax.optimization_barrier((core_0, taps_0, pad_1))
    piece_0 = plus(keep_0, core_0)
    (taps_1,) = call(
        tap_grads_1, "tap_grads_1", (flags, pad_1, du1, own_1, sums_1), [((SMALL, WIDE), bf16)],
        [((ROWS_DEV, W_1, WIDE), f32), ((SMALL, WIDE), f32)], 2_000_000_000,
    )
    held_0, got_0 = reduce_send(piece_0, 0)
    taps_1, du0_send_a, du0_send_b = lax.optimization_barrier((taps_1, du0_send_a, du0_send_b))
    du0_a, du0_b = lat_halo(du0_send_a, du0_send_b)
    got_0, got_1, du0_a, du0_b = lax.optimization_barrier((got_0, got_1, du0_a, du0_b))
    pieces = jnp.stack([plus(held_0, got_0), plus(held_1, got_1)])
    pieces = reduce_step(pieces, 1)
    (start,) = call(
        input_grad, "input_grad", (flags, du0, du0_a, du0_b, small_0, e_own), [((ROWS_DEV, COLS_DEV, WIDE), bf16)],
        [((2, deep, W_0, HALF), f32), taps_scratch, ((ROWS_DEV, W_OWN, WIDE), f32)], 2_000_000_000,
    )
    for step in range(2, len(bits)):
        pieces = reduce_step(pieces, step)
    pieces, start = lax.optimization_barrier((pieces, start))
    other_end = over_section(chosen(final, start))
    piece_0, piece_1 = pieces[0], pieces[1]
    cut = piece_0.shape[0]
    boundary = jnp.stack([chosen(start, other_end), chosen(other_end, final)])[None]

    def both(piece, small):
        return jnp.concatenate([piece, small], axis=0)

    got = over_section(both(chosen(piece_1, piece_0), chosen(taps_1, taps_0)))
    piece = plus(chosen(piece_0, piece_1), got[:cut])
    small = plus(chosen(taps_0, taps_1), got[cut:])
    for step in reversed(range(len(bits))):
        if step == 0:
            piece, boundary = lax.optimization_barrier((piece, boundary))
        got = exchange(both(piece, small), step)
        cut = piece.shape[0]
        small = plus(small, got[cut:])
        which = side(step) == 0
        piece = jnp.where(which, jnp.concatenate([piece, got[:cut]]), jnp.concatenate([got[:cut], piece]))
    got = over_core(both(piece, small))
    weight_outs = [((1, WIDE, HID), f32), ((1, HID, WIDE), f32)]
    weight_scratch = [((WIDE, HID), f32), ((HID, WIDE), f32)]
    halves = call(
        finish_own, "finish_own", (flags, piece), weight_outs, weight_scratch, 1_000_000, hbm_out=2, sems=((2, QUARTERS),)
    )
    grad_up, grad_down, grad_taps, grad_channels, grad_bias = call(
        finish_got,
        "finish_got",
        (flags, small, got, *halves),
        weight_outs + [((TAPS, 1, WIDE), f32), ((5, 1, WIDE), f32), ((1, HID), f32)],
        weight_scratch,
        1_000_000,
        hbm_in=2,
        hbm_out=2,
        sems=((2, QUARTERS),),
        aliases={3: 0, 4: 1},
    )
    grad_taps, grad_channels = jnp.swapaxes(grad_taps, 0, 1), jnp.swapaxes(grad_channels, 0, 1)
    return (
        boundary,
        grad_taps,
        grad_channels,
        grad_up,
        grad_bias,
        grad_down,
    )


def solution(mesh):
    in_specs = (
        P(None, "lat", "lon", None),
        P(None, "lat", "lon", None),
        P("lat", "lon"),
        P("section", None, None),
        P("section", None, None),
        P("section", None, None),
        P("section", None),
        P("section", None, None),
    )
    out_specs = (
        P("section", None, "lat", "lon", None),
        P("section", None, None),
        P("section", None, None),
        P("section", None, None),
        P("section", None),
        P("section", None, None),
    )
    return jax.shard_map(
        on_device, mesh=mesh, in_specs=in_specs, out_specs=out_specs, check_vma=False
    )
```

```python
import math

import jax
import jax.numpy as jnp
from jax import lax
from jax.experimental import pallas as pl
from jax.experimental.pallas import tpu as pltpu
from jax.sharding import PartitionSpec as P

KERNEL = 7
TAPS = KERNEL * KERNEL
REACH = KERNEL // 2
ROWS_DEV = 4
COLS_DEV = 68
BATCH = 2
HALF = 128
WIDE = 256
HID = 1024
QUARTERS = HID // WIDE
SIDE_X, SIDE_0, SIDE_1 = 12, 9, 6
W_X, W_0, W_1, W_OWN = 96, 88, 80, 72
CHUNK = 32
SMALL = 64
N_0, N_1 = ROWS_DEV * W_0, ROWS_DEV * W_1
AT_NORMED, AT_BASE, AT_INVERSE, AT_E_0, AT_E_1 = 0, N_0, 2 * N_0, 3 * N_0, 4 * N_0
KEPT_ROWS = 40960

norm_eps = 1e-06
gelu_scale = 0.7978845608028654
gelu_cubic = 0.044715
f32, bf16 = jnp.float32, jnp.bfloat16

nn = (((1,), (0,)), ((), ()))
nt = (((1,), (1,)), ((), ()))
tn = (((0,), (0,)), ((), ()))


def dot(left, right, dims=nn):
    return lax.dot_general(left, right, dims, preferred_element_type=f32)


def lanes(half):
    return slice(half * HALF, (half + 1) * HALF)


def load_padded(pad, odd, center, first, second, offset=0):
    width = center.shape[1]

    def put(row, value):
        value = value.astype(f32)
        for half in range(2):
            pad[half, row, offset : offset + width, :] = value[:, lanes(half)]

    at_first = jnp.where(odd == 1, 0, REACH + ROWS_DEV)
    at_second = jnp.where(odd == 1, REACH + ROWS_DEV, 0)
    for row in range(ROWS_DEV):
        put(REACH + row, center[row])
    for row in range(REACH):
        put(at_first + row, first[row])
        put(at_second + row, second[row])


def load_taps(taps, small):
    for half in range(2):
        taps[half] = jnp.broadcast_to(small[0:TAPS, lanes(half)][:, None, :], (TAPS, 8, HALF))


def groups(width, most):
    tiles = width // 8
    count = -(-tiles // most)
    bounds = [tiles * i // count for i in range(count + 1)]
    return [range(first, last) for first, last in zip(bounds, bounds[1:])]


def conv_tiles(pad, taps, half, starts, reverse):
    sums = [[None] * ROWS_DEV for _ in starts]
    for col_off in range(KERNEL):
        column = [taps[half, TAPS - 1 - tap if reverse else tap] for tap in range(col_off, TAPS, KERNEL)]
        for row in range(ROWS_DEV + KERNEL - 1):
            for index, start in enumerate(starts):
                window = pad[half, row, start + col_off : start + col_off + 8, :]
                for out_row in range(ROWS_DEV):
                    row_off = row - out_row
                    if 0 <= row_off < KERNEL:
                        term = window * column[row_off]
                        held = sums[index][out_row]
                        sums[index][out_row] = term if held is None else held + term
    return sums


def chunks(count, body, carry=0):
    for i in range(count // CHUNK):
        carry = body(slice(i * CHUNK, (i + 1) * CHUNK), carry)
    return carry


def fold(value):
    return jnp.sum(value.reshape(CHUNK // 8, 8, value.shape[-1]), axis=0)


def twice(value):
    return jnp.concatenate([value, value], axis=1)


def send_rows(odd, source, send_first, send_second):
    first, second = jnp.where(odd == 1, 0, 1), jnp.where(odd == 1, 1, 0)
    send_first[...] = source[pl.ds(first, REACH)]
    send_second[...] = source[pl.ds(second, REACH)]


def forward_conv(width, pad, taps, small, normed, inverse, z, base):
    count = ROWS_DEV * width
    load_taps(taps, small)
    for group in groups(width, 4):
        starts = [tile * 8 for tile in group]
        halves = [conv_tiles(pad, taps, half, starts, False) for half in range(2)]
        for index, row in [(index, row) for index in range(len(starts)) for row in range(ROWS_DEV)]:
            start = starts[index]
            u = [halves[half][index][row] + small[TAPS : TAPS + 1, lanes(half)] for half in range(2)]
            mean = jnp.sum(u[0] + u[1], axis=-1, keepdims=True) * (1.0 / WIDE)
            u = [value - mean for value in u]
            spread = jnp.sum(u[0] * u[0] + u[1] * u[1], axis=-1, keepdims=True) * (1.0 / WIDE)
            scale = lax.rsqrt(spread + norm_eps)
            at = slice(row * width + start, row * width + start + 8)
            inverse[at, :] = jnp.broadcast_to(scale, (8, HALF))
            for half in range(2):
                normed[at, lanes(half)] = u[half] * scale
                base[at, lanes(half)] = pad[half, REACH + row, start + REACH : start + REACH + 8, :]
    scale_cells(count, small, normed, z)


def scale_cells(count, small, normed, z):
    def scaled(at, carry):
        z[at, :] = (normed[at, :] * small[TAPS + 1 : TAPS + 2, :] + small[TAPS + 2 : TAPS + 3, :]).astype(bf16)
        return carry

    chunks(count, scaled, 0)


def forward_mlp(width, small, mask, w_up, w_down, z, base, hidden, active, slope, branch, out, before_down=None):
    count = ROWS_DEV * width
    for quarter in range(QUARTERS):
        cols = slice(quarter * WIDE, (quarter + 1) * WIDE)
        held = hidden.at[quarter % 2]
        held[...] = dot(z[...], w_up[:, cols])
        bias = small[TAPS + 5 + quarter : TAPS + 6 + quarter, :]

        def gelu(at, carry, held=held, cols=cols, bias=bias):
            h = held[at, :] + bias
            square = h * h
            tangent = jnp.tanh(h * (gelu_scale + (gelu_scale * gelu_cubic) * square))
            above = 0.5 + 0.5 * tangent
            active[at, cols] = (h * above).astype(bf16)
            slope[at, cols] = above + (0.5 * h) * (1.0 - tangent * tangent) * (
                gelu_scale + (3.0 * gelu_scale * gelu_cubic) * square
            )
            return carry

        chunks(count, gelu, 0)
    if before_down:
        before_down()
    branch[...] = dot(active[...], w_down[...]) + small[TAPS + 3 : TAPS + 4, :]
    if out is None:
        return

    def residual(at, carry):
        out[at, :] = twice(mask[at, :]) * (base[at, :] + small[TAPS + 4 : TAPS + 5, :] * branch[at, :])
        return carry

    chunks(count, residual, 0)


def backward_cells(
    width, odd, small, own, own_row, upstream, w_up, w_down, normed, inverse, z, active, slope, branch, hidden, dm, dh, du, keep, send, sums
):
    count = ROWS_DEV * width
    zero = jnp.zeros((8, WIDE), f32)

    def first(at, carry):
        sum_dm, sum_em = carry
        e = upstream[at, :]
        inside = twice(own[at, :])
        grad = (e * small[TAPS + 4 : TAPS + 5, :]).astype(bf16)
        dm[at, :] = grad
        sum_dm = sum_dm + fold(grad.astype(f32) * inside)
        sum_em = sum_em + fold(e * branch[at, :] * inside)
        return sum_dm, sum_em

    sum_dm, sum_em = chunks(count, first, (zero, zero))
    for quarter in range(QUARTERS):
        cols = slice(quarter * WIDE, (quarter + 1) * WIDE)
        held = hidden.at[quarter % 2]
        held[...] = dot(dm[...], w_down[cols, :], nt)

        def through(at, carry, held=held, cols=cols):
            dh[at, cols] = (held[at, :] * slope[at, cols]).astype(bf16)
            return carry

        chunks(count, through, 0)
    hidden[0] = dot(dh[...], w_up[...], nt)
    sum_dh = dot(own_row[...], dh[...])

    def norm(at, carry):
        sum_dzn, sum_dz, sum_du = carry
        dz = hidden[0, at, :]
        normal = normed[at, :]
        inside = twice(own[at, :])
        inner = dz * inside
        sum_dz = sum_dz + fold(inner)
        sum_dzn = sum_dzn + fold(inner * normal)
        dn = dz * small[TAPS + 1 : TAPS + 2, :]
        mean = jnp.sum(dn, axis=-1, keepdims=True) * (1.0 / WIDE)
        slant = jnp.sum(dn * normal, axis=-1, keepdims=True) * (1.0 / WIDE)
        grad = (twice(inverse[at, :]) * (dn - mean - normal * slant)).astype(bf16).astype(f32)
        du[at, :] = grad
        sum_du = sum_du + fold(grad * inside)
        dm[at, :] = (dm[at, :].astype(f32) * inside).astype(bf16)
        z[at, :] = (z[at, :].astype(f32) * inside).astype(bf16)
        return sum_dzn, sum_dz, sum_du

    sum_dzn, sum_dz, sum_du = chunks(count, norm, (zero, zero, zero))
    rows = [jnp.sum(value, axis=0, keepdims=True) for value in (sum_du, sum_dzn, sum_dz, sum_dm, sum_em)]
    rows += [sum_dh[0:1, quarter * WIDE : (quarter + 1) * WIDE] for quarter in range(QUARTERS)]
    for index, value in enumerate(rows):
        sums[index : index + 1, :] = value
    sums[len(rows) : 16, :] = jnp.zeros((16 - len(rows), WIDE), f32)

    def weights(up_ref, down_ref):
        for quarter in range(QUARTERS):
            cols = slice(quarter * WIDE, (quarter + 1) * WIDE)
            up_ref[cols, :] = dot(z[...], dh[:, cols], tn).astype(bf16)
            down_ref[cols, :] = dot(active[:, cols], dm[...], tn).astype(bf16)

    @pl.when(odd == 0)
    def _():
        weights(keep, send)

    @pl.when(odd == 1)
    def _():
        weights(send, keep)


def weight_copies(block, flags, parts, w_up, w_down, sems, act, which=(0, 1)):
    odd, section = flags[0], flags[1]
    own_up, own_down, got_up, got_down, other_up, other_down = parts

    @pl.when(section == block)
    def _():
        for index in which:
            act(pltpu.make_async_copy((own_up, own_down)[index], (w_up, w_down)[index], sems.at[index]))

    @pl.when(section != block)
    def _():
        for index, (ref, mine, other) in enumerate(((w_up, got_up, other_up), (w_down, got_down, other_down))):
            if index not in which:
                continue
            half = mine.shape[0]
            for place, part in enumerate((mine, other)):
                first = odd if place == 0 else 1 - odd
                rows = pl.ds(pl.multiple_of(first * half, half), half)
                act(pltpu.make_async_copy(part, ref.at[rows, :], sems.at[2 + 2 * index + place]))


def start_copy(copy):
    copy.start()


def wait_copy(copy):
    copy.wait()


def write_rows(source, width, out):
    for row in range(ROWS_DEV):
        out[row] = source[row * width : (row + 1) * width, :].astype(bf16)


def kept_copies(kept, sems, places, out):
    copies = []
    for index, (ref, first) in enumerate(places):
        rows = kept.at[first : first + ref.shape[0], 0 : ref.shape[1]]
        copies.append(pltpu.make_async_copy(ref, rows, sems.at[index]) if out else pltpu.make_async_copy(rows, ref, sems.at[index]))
    return copies


def first_conv(
    flags, x, x_a, x_b, small, mask, cot, left, right, kept, pad, taps, wide, normed, inverse, z, base, e_1, sems
):
    places = [(wide, AT_E_0), (e_1, AT_E_1), (normed, AT_NORMED), (base, AT_BASE), (inverse, AT_INVERSE)]
    copies = kept_copies(kept, sems, places, True)
    before = SIDE_0 - SIDE_1
    wide[...] = jnp.zeros((N_0, WIDE), f32)
    for row in range(ROWS_DEV):
        at = row * W_0 + before
        wide[at : at + SIDE_1, :] = left[row].astype(f32)[SIDE_X : SIDE_X + SIDE_1]
        wide[at + SIDE_1 : at + SIDE_1 + COLS_DEV, :] = cot[row].astype(f32)
        wide[at + SIDE_1 + COLS_DEV : at + W_1, :] = right[row].astype(f32)[SIDE_X : SIDE_X + SIDE_1]
    wide[...] = wide[...] * twice(mask[...])
    for row in range(ROWS_DEV):
        at = row * W_0 + before
        e_1[row * W_1 : (row + 1) * W_1, :] = wide[at : at + W_1, :]
    for copy in copies[:2]:
        copy.start()
    load_padded(pad, flags[0], x, x_a, x_b)
    forward_conv(W_0, pad, taps, small, normed, inverse, z, base)
    for copy in copies[2:]:
        copy.start()
    for copy in copies:
        copy.wait()


def first_forward(flags, small, mask, kept, *refs):
    parts, refs = refs[:6], refs[6:]
    y, send_a, send_b, normed, z, base, hidden, out, active, slope, branch, w_up, w_down, weight_sems, sems = refs
    copies = kept_copies(kept, sems, [(normed, AT_NORMED), (base, AT_BASE)], False)
    for copy in copies:
        copy.start()
    weight_copies(0, flags, parts, w_up, w_down, weight_sems, start_copy)
    for copy in copies:
        copy.wait()
    scale_cells(N_0, small, normed, z)
    weight_copies(0, flags, parts, w_up, w_down, weight_sems, wait_copy, (0,))

    def down_ready():
        weight_copies(0, flags, parts, w_up, w_down, weight_sems, wait_copy, (1,))

    forward_mlp(W_0, small, mask, w_up, w_down, z, base, hidden, active, slope, branch, out, down_ready)
    write_rows(out, W_0, y)
    send_rows(flags[0], y, send_a, send_b)


def first_again(flags, small, kept, *refs):
    parts, refs = refs[:6], refs[6:]
    active, slope, branch, w_up, w_down, normed, z, hidden, weight_sems, sems = refs
    (copy,) = kept_copies(kept, sems, [(normed, AT_NORMED)], False)
    copy.start()
    weight_copies(0, flags, parts, w_up, w_down, weight_sems, start_copy)
    copy.wait()
    scale_cells(N_0, small, normed, z)
    weight_copies(0, flags, parts, w_up, w_down, weight_sems, wait_copy, (0,))

    def down_ready():
        weight_copies(0, flags, parts, w_up, w_down, weight_sems, wait_copy, (1,))

    forward_mlp(W_0, small, None, w_up, w_down, z, None, hidden, active, slope, branch, None, down_ready)


def second_block(flags, y, y_a, y_b, small, mask, own, own_row, kept, *refs):
    parts, refs = refs[:6], refs[6:]
    final, du_out, send_a, send_b, keep, send, sums, pad = refs[:8]
    taps, hidden, out, normed, inverse, z, base, active, slope, branch, w_up, w_down, upstream, dm, dh, du, weight_sems, sems = refs[8:]
    (copy,) = kept_copies(kept, sems, [(upstream, AT_E_1)], False)
    copy.start()
    weight_copies(1, flags, parts, w_up, w_down, weight_sems, start_copy)
    load_padded(pad, flags[0], y, y_a, y_b)
    forward_conv(W_1, pad, taps, small, normed, inverse, z, base)
    weight_copies(1, flags, parts, w_up, w_down, weight_sems, wait_copy)
    copy.wait()
    forward_mlp(W_1, small, mask, w_up, w_down, z, base, hidden, active, slope, branch, out)
    for row in range(ROWS_DEV):
        at = row * W_1 + SIDE_1
        final[row] = out[at : at + COLS_DEV, :].astype(bf16)
    backward_cells(
        W_1, flags[0], small, own, own_row, upstream, w_up, w_down, normed, inverse, z, active, slope, branch, hidden, dm, dh, du, keep, send, sums
    )
    write_rows(du, W_1, du_out)
    send_rows(flags[0], du_out, send_a, send_b)


def first_backward(
    flags, du1, du1_a, du1_b, small1, small0, mask, own, own_row, active, slope, branch, w_up, w_down, kept,
    e_own, du_out, send_a, send_b, keep, send, sums,
    pad, taps, hidden, upstream, z, dm, dh, du, normed, inverse, sems,
):
    copies = kept_copies(kept, sems, [(upstream, AT_E_0), (normed, AT_NORMED), (inverse, AT_INVERSE)], False)
    for copy in copies:
        copy.start()
    shift = SIDE_0 + REACH - SIDE_1
    pad[:, :, 0:8, :] = jnp.zeros((2, ROWS_DEV + 2 * REACH, 8, HALF), f32)
    pad[:, :, W_X - 16 : W_X, :] = jnp.zeros((2, ROWS_DEV + 2 * REACH, 16, HALF), f32)
    load_padded(pad, flags[0], du1, du1_a, du1_b, shift)
    load_taps(taps, small1)
    copies[0].wait()
    for group in groups(W_0, 4):
        starts = [tile * 8 for tile in group]
        for half in range(2):
            spread = conv_tiles(pad, taps, half, starts, True)
            for index, start in enumerate(starts):
                for row in range(ROWS_DEV):
                    at = slice(row * W_0 + start, row * W_0 + start + 8)
                    value = (upstream[at, lanes(half)] + spread[index][row]).astype(bf16).astype(f32)
                    upstream[at, lanes(half)] = mask[at, :] * value
    for row in range(ROWS_DEV):
        at = row * W_0 + SIDE_0
        e_own[row] = upstream[at : at + W_OWN, :]
    for copy in copies[1:]:
        copy.wait()
    scale_cells(N_0, small0, normed, z)
    backward_cells(
        W_0, flags[0], small0, own, own_row, upstream, w_up, w_down, normed, inverse, z, active, slope, branch, hidden, dm, dh, du, keep, send, sums
    )
    write_rows(du, W_0, du_out)
    send_rows(flags[0], du_out, send_a, send_b)


def input_grad(flags, du, du_a, du_b, small, e_own, out, pad, taps, total):
    load_padded(pad, flags[0], du, du_a, du_b)
    load_taps(taps, small)
    for group in groups(W_OWN, 5):
        starts = [tile * 8 for tile in group]
        for half in range(2):
            spread = conv_tiles(pad, taps, half, [start + SIDE_0 - REACH for start in starts], True)
            for index, start in enumerate(starts):
                for row in range(ROWS_DEV):
                    at = slice(start, start + 8)
                    total[row, at, lanes(half)] = e_own[row, at, lanes(half)] + spread[index][row]
    for row in range(ROWS_DEV):
        out[row] = total[row, 0:COLS_DEV, :].astype(bf16)


def tap_grads_1(flags, pad, du, own, sums, out, grads, total):
    tap_sums(W_1, pad, du, own, sums, out, grads, total)


def tap_grads_0(flags, v, v_a, v_b, du, own, sums, out, pad, grads, total):
    load_padded(pad, flags[0], v, v_a, v_b)
    tap_sums(W_0, pad, du, own, sums, out, grads, total)


def tap_sums(width, pad, du, own, sums, out, grads, total):
    for row in range(ROWS_DEV):
        inside = own[row * width : (row + 1) * width, :]
        grads[row] = du[row].astype(f32) * twice(inside)
    total[...] = jnp.zeros((SMALL, WIDE), f32)
    for half in range(2):
        for offsets in (range(0, 4), range(4, KERNEL)):
            partial = [[None] * KERNEL for _ in offsets]
            for tile in range(width // 8):
                start = tile * 8
                grad = [grads[row, start : start + 8, lanes(half)] for row in range(ROWS_DEV)]
                for row in range(ROWS_DEV + KERNEL - 1):
                    for index, col_off in enumerate(offsets):
                        window = pad[half, row, start + col_off : start + col_off + 8, :]
                        for out_row in range(ROWS_DEV):
                            row_off = row - out_row
                            if 0 <= row_off < KERNEL:
                                term = window * grad[out_row]
                                held = partial[index][row_off]
                                partial[index][row_off] = term if held is None else held + term
            for index, col_off in enumerate(offsets):
                for row_off in range(KERNEL):
                    tap = row_off * KERNEL + col_off
                    total[tap : tap + 1, lanes(half)] = jnp.sum(partial[index][row_off], axis=0, keepdims=True)
    total[TAPS : TAPS + 9, :] = sums[0:9, :]
    out[...] = total[...].astype(bf16)


factor = 1.0 / math.sqrt(BATCH * ROWS_DEV * COLS_DEV)


def write_weights(is_up, rows, up, down, up_vmem, down_vmem, sems, beside=None):
    def send(copies, fill):
        for quarter in range(QUARTERS):
            fill(quarter, rows[quarter * WIDE : (quarter + 1) * WIDE, :].astype(f32) * factor)
            copies[quarter].start()
        if beside:
            beside()
        for copy in copies:
            copy.wait()

    def cols(quarter):
        return slice(quarter * WIDE, (quarter + 1) * WIDE)

    @pl.when(is_up)
    def _():
        def fill(quarter, value):
            up_vmem[:, cols(quarter)] = value

        send([pltpu.make_async_copy(up_vmem.at[:, cols(q)], up.at[0, :, cols(q)], sems.at[0, q]) for q in range(QUARTERS)], fill)

    @pl.when(jnp.logical_not(is_up))
    def _():
        def fill(quarter, value):
            down_vmem[cols(quarter), :] = value

        send([pltpu.make_async_copy(down_vmem.at[cols(q), :], down.at[0, cols(q), :], sems.at[1, q]) for q in range(QUARTERS)], fill)


def finish_own(flags, piece, up, down, up_vmem, down_vmem, sems):
    write_weights(flags[0] == 0, piece, up, down, up_vmem, down_vmem, sems)


def finish_got(flags, small, got, up_in, down_in, up, down, taps, channels, bias, up_vmem, down_vmem, sems):
    def rest():
        sums = (small[...].astype(f32) + got[HID:, :].astype(f32)) * factor
        for tap in range(TAPS):
            taps[tap] = sums[tap : tap + 1]
        for index in range(5):
            channels[index] = sums[TAPS + index : TAPS + index + 1]
        for quarter in range(QUARTERS):
            bias[:, quarter * WIDE : (quarter + 1) * WIDE] = sums[TAPS + 5 + quarter : TAPS + 6 + quarter]

    write_weights(flags[0] == 1, got, up, down, up_vmem, down_vmem, sems, rest)


def in_vmem():
    return pl.BlockSpec(memory_space=pltpu.VMEM)


def call(body, name, inputs, outputs, scratch, flops, hbm_in=0, hbm_out=0, sems=(), aliases=None):
    in_hbm = pl.BlockSpec(memory_space=pltpu.HBM)
    return pl.pallas_call(
        body,
        name=name,
        out_shape=[jax.ShapeDtypeStruct(shape, dtype) for shape, dtype in outputs],
        in_specs=[pl.BlockSpec(memory_space=pltpu.SMEM)] + [in_vmem()] * (len(inputs) - 1 - hbm_in) + [in_hbm] * hbm_in,
        out_specs=[in_hbm] * hbm_out + [in_vmem()] * (len(outputs) - hbm_out),
        input_output_aliases=aliases or {},
        scratch_shapes=[pltpu.VMEM(shape, dtype) for shape, dtype in scratch] + [pltpu.SemaphoreType.DMA(shape) for shape in sems],
        compiler_params=pltpu.CompilerParams(vmem_limit_bytes=28 << 20),
        cost_estimate=pl.CostEstimate(flops=10 * flops, bytes_accessed=4 << 20, transcendentals=0),
    )(*inputs)


def swap_pairs(count, bit):
    return [(i, i ^ bit) for i in range(count)]


def on_device(
    window_input,
    output_cotangent,
    ocean_mask,
    dw_kernel,
    channel_params,
    up_weight,
    up_bias,
    down_weight,
):
    section = lax.axis_index("section")
    lat = lax.axis_index("lat")
    lon = lax.axis_index("lon")
    n_lat, n_lon = lax.axis_size("lat"), lax.axis_size("lon")
    odd = lat % 2
    flags = jnp.stack([odd, section]).astype(jnp.int32)
    channels = window_input.shape[-1]

    def over_section(value):
        return lax.ppermute(value, "section", [(0, 1), (1, 0)])

    def over_core(value):
        return lax.ppermute(value, "lat", swap_pairs(n_lat, 1))

    def lat_halo(send_a, send_b, choose=False):
        pairs = [(i, i + 1) for i in range(1, n_lat - 1, 2)]
        pairs += [(j, i) for i, j in pairs]
        got_b = lax.ppermute(send_b, "lat", pairs)
        if not choose:
            return over_core(send_a), got_b
        beside = jnp.where(odd == 1, lat < n_lat - 1, lat > 0)
        return over_core(send_a), jnp.where(beside, got_b, jnp.zeros_like(got_b))

    def by_core(even, other):
        return jnp.where(odd == 0, even, other)

    x = lax.dynamic_index_in_dim(window_input, section, 0, False)
    cot = lax.dynamic_index_in_dim(output_cotangent, section, 0, False)
    sea = ocean_mask.astype(bf16)

    def packed(x_part, cot_part, sea_part):
        sea_row = jnp.pad(sea_part, ((0, 0), (0, channels - sea_part.shape[1])))[:, None, :]
        return jnp.concatenate([x_part, cot_part, sea_row], axis=1)

    ring = [(i, (i + 1) % n_lon) for i in range(n_lon)]
    to_right = packed(x[:, -SIDE_X:], cot[:, -SIDE_1:], sea[:, -SIDE_0:])
    to_left = packed(x[:, :SIDE_X], cot[:, :SIDE_1], sea[:, :SIDE_0])
    to_right, to_left, dw_kernel, up_bias = lax.optimization_barrier((to_right, to_left, dw_kernel, up_bias))
    left = lax.ppermute(to_right, "lon", ring)
    right = lax.ppermute(to_left, "lon", [(j, i) for i, j in ring])
    small_own = jnp.concatenate(
        [dw_kernel[0], channel_params[0], up_bias[0].reshape(QUARTERS, WIDE), jnp.zeros((SMALL - TAPS - 9, WIDE), bf16)], axis=0
    )
    up, down = up_weight[0], down_weight[0]
    cut = channels // 2
    small_got = over_section(small_own)
    send_up = by_core(up[:cut], up[cut:])
    send_down = by_core(down[: HID // 2], down[HID // 2 :])
    send_up, send_down, small_got = lax.optimization_barrier((send_up, send_down, small_got))
    got_up, got_down = over_section(send_up), over_section(send_down)
    small_0 = jnp.where(section == 0, small_own, small_got).astype(f32)
    small_1 = jnp.where(section == 0, small_got, small_own).astype(f32)

    before = SIDE_0 - SIDE_1
    sea_at = SIDE_X + SIDE_1
    x_wide = jnp.concatenate([left[:, :SIDE_X], x, right[:, :SIDE_X], jnp.zeros((ROWS_DEV, W_X - COLS_DEV - 2 * SIDE_X, channels), bf16)], axis=1)
    x_a, x_b = lat_halo(by_core(x_wide[1:], x_wide[:REACH]), by_core(x_wide[:REACH], x_wide[1:]), True)
    mask_wide = jnp.concatenate(
        [left[:, sea_at, :SIDE_0], sea, right[:, sea_at, :SIDE_0], jnp.zeros((ROWS_DEV, W_0 - COLS_DEV - 2 * SIDE_0), bf16)], axis=1
    )
    before = SIDE_0 - SIDE_1
    def spread_lanes(mask):
        flat = mask.astype(f32).reshape(-1, 1)
        return jnp.broadcast_to(flat, (flat.shape[0], HALF))

    mask_0, mask_1 = spread_lanes(mask_wide), spread_lanes(mask_wide[:, before : before + W_1])

    def own_cells(width, side):
        column = jnp.arange(width)
        inside = ((column >= side) & (column < side + COLS_DEV)).astype(f32)
        flat = jnp.tile(inside, ROWS_DEV)
        return jnp.broadcast_to(flat[:, None], (flat.shape[0], HALF)), jnp.broadcast_to(flat[None, :], (16, flat.shape[0])).astype(bf16)

    own_0, row_0 = own_cells(W_0, SIDE_0)
    own_1, row_1 = own_cells(W_1, SIDE_1)

    deep = ROWS_DEV + 2 * REACH
    taps_scratch = ((2, TAPS, 8, HALF), f32)

    (kept,) = call(
        first_conv,
        "first_conv",
        (flags, x_wide, x_a, x_b, small_0, mask_0, cot, left, right),
        [((KEPT_ROWS, WIDE), f32)],
        [
            ((2, deep, W_X, HALF), f32), taps_scratch, ((N_0, WIDE), f32), ((N_0, WIDE), f32), ((N_0, HALF), f32),
            ((N_0, WIDE), bf16), ((N_0, WIDE), f32), ((N_1, WIDE), f32),
        ],
        2_000_000_000,
        hbm_out=1,
        sems=((5,),),
    )
    got_up, got_down, kept = lax.optimization_barrier((got_up, got_down, kept))
    other_up, other_down = over_core(got_up), over_core(got_down)
    weights = (up, down, got_up, got_down, other_up, other_down)
    y, y_send_a, y_send_b = call(
        first_forward,
        "first_forward",
        (flags, small_0, mask_0, kept) + weights,
        [((ROWS_DEV, W_0, WIDE), bf16), ((REACH, W_0, WIDE), bf16), ((REACH, W_0, WIDE), bf16)],
        [
            ((N_0, WIDE), f32), ((N_0, WIDE), bf16), ((N_0, WIDE), f32), ((2, N_0, WIDE), f32), ((N_0, WIDE), f32),
            ((N_0, HID), bf16), ((N_0, HID), f32), ((N_0, WIDE), f32), ((WIDE, HID), bf16), ((HID, WIDE), bf16),
        ],
        2_000_000_000,
        hbm_in=7,
        sems=((6,), (2,)),
    )
    y_a, y_b = lat_halo(y_send_a, y_send_b, True)
    final, du1, du1_send_a, du1_send_b, keep_1, send_1, sums_1, pad_1 = call(
        second_block,
        "second_block",
        (flags, y, y_a, y_b, small_1, mask_1, own_1, row_1, kept) + weights,
        [
            ((ROWS_DEV, COLS_DEV, WIDE), bf16), ((ROWS_DEV, W_1, WIDE), bf16), ((REACH, W_1, WIDE), bf16), ((REACH, W_1, WIDE), bf16),
            ((HID, WIDE), bf16), ((HID, WIDE), bf16), ((16, WIDE), f32), ((2, deep, W_0, HALF), f32),
        ],
        [
            taps_scratch, ((2, N_1, WIDE), f32), ((N_1, WIDE), f32),
            ((N_1, WIDE), f32), ((N_1, HALF), f32), ((N_1, WIDE), bf16), ((N_1, WIDE), f32), ((N_1, HID), bf16), ((N_1, HID), f32), ((N_1, WIDE), f32),
            ((WIDE, HID), bf16), ((HID, WIDE), bf16), ((N_1, WIDE), f32), ((N_1, WIDE), bf16), ((N_1, HID), bf16), ((N_1, WIDE), f32),
        ],
        4_000_000_000,
        hbm_in=7,
        sems=((6,), (1,)),
    )
    du1_a, du1_b = lat_halo(du1_send_a, du1_send_b)
    bits = [("lat", 1 << i) for i in range(1, n_lat.bit_length() - 1)] + [("lon", 1 << i) for i in range(n_lon.bit_length() - 1)]
    orders = (bits, bits[1:2] + bits[:1] + bits[2:])

    def partner(place, step):
        row, col = place
        axis, bit = orders[row % 2][step]
        return (row ^ bit, col) if axis == "lat" else (row, col ^ bit)

    def exchange(value, step):
        pairs = []
        for row in range(n_lat):
            for col in range(n_lon):
                other = partner((row, col), step)
                pairs.append((row * n_lon + col, other[0] * n_lon + other[1]))
        return lax.ppermute(value, ("lat", "lon"), pairs)

    def side(step):
        def of(order):
            axis, bit = order[step]
            return ((lat if axis == "lat" else lon) // bit) % 2

        return jnp.where(odd == 0, of(orders[0]), of(orders[1]))

    def plus(first, second):
        return (first.astype(f32) + second.astype(f32)).astype(bf16)

    def reduce_scatter(keep, send):
        piece = plus(keep, over_core(send))
        for step in range(len(bits)):
            half = piece.shape[0] // 2
            low, high = piece[:half], piece[half:]
            which = side(step) == 0
            piece = plus(jnp.where(which, low, high), exchange(jnp.where(which, high, low), step))
        return piece

    def reduce_send(piece, step):
        half = piece.shape[-2] // 2
        low, high = piece[..., :half, :], piece[..., half:, :]
        which = side(step) == 0
        return jnp.where(which, low, high), exchange(jnp.where(which, high, low), step)

    def reduce_step(piece, step):
        return plus(*reduce_send(piece, step))

    small_again, _ = lax.optimization_barrier((small_0, du1_send_a))
    active, slope, branch, w_up, w_down = call(
        first_again,
        "first_again",
        (flags, small_again, kept) + weights,
        [((N_0, HID), bf16), ((N_0, HID), f32), ((N_0, WIDE), f32), ((WIDE, HID), bf16), ((HID, WIDE), bf16)],
        [((N_0, WIDE), f32), ((N_0, WIDE), bf16), ((2, N_0, WIDE), f32)],
        2_000_000_000,
        hbm_in=7,
        sems=((6,), (1,)),
    )
    send_1, du1_a = lax.optimization_barrier((send_1, du1_a))
    held_1, got_1 = reduce_send(plus(keep_1, over_core(send_1)), 0)
    e_own, du0, du0_send_a, du0_send_b, keep_0, send_0, sums_0 = call(
        first_backward,
        "first_backward",
        (flags, du1, du1_a, du1_b, small_1, small_0, mask_0, own_0, row_0, active, slope, branch, w_up, w_down, kept),
        [
            ((ROWS_DEV, W_OWN, WIDE), f32), ((ROWS_DEV, W_0, WIDE), bf16), ((REACH, W_0, WIDE), bf16), ((REACH, W_0, WIDE), bf16),
            ((HID, WIDE), bf16), ((HID, WIDE), bf16), ((16, WIDE), f32),
        ],
        [
            ((2, deep, W_X, HALF), f32), taps_scratch, ((2, N_0, WIDE), f32), ((N_0, WIDE), f32), ((N_0, WIDE), bf16),
            ((N_0, WIDE), bf16), ((N_0, HID), bf16), ((N_0, WIDE), f32),
            ((N_0, WIDE), f32), ((N_0, HALF), f32),
        ],
        3_000_000_000,
        hbm_in=1,
        sems=((3,),),
    )
    to_first = section == 0

    def chosen(first, second):
        return jnp.where(to_first, first, second)

    core_0 = over_core(send_0)
    (taps_0,) = call(
        tap_grads_0, "tap_grads_0", (flags, x_wide, x_a, x_b, du0, own_0, sums_0), [((SMALL, WIDE), bf16)],
        [((2, deep, W_X, HALF), f32), ((ROWS_DEV, W_0, WIDE), f32), ((SMALL, WIDE), f32)], 2_000_000_000,
    )
    core_0, taps_0, pad_1 = lax.optimization_barrier((core_0, taps_0, pad_1))
    piece_0 = plus(keep_0, core_0)
    (taps_1,) = call(
        tap_grads_1, "tap_grads_1", (flags, pad_1, du1, own_1, sums_1), [((SMALL, WIDE), bf16)],
        [((ROWS_DEV, W_1, WIDE), f32), ((SMALL, WIDE), f32)], 2_000_000_000,
    )
    held_0, got_0 = reduce_send(piece_0, 0)
    taps_1, du0_send_a, du0_send_b = lax.optimization_barrier((taps_1, du0_send_a, du0_send_b))
    du0_a, du0_b = lat_halo(du0_send_a, du0_send_b)
    got_0, got_1, du0_a, du0_b = lax.optimization_barrier((got_0, got_1, du0_a, du0_b))
    pieces = jnp.stack([plus(held_0, got_0), plus(held_1, got_1)])
    pieces = reduce_step(pieces, 1)
    (start,) = call(
        input_grad, "input_grad", (flags, du0, du0_a, du0_b, small_0, e_own), [((ROWS_DEV, COLS_DEV, WIDE), bf16)],
        [((2, deep, W_0, HALF), f32), taps_scratch, ((ROWS_DEV, W_OWN, WIDE), f32)], 2_000_000_000,
    )
    for step in range(2, len(bits)):
        pieces = reduce_step(pieces, step)
    pieces, start = lax.optimization_barrier((pieces, start))
    other_end = over_section(chosen(final, start))
    piece_0, piece_1 = pieces[0], pieces[1]
    cut = piece_0.shape[0]
    boundary = jnp.stack([chosen(start, other_end), chosen(other_end, final)])[None]

    def both(piece, small):
        return jnp.concatenate([piece, small], axis=0)

    got = over_section(both(chosen(piece_1, piece_0), chosen(taps_1, taps_0)))
    piece = plus(chosen(piece_0, piece_1), got[:cut])
    small = plus(chosen(taps_0, taps_1), got[cut:])
    for step in reversed(range(len(bits))):
        if step == 0:
            piece, boundary = lax.optimization_barrier((piece, boundary))
        got = exchange(both(piece, small), step)
        cut = piece.shape[0]
        small = plus(small, got[cut:])
        which = side(step) == 0
        piece = jnp.where(which, jnp.concatenate([piece, got[:cut]]), jnp.concatenate([got[:cut], piece]))
    got = over_core(both(piece, small))
    weight_outs = [((1, WIDE, HID), f32), ((1, HID, WIDE), f32)]
    weight_scratch = [((WIDE, HID), f32), ((HID, WIDE), f32)]
    halves = call(
        finish_own, "finish_own", (flags, piece), weight_outs, weight_scratch, 1_000_000, hbm_out=2, sems=((2, QUARTERS),)
    )
    grad_up, grad_down, grad_taps, grad_channels, grad_bias = call(
        finish_got,
        "finish_got",
        (flags, small, got, *halves),
        weight_outs + [((TAPS, 1, WIDE), f32), ((5, 1, WIDE), f32), ((1, HID), f32)],
        weight_scratch,
        1_000_000,
        hbm_in=2,
        hbm_out=2,
        sems=((2, QUARTERS),),
        aliases={3: 0, 4: 1},
    )
    grad_taps, grad_channels = jnp.swapaxes(grad_taps, 0, 1), jnp.swapaxes(grad_channels, 0, 1)
    return (
        boundary,
        grad_taps,
        grad_channels,
        grad_up,
        grad_bias,
        grad_down,
    )


def solution(mesh):
    in_specs = (
        P(None, "lat", "lon", None),
        P(None, "lat", "lon", None),
        P("lat", "lon"),
        P("section", None, None),
        P("section", None, None),
        P("section", None, None),
        P("section", None),
        P("section", None, None),
    )
    out_specs = (
        P("section", None, "lat", "lon", None),
        P("section", None, None),
        P("section", None, None),
        P("section", None, None),
        P("section", None),
        P("section", None, None),
    )
    return jax.shard_map(
        on_device, mesh=mesh, in_specs=in_specs, out_specs=out_specs, check_vma=False
    )
```
